256 devices in a mesh: dp: 4 (over z_lo), row: 4 (over x), col: 16 (over z_hi, y, core).
Axes of the slice: x: 4, y: 4, z: 8 (z_hi: 2, z_lo: 4; z = z_hi * 4 + z_lo), core: 2. Of those that a mesh axis runs over, the one named last changes fastest.
Arguments:
- activations: bfloat16 [4096, 8192], P('dp', 'row'), may hold values from -6 to 6
- grad_out: bfloat16 [4096, 26624], P('dp', 'col'), may hold values from -0.09375 to 0.09375
- sketch: float32 [26624, 128], P('col'), may hold values from -6 to 6
Outputs:
- basis: float32 [8192, 128], P('row')
- coef: float32 [128, 26624], P(None, 'col')
The draws below stay inside these ranges and needn't reach their ends.
All inputs are finite; a program needn't handle non-finite values.
Results may differ from the reference program's by a relative error of at most 0.0003.
Values sent between devices are 32-bit elements; how exact they have to be, the bound alone decides.
A program may use at most 128 MiB of HBM per device.

```python
import math
import jax
import jax.numpy as jnp
from jax import lax

D = 8192
FF = 26624
RANK = 128
ITERS = 2
TOKENS = 4096


def block_levels(stream_key, extent, shards, low, top_value):
    loudness, own = 1.0, jax.random.fold_in(stream_key, 6)
    for position, shards_of in shards:
        steps = jnp.exp(jax.random.uniform(jax.random.fold_in(own, position), (shards_of,), jnp.float32, low / len(shards), top_value / len(shards)))
        loudness = loudness * jnp.repeat(steps, extent[position] // shards_of).reshape([-1 if axis == position else 1 for axis in range(len(extent))])
    return loudness


def centred(own_key, extent, width, limit, split=(), dtype=jnp.bfloat16):
    result = jax.random.normal(own_key, extent, jnp.float32) * width
    if len(split) > 0:
        result = block_levels(own_key, extent, split, -0.22, 0.18) * result
    return jnp.clip(result, min=-limit, max=limit).astype(dtype)


def setup_inputs(seed: int = 0) -> dict:
    streams_of = jax.random.split(jax.random.key(seed), 4)
    return {
        "activations": centred(streams_of[0], (TOKENS, D), 1.0, 6.0, ((0, 4), (1, 4))),
        "grad_out": centred(streams_of[1], (TOKENS, FF), TOKENS ** -0.5, 0.09375, ((0, 4), (1, 16))),
        "sketch": centred(streams_of[2], (FF, RANK), 1.0, 6.0, ((0, 16),), jnp.float32),
    }


def orthonormal(mat):
    hp = lax.Precision.HIGHEST
    gram = jnp.dot(mat.T, mat, precision=hp)
    lower = jnp.linalg.cholesky(gram)
    return jax.scipy.linalg.solve_triangular(lower, mat.T, lower=True).T

def reference(activations, grad_out, sketch):
    hp = lax.Precision.HIGHEST
    inputs = activations.astype(jnp.float32)
    cotangent = grad_out.astype(jnp.float32)

    def apply_grad(mat):
        return jnp.dot(inputs.T, jnp.dot(cotangent, mat, precision=hp), precision=hp)

    def apply_trans(mat):
        return jnp.dot(cotangent.T, jnp.dot(inputs, mat, precision=hp), precision=hp)
    basis = orthonormal(apply_grad(sketch))
    for step in range(ITERS):
        cobasis = apply_trans(basis)
        basis = orthonormal(apply_grad(cobasis))
    coef = apply_trans(basis).T
    return (basis * math.sqrt(D), coef)
```

```python
import math

import jax
import jax.numpy as jnp
from jax import lax
from jax.sharding import PartitionSpec as P

D = 8192
ITERS = 2


def halves(mat):
    high = lax.reduce_precision(mat, 8, 7)
    low = lax.reduce_precision(mat - high, 8, 7)
    return jnp.concatenate([high.astype(jnp.bfloat16), low.astype(jnp.bfloat16)], axis=1)


def product(lhs, mat, dim):
    wide = lax.dot_general(
        lhs, halves(mat), (((dim,), (0,)), ((), ())), preferred_element_type=jnp.float32
    )
    rank = mat.shape[1]
    return wide[:, :rank] + wide[:, rank:]


def body(activations, grad_out, sketch):
    hp = lax.Precision.HIGHEST

    def apply_grad(mat):
        tokens = lax.psum(product(grad_out, mat, 1), "col")
        return lax.psum(product(activations, tokens, 0), "dp")

    def apply_trans(mat):
        tokens = lax.psum(product(activations, mat, 1), "row")
        return lax.psum(product(grad_out, tokens, 0), "dp")

    def orthonormal(mat):
        gram = lax.psum(jnp.dot(mat.T, mat, precision=hp), "row")
        lower = jnp.linalg.cholesky(gram)
        inverse = jax.scipy.linalg.solve_triangular(
            lower, jnp.eye(lower.shape[0], dtype=jnp.float32), lower=True
        )
        return jnp.dot(mat, inverse.T, precision=hp)

    basis = orthonormal(apply_grad(sketch))
    for step in range(ITERS):
        basis = orthonormal(apply_grad(apply_trans(basis)))
    coef = apply_trans(basis).T
    return (basis * math.sqrt(D), coef)


def solution(mesh):
    in_specs = (P("dp", "row"), P("dp", "col"), P("col", None))
    out_specs = (P("row", None), P(None, "col"))
    return jax.shard_map(body, mesh=mesh, in_specs=in_specs, out_specs=out_specs, check_vma=False)
```

```python
import functools
import math

import jax
import jax.numpy as jnp
from jax import lax
from jax.experimental import pallas as pl
from jax.experimental.pallas import tpu as pltpu
from jax.sharding import PartitionSpec as P

MESH = pl.DeviceIdType.MESH
F32 = jnp.float32
BF16 = jnp.bfloat16
HIGHEST = lax.Precision.HIGHEST
D = 8192
RANK = 128
ROUNDS = 3
TOK = 1024
HID = 1664
NN = (((1,), (0,)), ((), ()))
NT = (((1,), (1,)), ((), ()))
TN = (((0,), (0,)), ((), ()))
YC, YR, YG, YX, MZ, XC, XR, XG, XX, PR, PG, GC, GR, GX, GZ = range(15)
PHASES = 15
LA, LB, LS, FX, FB, FC = range(6)


def terms(mat):
    high = mat.astype(BF16)
    low = (mat - high.astype(F32)).astype(BF16)
    return high, low


def twice(mat):
    return jnp.concatenate(terms(mat), axis=0)


def folded(wide):
    rows = wide.shape[0] // 2
    return wide[:rows] + wide[rows:]


def kernel(
    a_hbm, b_hbm, s_hbm, basis_ref, coef_ref,
    a, at, b, s, st, pt, ysend, ycore, yown, yrs, yt, ylhs, mzs, mt, xs, xcore, xown, xrs, xt, xlhs,
    ps, prs, gown, gcore, gsum, grs, gpart, grx, gfull, work, linv, cf, mg,
    load_sem, send_sem, recv_sem,
):
    z, x, j = lax.axis_index("dp"), lax.axis_index("row"), lax.axis_index("col")
    c, t = j % 2, j // 2
    o = 1 - c

    barrier = pltpu.get_barrier_semaphore()

    def greet(dev):
        pl.semaphore_signal(barrier, inc=1, device_id=dev, device_id_type=MESH)

    def layer_peer(k):
        x2 = (x + k // 8) % 4
        t2 = (t + k) % 8
        return x2, t2

    loads = [
        pltpu.make_async_copy(s_hbm, s, load_sem.at[LS]),
        pltpu.make_async_copy(b_hbm, b, load_sem.at[LB]),
        pltpu.make_async_copy(
            a_hbm.at[:, pl.ds(pl.multiple_of(j * 128, 128), 128)], a, load_sem.at[LA]
        ),
    ]
    for load in loads:
        load.start()

    greet((z, x, t * 2 + o))
    for k in range(1, 4):
        greet(((z + k) % 4, x, j))

    def greet_layer(k, carry):
        x2, t2 = layer_peer(k)
        greet((z, x2, t2 * 2 + c))
        return carry

    lax.fori_loop(1, 32, greet_layer, 0)

    def send(src, dst, rnd, phase, dev):
        pltpu.make_async_remote_copy(
            src_ref=src,
            dst_ref=dst,
            send_sem=send_sem.at[rnd, phase],
            recv_sem=recv_sem.at[rnd, phase],
            device_id=dev,
            device_id_type=MESH,
        ).start()

    def landed(like, rnd, phase):
        pltpu.make_async_copy(like, like, recv_sem.at[rnd, phase]).wait()

    def left(like, rnd, phase):
        pltpu.make_async_copy(like, like, send_sem.at[rnd, phase]).wait()

    partner = (z, x, t * 2 + o)
    row_iota = lax.broadcasted_iota(jnp.int32, (RANK, RANK), 0)
    col_iota = lax.broadcasted_iota(jnp.int32, (RANK, RANK), 1)
    eye = jnp.where(row_iota == col_iota, 1.0, 0.0).astype(F32)

    def factor_start(rnd):
        work[:, :RANK] = gfull[rnd].reshape(RANK, RANK)
        work[:, RANK:] = eye

    sub = lax.broadcasted_iota(jnp.int32, (8, RANK), 0)
    lane = lax.broadcasted_iota(jnp.int32, (8, RANK), 1)

    def spread(row):
        return jnp.broadcast_to(row, (8, RANK))

    def factor_block(blk, carry):
        r0 = pl.multiple_of(blk * 8, 8)
        gp = work[pl.ds(r0, 8), :RANK]
        ep = work[pl.ds(r0, 8), RANK:]
        diag = pltpu.roll(gp, RANK - r0, 1)
        cols = [jnp.broadcast_to(diag[:, i : i + 1], (8, RANK)) for i in range(8)]
        inv = [jnp.where(sub == i, 1.0, 0.0).astype(F32) for i in range(8)]
        pivots = jnp.ones((8, RANK), F32)
        for i in range(8):
            pivot = spread(cols[i][i : i + 1])
            pivots = jnp.where(sub == i, pivot, pivots)
            if i == 7:
                break
            scale = jnp.where(sub > i, cols[i] * (1.0 / pivot), 0.0)
            for m in range(i + 1, 8):
                cols[m] = cols[m] - scale * spread(cols[m][i : i + 1])
            for m in range(i + 1):
                inv[m] = inv[m] - scale * spread(inv[m][i : i + 1])
        root = lax.rsqrt(pivots)
        root = root * (1.5 - 0.5 * pivots * root * root)
        ug = jnp.zeros((8, RANK), F32)
        ue = jnp.zeros((8, RANK), F32)
        for m in range(8):
            weight = inv[m] * root
            ug = ug + weight * spread(gp[m : m + 1])
            ue = ue + weight * spread(ep[m : m + 1])
        work[pl.ds(r0, 8), RANK:] = ue
        rest = jnp.where(lane >= r0 + 8, ug, 0.0)
        work[...] -= lax.dot_general(
            rest, jnp.concatenate([ug, ue], axis=1), TN, precision=HIGHEST, preferred_element_type=F32
        )
        return carry

    def factor_blocks(lo, hi):
        lax.fori_loop(lo, hi, factor_block, 0)

    loads[0].wait()
    st[...] = s[...].T
    pt[0] = st[pl.ds(pl.multiple_of(x * 32, 32), 32), :].reshape(4, 8, HID)
    gfull[0] = eye.reshape(4, 32, RANK)
    loads[2].wait()
    at[...] = a[...].T
    loads[1].wait()

    pl.semaphore_wait(barrier, 35)

    def one_round(rnd, carry):
        lhs = twice(pt[rnd].reshape(32, HID))
        part = folded(lax.dot_general(lhs, b[...], NT, preferred_element_type=F32))
        for h in range(2):
            for i in range(8):
                ysend[rnd, h, i] = part[h * 16 : h * 16 + 16, i * 128 : i * 128 + 128]
        send(ysend.at[rnd, o], ycore.at[rnd], rnd, YC, partner)
        landed(ycore.at[rnd], rnd, YC)
        yown[rnd] = ysend[rnd, c] + ycore[rnd]

        def reduce_y(k, carry):
            t2 = (t + k) % 8
            send(yown.at[rnd, t2], yrs.at[rnd, t], rnd, YR, (z, x, t2 * 2 + c))
            return carry

        lax.fori_loop(1, 8, reduce_y, 0)
        yrs[rnd, t] = yown[rnd, t]
        factor_start(rnd)
        factor_blocks(0, 6)
        landed(yrs.at[rnd, pl.ds(0, 7)], rnd, YR)
        total = yrs[rnd, 0]
        for i in range(1, 8):
            total = total + yrs[rnd, i]
        mine = x * 8 + t
        yt[rnd, c, mine] = total

        def gather_y(k, carry):
            x2, t2 = layer_peer(k)
            piece = yt.at[rnd, c, mine]
            send(piece, piece, rnd, YG, (z, x2, t2 * 2 + c))
            return carry

        lax.fori_loop(1, 32, gather_y, 0)
        factor_blocks(6, 16)
        linv[rnd] = work[:, RANK:]
        landed(yt.at[rnd, c, pl.ds(0, 31)], rnd, YG)
        send(yt.at[rnd, c], yt.at[rnd, c], rnd, YX, partner)

        def m_half(h):
            for i in range(4):
                for m in range(8):
                    high, low = terms(yt[rnd, h, i * 8 + m])
                    ylhs[i * 16 : i * 16 + 16, m * 128 : m * 128 + 128] = high
                    ylhs[64 + i * 16 : 64 + i * 16 + 16, m * 128 : m * 128 + 128] = low
            half = folded(jnp.dot(ylhs[...], a[...], preferred_element_type=F32))
            for i in range(4):
                mzs[rnd, z, pl.ds(pl.multiple_of(i * 32 + h * 16, 16), 16), :] = half[i * 16 : i * 16 + 16]

        m_half(c)
        landed(yt.at[rnd, o], rnd, YX)
        m_half(o)
        for k in range(1, 4):
            send(mzs.at[rnd, z], mzs.at[rnd, z], rnd, MZ, ((z + k) % 4, x, j))
        landed(mzs.at[rnd, pl.ds(0, 3)], rnd, MZ)
        raw = (mzs[rnd, 0] + mzs[rnd, 1]) + (mzs[rnd, 2] + mzs[rnd, 3])
        mt[rnd] = jnp.dot(linv[rnd], raw, precision=HIGHEST, preferred_element_type=F32)

        def x_half(h):
            rows = [mt[rnd, pl.ds(pl.multiple_of(i * 32 + h * 16, 16), 16), :] for i in range(4)]
            half = folded(jnp.dot(twice(jnp.concatenate(rows, axis=0)), at[...], preferred_element_type=F32))
            for i in range(4):
                for m in range(8):
                    xs[rnd, h, i * 8 + m] = half[i * 16 : i * 16 + 16, m * 128 : m * 128 + 128]

        x_half(o)
        send(xs.at[rnd, o], xcore.at[rnd], rnd, XC, partner)
        gown[rnd] = lax.dot_general(
            mt[rnd, pl.ds(pl.multiple_of(z * 32, 32), 32), :], mt[rnd], NT, precision=HIGHEST, preferred_element_type=F32
        )
        send(gown.at[rnd], gcore.at[rnd], rnd, GC, partner)
        x_half(c)
        landed(xcore.at[rnd], rnd, XC)
        xown[rnd] = xs[rnd, c] + xcore[rnd]

        def reduce_x(k, carry):
            x2, t2 = layer_peer(k)
            send(xown.at[rnd, x2 * 8 + t2], xrs.at[rnd, mine], rnd, XR, (z, x2, t2 * 2 + c))
            return carry

        lax.fori_loop(1, 32, reduce_x, 0)
        xrs[rnd, mine] = xown[rnd, mine]
        landed(gcore.at[rnd], rnd, GC)
        gsum[rnd] = gown[rnd] + gcore[rnd]

        def reduce_g(k, carry):
            t2 = (t + k) % 8
            send(gsum.at[rnd], grs.at[rnd, t], rnd, GR, (z, x, t2 * 2 + c))
            return carry

        lax.fori_loop(1, 8, reduce_g, 0)
        grs[rnd, t] = gsum[rnd]
        landed(xrs.at[rnd, pl.ds(0, 31)], rnd, XR)
        total = xrs[rnd, 0]
        for i in range(1, 32):
            total = total + xrs[rnd, i]
        xt[rnd, c, t] = total

        def gather_x(k, carry):
            t2 = (t + k) % 8
            piece = xt.at[rnd, c, t]
            send(piece, piece, rnd, XG, (z, x, t2 * 2 + c))
            return carry

        lax.fori_loop(1, 8, gather_x, 0)
        landed(grs.at[rnd, pl.ds(0, 7)], rnd, GR)
        total = grs[rnd, 0]
        for i in range(1, 8):
            total = total + grs[rnd, i]
        gpart[rnd] = total
        for k in range(1, 4):
            send(gpart.at[rnd], grx.at[rnd, x], rnd, GX, (z, (x + k) % 4, j))
        grx[rnd, x] = gpart[rnd]
        landed(xt.at[rnd, c, pl.ds(0, 7)], rnd, XG)
        send(xt.at[rnd, c], xt.at[rnd, c], rnd, XX, partner)
        landed(xt.at[rnd, o], rnd, XX)

        for h in range(2):
            for m in range(8):
                high, low = terms(xt[rnd, h, m])
                xlhs[h * 16 : h * 16 + 16, m * 128 : m * 128 + 128] = high
                xlhs[32 + h * 16 : 48 + h * 16, m * 128 : m * 128 + 128] = low
        ps[rnd] = folded(jnp.dot(xlhs[...], b[...], preferred_element_type=F32)).reshape(4, 8, HID)
        for k in range(1, 4):
            z2 = (z + k) % 4
            send(ps.at[rnd, z2], prs.at[rnd, z], rnd, PR, (z2, x, j))
        prs[rnd, z] = ps[rnd, z]
        landed(grx.at[rnd, pl.ds(0, 3)], rnd, GX)
        gfull[rnd + 1, z] = (grx[rnd, 0] + grx[rnd, 1]) + (grx[rnd, 2] + grx[rnd, 3])
        for k in range(1, 4):
            piece = gfull.at[rnd + 1, z]
            send(piece, piece, rnd, GZ, ((z + k) % 4, x, j))
        landed(prs.at[rnd, pl.ds(0, 3)], rnd, PR)
        pt[rnd + 1, z] = (prs[rnd, 0] + prs[rnd, 1]) + (prs[rnd, 2] + prs[rnd, 3])
        for k in range(1, 4):
            piece = pt.at[rnd + 1, z]
            send(piece, piece, rnd, PG, ((z + k) % 4, x, j))
        landed(gfull.at[rnd + 1, pl.ds(0, 3)], rnd, GZ)
        landed(pt.at[rnd + 1, pl.ds(0, 3)], rnd, PG)
        return carry

    lax.fori_loop(0, ROUNDS, one_round, 0)

    cf[x] = pt[ROUNDS]
    mg[c, t] = mt[ROUNDS - 1]
    for k in range(1, 4):
        piece = cf.at[x]
        send(piece, piece, 0, PHASES, (z, (x + k) % 4, j))

    def gather_m(k, carry):
        t2 = (t + k) % 8
        piece = mg.at[c, t]
        send(piece, piece, 1, PHASES, (z, x, t2 * 2 + c))
        return carry

    lax.fori_loop(1, 8, gather_m, 0)
    factor_start(ROUNDS)
    factor_blocks(0, 16)
    linv[ROUNDS] = work[:, RANK:]
    landed(mg.at[c, pl.ds(0, 7)], 1, PHASES)
    send(mg.at[c], mg.at[c], 2, PHASES, partner)
    last = linv[ROUNDS]
    scaled = last * math.sqrt(D)

    def emit_basis(h):
        for i in range(8):
            rows = pl.ds(pl.multiple_of((i * 2 + h) * 128, 128), 128)
            basis_ref[rows, :] = lax.dot_general(
                mg[h, i].T, scaled, NT, precision=HIGHEST, preferred_element_type=F32
            )

    emit_basis(c)
    landed(mg.at[o], 2, PHASES)
    emit_basis(o)
    landed(cf.at[pl.ds(0, 3)], 0, PHASES)
    coef_ref[...] = jnp.dot(last, cf[...].reshape(RANK, HID), precision=HIGHEST, preferred_element_type=F32)

    def drain(rnd, carry):
        left(ycore.at[rnd], rnd, YC)
        left(yrs.at[rnd, pl.ds(0, 7)], rnd, YR)
        left(yt.at[rnd, 0, pl.ds(0, 31)], rnd, YG)
        left(yt.at[rnd, 0], rnd, YX)
        left(mzs.at[rnd, pl.ds(0, 3)], rnd, MZ)
        left(xcore.at[rnd], rnd, XC)
        left(xrs.at[rnd, pl.ds(0, 31)], rnd, XR)
        left(xt.at[rnd, 0, pl.ds(0, 7)], rnd, XG)
        left(xt.at[rnd, 0], rnd, XX)
        left(prs.at[rnd, pl.ds(0, 3)], rnd, PR)
        left(pt.at[rnd, pl.ds(0, 3)], rnd, PG)
        left(gcore.at[rnd], rnd, GC)
        left(grs.at[rnd, pl.ds(0, 7)], rnd, GR)
        left(grx.at[rnd, pl.ds(0, 3)], rnd, GX)
        left(gfull.at[rnd, pl.ds(0, 3)], rnd, GZ)
        return carry

    lax.fori_loop(0, ROUNDS, drain, 0)
    left(cf.at[pl.ds(0, 3)], 0, PHASES)
    left(mg.at[0, pl.ds(0, 7)], 1, PHASES)
    left(mg.at[0], 2, PHASES)


def body(activations, grad_out, sketch):
    anywhere = pl.BlockSpec(memory_space=pl.ANY)
    inside = pl.BlockSpec(memory_space=pltpu.VMEM)
    vm = pltpu.VMEM
    n = ROUNDS
    return pl.pallas_call(
        kernel,
        name="range_finder",
        out_shape=(
            jax.ShapeDtypeStruct((2048, RANK), F32),
            jax.ShapeDtypeStruct((RANK, HID), F32),
        ),
        in_specs=[anywhere] * 3,
        out_specs=(inside, inside),
        scratch_shapes=[
            vm((TOK, 128), BF16),
            vm((128, TOK), BF16),
            vm((TOK, HID), BF16),
            vm((HID, RANK), F32),
            vm((RANK, HID), F32),
            vm((n + 1, 4, 8, HID), F32),
            vm((n, 2, 8, 16, 128), F32),
            vm((n, 8, 16, 128), F32),
            vm((n, 8, 16, 128), F32),
            vm((n, 8, 16, 128), F32),
            vm((n, 2, 32, 16, 128), F32),
            vm((128, TOK), BF16),
            vm((n, 4, RANK, 128), F32),
            vm((n, RANK, 128), F32),
            vm((n, 2, 32, 16, 128), F32),
            vm((n, 32, 16, 128), F32),
            vm((n, 32, 16, 128), F32),
            vm((n, 32, 16, 128), F32),
            vm((n, 2, 8, 16, 128), F32),
            vm((64, TOK), BF16),
            vm((n, 4, 8, HID), F32),
            vm((n, 4, 8, HID), F32),
            vm((n, 32, RANK), F32),
            vm((n, 32, RANK), F32),
            vm((n, 32, RANK), F32),
            vm((n, 8, 32, RANK), F32),
            vm((n, 32, RANK), F32),
            vm((n, 4, 32, RANK), F32),
            vm((n + 1, 4, 32, RANK), F32),
            vm((RANK, 2 * RANK), F32),
            vm((n + 1, RANK, RANK), F32),
            vm((4, 4, 8, HID), F32),
            vm((2, 8, RANK, 128), F32),
            pltpu.SemaphoreType.DMA((3,)),
            pltpu.SemaphoreType.DMA((n, PHASES + 1)),
            pltpu.SemaphoreType.DMA((n, PHASES + 1)),
        ],
        compiler_params=pltpu.CompilerParams(
            collective_id=0, has_side_effects=True, vmem_limit_bytes=48 * 2**20
        ),
    )(activations, grad_out, sketch)


def solution(mesh):
    in_specs = (P("dp", "row"), P("dp", "col"), P("col", None))
    out_specs = (P("row", None), P(None, "col"))
    return jax.shard_map(body, mesh=mesh, in_specs=in_specs, out_specs=out_specs, check_vma=False)
```

```python
import functools
import math

import jax
import jax.numpy as jnp
from jax import lax
from jax.experimental import pallas as pl
from jax.experimental.pallas import tpu as pltpu
from jax.sharding import PartitionSpec as P

MESH = pl.DeviceIdType.MESH
F32 = jnp.float32
BF16 = jnp.bfloat16
HIGHEST = lax.Precision.HIGHEST
D = 8192
RANK = 128
ROUNDS = 3
TOK = 1024
HID = 1664
FEAT = 512
NT = (((1,), (1,)), ((), ()))
TN = (((0,), (0,)), ((), ()))
PARTS = ((0, 896), (896, 768))
YC, YR, YG, MR, MG, MC, XR, XG, XC, PRA, PRB, PGA, PGB, GY, GX, GZ = range(16)
PR, PG = (PRA, PRB), (PGA, PGB)
PHASES = 16
HY = ((1, 2), (1, 1), (1, 3), (1, 0), (0, 2), (0, 1), (0, 3))
XY = (
    (2, 2), (2, 1), (2, 3), (1, 2), (3, 2), (1, 1), (1, 3), (3, 1), (3, 3),
    (2, 0), (0, 2), (1, 0), (3, 0), (0, 1), (0, 3),
)
ZH = ((2, 1), (1, 1), (3, 1), (0, 1), (2, 0), (1, 0), (3, 0))


def stacked(mat):
    high = mat.astype(BF16)
    rest = mat - high.astype(F32)
    mid = rest.astype(BF16)
    low = (rest - mid.astype(F32)).astype(BF16)
    return jnp.concatenate([high, mid, low], axis=0)


def folded(wide):
    rows = wide.shape[0] // 3
    return wide[:rows] + (wide[rows : 2 * rows] + wide[2 * rows :])


def kernel(
    a_hbm, b_hbm, s_hbm, basis_ref, coef_ref,
    a, b, s, st, pt, ysend, ycore, yown, yrs, yt, ms, mrs, mraw, mfull, mt, xs, xrs, xt,
    ps, prs, gown, gys, gsum, gxs, gfull, work, linv, cf, mg,
    load_sem, send_sem, recv_sem,
):
    z, x, j = lax.axis_index("dp"), lax.axis_index("row"), lax.axis_index("col")
    c = j % 2
    y = (j // 2) % 4
    h = j // 8
    o = 1 - c
    mine_hy = h * 4 + y
    mine_xy = x * 4 + y
    mine_hz = h * 4 + z

    def dev(z_, x_, h_, y_, c_):
        return (z_, x_, (h_ * 4 + y_) * 2 + c_)

    partner = dev(z, x, h, y, o)
    hy_peers = [((h + dh) % 2, (y + dy) % 4) for dh, dy in HY]
    xy_peers = [((x + dx) % 4, (y + dy) % 4) for dx, dy in XY]
    zh_peers = [((z + dz) % 4, (h + dh) % 2) for dz, dh in ZH]
    z_peers = [(z + k) % 4 for k in (2, 1, 3)]
    y_peers = [(y + k) % 4 for k in (2, 1, 3)]
    x_peers = [(x + k) % 4 for k in (2, 1, 3)]

    barrier = pltpu.get_barrier_semaphore()

    def greet(device):
        pl.semaphore_signal(barrier, inc=1, device_id=device, device_id_type=MESH)

    loads = [
        pltpu.make_async_copy(s_hbm, s, load_sem.at[0]),
        pltpu.make_async_copy(b_hbm, b, load_sem.at[1]),
        pltpu.make_async_copy(
            a_hbm.at[:, pl.ds(pl.multiple_of(y * FEAT, FEAT), FEAT)], a, load_sem.at[2]
        ),
    ]
    for load in loads:
        load.start()

    for h2, y2 in hy_peers:
        greet(dev(z, x, h2, y2, c))
    for (x2, y2), (dx, _) in zip(xy_peers, XY):
        if dx:
            greet(dev(z, x2, h, y2, c))
    for (z2, h2), (dz, _) in zip(zh_peers, ZH):
        if dz:
            greet(dev(z2, x, h2, y, c))
    greet(partner)

    def send(src, dst, rnd, phase, device):
        pltpu.make_async_remote_copy(
            src_ref=src,
            dst_ref=dst,
            send_sem=send_sem.at[rnd, phase],
            recv_sem=recv_sem.at[rnd, phase],
            device_id=device,
            device_id_type=MESH,
        ).start()

    def landed(like, rnd, phase):
        pltpu.make_async_copy(like, like, recv_sem.at[rnd, phase]).wait()

    def left(like, rnd, phase):
        pltpu.make_async_copy(like, like, send_sem.at[rnd, phase]).wait()

    row_iota = lax.broadcasted_iota(jnp.int32, (RANK, RANK), 0)
    col_iota = lax.broadcasted_iota(jnp.int32, (RANK, RANK), 1)
    eye = jnp.where(row_iota == col_iota, 1.0, 0.0).astype(F32)

    def factor_start(rnd):
        work[:, :RANK] = gfull[rnd].reshape(RANK, RANK)
        work[:, RANK:] = eye

    sub = lax.broadcasted_iota(jnp.int32, (8, RANK), 0)
    lane = lax.broadcasted_iota(jnp.int32, (8, RANK), 1)

    def spread(row):
        return jnp.broadcast_to(row, (8, RANK))

    def factor_block(blk, carry):
        r0 = pl.multiple_of(blk * 8, 8)
        gp = work[pl.ds(r0, 8), :RANK]
        ep = work[pl.ds(r0, 8), RANK:]
        diag = pltpu.roll(gp, RANK - r0, 1)
        cols = [jnp.broadcast_to(diag[:, i : i + 1], (8, RANK)) for i in range(8)]
        inv = [jnp.where(sub == i, 1.0, 0.0).astype(F32) for i in range(8)]
        pivots = jnp.ones((8, RANK), F32)
        for i in range(8):
            pivot = spread(cols[i][i : i + 1])
            pivots = jnp.where(sub == i, pivot, pivots)
            if i == 7:
                break
            scale = jnp.where(sub > i, cols[i] * (1.0 / pivot), 0.0)
            for m in range(i + 1, 8):
                cols[m] = cols[m] - scale * spread(cols[m][i : i + 1])
            for m in range(i + 1):
                inv[m] = inv[m] - scale * spread(inv[m][i : i + 1])
        root = lax.rsqrt(pivots)
        root = root * (1.5 - 0.5 * pivots * root * root)
        ug = jnp.zeros((8, RANK), F32)
        ue = jnp.zeros((8, RANK), F32)
        for m in range(8):
            weight = inv[m] * root
            ug = ug + weight * spread(gp[m : m + 1])
            ue = ue + weight * spread(ep[m : m + 1])
        work[pl.ds(r0, 8), RANK:] = ue
        rest = jnp.where(lane >= r0 + 8, ug, 0.0)
        work[...] -= lax.dot_general(
            rest, jnp.concatenate([ug, ue], axis=1), TN, precision=HIGHEST, preferred_element_type=F32
        )
        return carry

    def factor_blocks(lo, hi):
        lax.fori_loop(lo, hi, factor_block, 0)

    def tokens_part(rnd):
        lhs = stacked(pt[rnd].reshape(32, HID))
        part = folded(lax.dot_general(lhs, b[...], NT, preferred_element_type=F32))
        for i in range(4):
            for m in range(4):
                ysend[rnd, i // 2, (i % 2) * 4 + m] = part[i * 8 : i * 8 + 8, m * 256 : m * 256 + 256]

    loads[0].wait()
    st[...] = s[...].T
    pt[0] = st[pl.ds(pl.multiple_of(x * 32, 32), 32), :].reshape(4, 8, HID)
    work[:, :RANK] = eye
    work[:, RANK:] = eye
    loads[1].wait()
    tokens_part(0)
    loads[2].wait()

    pl.semaphore_wait(barrier, 26)

    def one_round(rnd, carry):
        send(ysend.at[rnd, o], ycore.at[rnd], rnd, YC, partner)
        landed(ycore.at[rnd], rnd, YC)
        yown[rnd] = ysend[rnd, c] + ycore[rnd]
        for h2, y2 in hy_peers:
            send(yown.at[rnd, h2 * 4 + y2], yrs.at[rnd, mine_hy], rnd, YR, dev(z, x, h2, y2, c))
        yrs[rnd, mine_hy] = yown[rnd, mine_hy]
        factor_blocks(6, 12)
        landed(yrs.at[rnd, pl.ds(0, 7)], rnd, YR)
        total = yrs[rnd, 0]
        for i in range(1, 8):
            total = total + yrs[rnd, i]
        yt[rnd, mine_xy] = total
        for x2, y2 in xy_peers:
            piece = yt.at[rnd, mine_xy]
            send(piece, piece, rnd, YG, dev(z, x2, h, y2, c))
        factor_blocks(12, 16)
        linv[rnd] = work[:, RANK:]
        landed(yt.at[rnd, pl.ds(0, 15)], rnd, YG)

        rows = [jnp.concatenate([yt[rnd, i * 4 + m] for m in range(4)], axis=1) for i in range(4)]
        lhs = stacked(jnp.concatenate(rows, axis=0))
        part = folded(jnp.dot(lhs, a[...], preferred_element_type=F32))
        for i in range(4):
            ms[rnd, i] = part[:, i * 128 : i * 128 + 128]
        for z2 in z_peers:
            send(ms.at[rnd, z2], mrs.at[rnd, z], rnd, MR, dev(z2, x, h, y, c))
        mrs[rnd, z] = ms[rnd, z]
        landed(mrs.at[rnd, pl.ds(0, 3)], rnd, MR)
        mraw[rnd, c, mine_hz] = (mrs[rnd, 0] + mrs[rnd, 1]) + (mrs[rnd, 2] + mrs[rnd, 3])
        for z2, h2 in zh_peers:
            piece = mraw.at[rnd, c, mine_hz]
            send(piece, piece, rnd, MG, dev(z2, x, h2, y, c))
        landed(mraw.at[rnd, c, pl.ds(0, 7)], rnd, MG)
        send(mraw.at[rnd, c], mraw.at[rnd, c], rnd, MC, partner)
        landed(mraw.at[rnd, o], rnd, MC)
        for cc in range(2):
            for hh in range(2):
                for zz in range(4):
                    for i in range(4):
                        r0 = i * 32 + cc * 16 + hh * 8
                        mfull[r0 : r0 + 8, zz * 128 : zz * 128 + 128] = mraw[
                            rnd, cc, hh * 4 + zz, i * 8 : i * 8 + 8, :
                        ]
        mt[rnd] = jnp.dot(linv[rnd], mfull[...], precision=HIGHEST, preferred_element_type=F32)

        rows = [mt[rnd, pl.ds(pl.multiple_of(i * 32 + c * 16 + h * 8, 8), 8), :] for i in range(4)]
        lhs = stacked(jnp.concatenate(rows, axis=0))
        part = folded(lax.dot_general(lhs, a[...], NT, preferred_element_type=F32))
        for i in range(4):
            for m in range(4):
                xs[rnd, i * 4 + m] = part[i * 8 : i * 8 + 8, m * 256 : m * 256 + 256]
        for x2, y2 in xy_peers:
            send(xs.at[rnd, x2 * 4 + y2], xrs.at[rnd, mine_xy], rnd, XR, dev(z, x2, h, y2, c))
        xrs[rnd, mine_xy] = xs[rnd, mine_xy]
        gown[rnd] = lax.dot_general(
            mt[rnd, pl.ds(pl.multiple_of(z * 32, 32), 32), :], mt[rnd], NT, precision=HIGHEST, preferred_element_type=F32
        )
        for y2 in y_peers:
            send(gown.at[rnd], gys.at[rnd, y], rnd, GY, dev(z, x, h, y2, c))
        gys[rnd, y] = gown[rnd]
        landed(xrs.at[rnd, pl.ds(0, 15)], rnd, XR)
        total = xrs[rnd, 0]
        for i in range(1, 16):
            total = total + xrs[rnd, i]
        xt[rnd, c, mine_hy] = total
        for h2, y2 in hy_peers:
            piece = xt.at[rnd, c, mine_hy]
            send(piece, piece, rnd, XG, dev(z, x, h2, y2, c))
        landed(gys.at[rnd, pl.ds(0, 3)], rnd, GY)
        gsum[rnd] = (gys[rnd, 0] + gys[rnd, 1]) + (gys[rnd, 2] + gys[rnd, 3])
        for x2 in x_peers:
            send(gsum.at[rnd], gxs.at[rnd, x], rnd, GX, dev(z, x2, h, y, c))
        gxs[rnd, x] = gsum[rnd]

        landed(xt.at[rnd, c, pl.ds(0, 7)], rnd, XG)
        send(xt.at[rnd, c], xt.at[rnd, c], rnd, XC, partner)

        @pl.when(rnd == ROUNDS - 1)
        def _():
            for y2 in y_peers:
                send(
                    mt.at[rnd, :, pl.ds(pl.multiple_of(c * 256, 256), 256)],
                    mg.at[y, c],
                    0, PHASES,
                    dev(z, x, h, y2, c),
                )

        landed(xt.at[rnd, o], rnd, XC)

        rows = [jnp.concatenate([xt[rnd, i // 2, (i % 2) * 4 + m] for m in range(4)], axis=1) for i in range(4)]
        lhs = stacked(jnp.concatenate(rows, axis=0))
        for n, (lo, size) in enumerate(PARTS):
            part = folded(jnp.dot(lhs, b[:, lo : lo + size], preferred_element_type=F32))
            ps[rnd, :, :, lo : lo + size] = part.reshape(4, 8, size)
            for z2 in z_peers:
                span = pl.ds(lo, size)
                send(ps.at[rnd, z2, :, span], prs.at[rnd, z, :, span], rnd, PR[n], dev(z2, x, h, y, c))
        prs[rnd, z] = ps[rnd, z]
        landed(gxs.at[rnd, pl.ds(0, 3)], rnd, GX)
        gfull[rnd, z] = (gxs[rnd, 0] + gxs[rnd, 1]) + (gxs[rnd, 2] + gxs[rnd, 3])
        for z2 in z_peers:
            piece = gfull.at[rnd, z]
            send(piece, piece, rnd, GZ, dev(z2, x, h, y, c))
        for n, (lo, size) in enumerate(PARTS):
            span = pl.ds(lo, size)
            landed(prs.at[rnd, pl.ds(0, 3), :, span], rnd, PR[n])
            got = [prs[rnd, i, :, lo : lo + size] for i in range(4)]
            pt[rnd + 1, z, :, lo : lo + size] = (got[0] + got[1]) + (got[2] + got[3])
            for z2 in z_peers:
                piece = pt.at[rnd + 1, z, :, span]
                send(piece, piece, rnd, PG[n], dev(z2, x, h, y, c))
        landed(gfull.at[rnd, pl.ds(0, 3)], rnd, GZ)
        factor_start(rnd)
        factor_blocks(0, 6)

        @pl.when(rnd < ROUNDS - 1)
        def _():
            for n, (lo, size) in enumerate(PARTS):
                landed(pt.at[rnd + 1, pl.ds(0, 3), :, pl.ds(lo, size)], rnd, PG[n])
            tokens_part(rnd + 1)

        return carry

    lax.fori_loop(0, ROUNDS, one_round, 0)

    last = ROUNDS - 1
    for x2 in x_peers:
        send(pt.at[ROUNDS, z], cf.at[x, z], 2, PHASES, dev(z, x2, h, y, c))
    for n, (lo, size) in enumerate(PARTS):
        landed(pt.at[ROUNDS, pl.ds(0, 3), :, pl.ds(lo, size)], last, PG[n])
    for z2 in z_peers:
        for x2 in x_peers:
            send(pt.at[ROUNDS, z2], cf.at[x, z2], 2, PHASES, dev(z, x2, h, y, c))
    landed(mg.at[pl.ds(0, 3), 0], 0, PHASES)
    for y2 in y_peers:
        piece = mg.at[y2, c]
        send(piece, piece, 1, PHASES, partner)
    for cc in range(2):
        mg[y, cc] = mt[last, :, cc * 256 : cc * 256 + 256]
    cf[x] = pt[ROUNDS]
    factor_blocks(6, 16)
    final = work[:, RANK:]
    scaled = final * math.sqrt(D)
    landed(mg.at[pl.ds(0, 3), 0], 1, PHASES)
    for i in range(4):
        for cc in range(2):
            r0 = i * FEAT + cc * 256
            basis_ref[r0 : r0 + 256, :] = lax.dot_general(
                mg[i, cc].T, scaled, NT, precision=HIGHEST, preferred_element_type=F32
            )
    landed(cf.at[pl.ds(0, 3)], 2, PHASES)
    coef_ref[...] = jnp.dot(final, cf[...].reshape(RANK, HID), precision=HIGHEST, preferred_element_type=F32)

    def drain(rnd, carry):
        left(ycore.at[rnd], rnd, YC)
        left(yrs.at[rnd, pl.ds(0, 7)], rnd, YR)
        left(yt.at[rnd, pl.ds(0, 15)], rnd, YG)
        left(mrs.at[rnd, pl.ds(0, 3)], rnd, MR)
        left(mraw.at[rnd, 0, pl.ds(0, 7)], rnd, MG)
        left(mraw.at[rnd, 0], rnd, MC)
        left(xrs.at[rnd, pl.ds(0, 15)], rnd, XR)
        left(xt.at[rnd, 0, pl.ds(0, 7)], rnd, XG)
        left(xt.at[rnd, 0], rnd, XC)
        for n, (lo, size) in enumerate(PARTS):
            span = pl.ds(lo, size)
            left(prs.at[rnd, pl.ds(0, 3), :, span], rnd, PR[n])
            left(pt.at[rnd, pl.ds(0, 3), :, span], rnd, PG[n])
        left(gys.at[rnd, pl.ds(0, 3)], rnd, GY)
        left(gxs.at[rnd, pl.ds(0, 3)], rnd, GX)
        left(gfull.at[rnd, pl.ds(0, 3)], rnd, GZ)
        return carry

    lax.fori_loop(0, ROUNDS, drain, 0)
    left(mg.at[pl.ds(0, 3), 0], 0, PHASES)
    left(mg.at[pl.ds(0, 3), 0], 1, PHASES)
    left(cf.at[pl.ds(0, 3)], 2, PHASES)


def body(activations, grad_out, sketch):
    anywhere = pl.BlockSpec(memory_space=pl.ANY)
    inside = pl.BlockSpec(memory_space=pltpu.VMEM)
    vm = pltpu.VMEM
    n = ROUNDS
    return pl.pallas_call(
        kernel,
        name="range_finder",
        out_shape=(
            jax.ShapeDtypeStruct((2048, RANK), F32),
            jax.ShapeDtypeStruct((RANK, HID), F32),
        ),
        in_specs=[anywhere] * 3,
        out_specs=(inside, inside),
        scratch_shapes=[
            vm((TOK, FEAT), BF16),
            vm((TOK, HID), BF16),
            vm((HID, RANK), F32),
            vm((RANK, HID), F32),
            vm((n + 1, 4, 8, HID), F32),
            vm((n, 2, 8, 8, 256), F32),
            vm((n, 8, 8, 256), F32),
            vm((n, 8, 8, 256), F32),
            vm((n, 8, 8, 256), F32),
            vm((n, 16, 8, 256), F32),
            vm((n, 4, 32, 128), F32),
            vm((n, 4, 32, 128), F32),
            vm((n, 2, 8, 32, 128), F32),
            vm((RANK, FEAT), F32),
            vm((n, RANK, FEAT), F32),
            vm((n, 16, 8, 256), F32),
            vm((n, 16, 8, 256), F32),
            vm((n, 2, 8, 8, 256), F32),
            vm((n, 4, 8, HID), F32),
            vm((n, 4, 8, HID), F32),
            vm((n, 32, RANK), F32),
            vm((n, 4, 32, RANK), F32),
            vm((n, 32, RANK), F32),
            vm((n, 4, 32, RANK), F32),
            vm((n, 4, 32, RANK), F32),
            vm((RANK, 2 * RANK), F32),
            vm((n, RANK, RANK), F32),
            vm((4, 4, 8, HID), F32),
            vm((4, 2, RANK, 256), F32),
            pltpu.SemaphoreType.DMA((3,)),
            pltpu.SemaphoreType.DMA((n, PHASES + 1)),
            pltpu.SemaphoreType.DMA((n, PHASES + 1)),
        ],
        compiler_params=pltpu.CompilerParams(
            collective_id=0, has_side_effects=True, vmem_limit_bytes=48 * 2**20
        ),
    )(activations, grad_out, sketch)


def solution(mesh):
    in_specs = (P("dp", "row"), P("dp", "col"), P("col", None))
    out_specs = (P("row", None), P(None, "col"))
    return jax.shard_map(body, mesh=mesh, in_specs=in_specs, out_specs=out_specs, check_vma=False)
```

```python
import functools
import math

import jax
import jax.numpy as jnp
from jax import lax
from jax.experimental import pallas as pl
from jax.experimental.pallas import tpu as pltpu
from jax.sharding import PartitionSpec as P

MESH = pl.DeviceIdType.MESH
F32 = jnp.float32
BF16 = jnp.bfloat16
HIGHEST = lax.Precision.HIGHEST
D = 8192
RANK = 128
ROUNDS = 3
TOK = 1024
HID = 1664
FEAT = 512
NT = (((1,), (1,)), ((), ()))
TN = (((0,), (0,)), ((), ()))
PARTS = ((0, 896), (896, 768))
YC, YR, YG, MRA, MRB, MGA, MGB, MC, XR, XG, XC, PRA, PRB, GY, GX, GZ, GC = range(17)
MR, MG, PR = (MRA, MRB), (MGA, MGB), (PRA, PRB)
PG = (17, 21)
PHASES = 25
XY = (
    (2, 2), (2, 1), (2, 3), (1, 2), (3, 2), (1, 1), (1, 3), (3, 1), (3, 3),
    (2, 0), (0, 2), (1, 0), (3, 0), (0, 1), (0, 3),
)
ZH = ((2, 1), (1, 1), (3, 1), (0, 1), (2, 0), (1, 0), (3, 0))


def stacked(mat):
    high = mat.astype(BF16)
    rest = mat - high.astype(F32)
    mid = rest.astype(BF16)
    low = (rest - mid.astype(F32)).astype(BF16)
    return jnp.concatenate([high, mid, low], axis=0)


def folded(wide):
    rows = wide.shape[0] // 3
    return wide[:rows] + (wide[rows : 2 * rows] + wide[2 * rows :])


def kernel(
    a_hbm, b_hbm, s_hbm, basis_ref, coef_ref,
    a, b, s, st, pt, ysend, ycore, yown, yrs, yt, ms, mrs, mraw, mfull, mt, xl, xs, xrs, xt,
    ps, prs, gown, gys, gsum, gxs, gfull, work, linv, cf, mg,
    load_sem, send_sem, recv_sem,
):
    z, x, j = lax.axis_index("dp"), lax.axis_index("row"), lax.axis_index("col")
    c = j % 2
    y = (j // 2) % 4
    h = j // 8
    o = 1 - c
    mine_xy = x * 4 + y
    mine_hz = h * 4 + z

    def dev(z_, x_, h_, y_, c_):
        return (z_, x_, (h_ * 4 + y_) * 2 + c_)

    partner = dev(z, x, h, y, o)
    xy_peers = [((x + dx) % 4, (y + dy) % 4) for dx, dy in XY]
    zh_peers = [((z + dz) % 4, (h + dh) % 2) for dz, dh in ZH]
    z_peers = [(z + k) % 4 for k in (2, 1, 3)]
    y_peers = [(y + k) % 4 for k in (2, 1, 3)]
    x_peers = [(x + k) % 4 for k in (2, 1, 3)]

    barrier = pltpu.get_barrier_semaphore()

    def greet(device):
        pl.semaphore_signal(barrier, inc=1, device_id=device, device_id_type=MESH)

    loads = [
        pltpu.make_async_copy(s_hbm, s, load_sem.at[0]),
        pltpu.make_async_copy(b_hbm, b, load_sem.at[1]),
        pltpu.make_async_copy(
            a_hbm.at[:, pl.ds(pl.multiple_of(y * FEAT, FEAT), FEAT)], a, load_sem.at[2]
        ),
    ]
    for load in loads:
        load.start()

    for x2, y2 in xy_peers:
        greet(dev(z, x2, h, y2, c))
    for z2, h2 in zh_peers:
        greet(dev(z2, x, h2, y, c))
    greet(partner)

    def send(src, dst, rnd, phase, device):
        pltpu.make_async_remote_copy(
            src_ref=src,
            dst_ref=dst,
            send_sem=send_sem.at[rnd, phase],
            recv_sem=recv_sem.at[rnd, phase],
            device_id=device,
            device_id_type=MESH,
        ).start()

    def landed(like, rnd, phase):
        pltpu.make_async_copy(like, like, recv_sem.at[rnd, phase]).wait()

    def left(like, rnd, phase):
        pltpu.make_async_copy(like, like, send_sem.at[rnd, phase]).wait()

    row_iota = lax.broadcasted_iota(jnp.int32, (RANK, RANK), 0)
    col_iota = lax.broadcasted_iota(jnp.int32, (RANK, RANK), 1)
    eye = jnp.where(row_iota == col_iota, 1.0, 0.0).astype(F32)

    def factor_start(rnd):
        work[:, :RANK] = gfull[rnd].reshape(RANK, RANK)
        work[:, RANK:] = eye

    sub = lax.broadcasted_iota(jnp.int32, (8, RANK), 0)
    lane = lax.broadcasted_iota(jnp.int32, (8, RANK), 1)

    def spread(row):
        return jnp.broadcast_to(row, (8, RANK))

    def factor_block(blk, carry):
        r0 = pl.multiple_of(blk * 8, 8)
        gp = work[pl.ds(r0, 8), :RANK]
        ep = work[pl.ds(r0, 8), RANK:]
        diag = pltpu.roll(gp, RANK - r0, 1)
        cols = [jnp.broadcast_to(diag[:, i : i + 1], (8, RANK)) for i in range(8)]
        inv = [jnp.where(sub == i, 1.0, 0.0).astype(F32) for i in range(8)]
        pivots = jnp.ones((8, RANK), F32)
        for i in range(8):
            pivot = spread(cols[i][i : i + 1])
            pivots = jnp.where(sub == i, pivot, pivots)
            if i == 7:
                break
            scale = jnp.where(sub > i, cols[i] * (1.0 / pivot), 0.0)
            for m in range(i + 1, 8):
                cols[m] = cols[m] - scale * spread(cols[m][i : i + 1])
            for m in range(i + 1):
                inv[m] = inv[m] - scale * spread(inv[m][i : i + 1])
        root = lax.rsqrt(pivots)
        root = root * (1.5 - 0.5 * pivots * root * root)
        ug = jnp.zeros((8, RANK), F32)
        ue = jnp.zeros((8, RANK), F32)
        for m in range(8):
            weight = inv[m] * root
            ug = ug + weight * spread(gp[m : m + 1])
            ue = ue + weight * spread(ep[m : m + 1])
        work[pl.ds(r0, 8), RANK:] = ue
        rest = jnp.where(lane >= r0 + 8, ug, 0.0)
        work[...] -= lax.dot_general(
            rest, jnp.concatenate([ug, ue], axis=1), TN, precision=HIGHEST, preferred_element_type=F32
        )
        return carry

    def factor_blocks(lo, hi):
        lax.fori_loop(lo, hi, factor_block, 0)

    def tokens_part(rnd):
        lhs = stacked(pt[rnd].reshape(32, HID))
        part = folded(lax.dot_general(lhs, b[...], NT, preferred_element_type=F32))
        for i in range(2):
            for m in range(4):
                ysend[rnd, i, m] = part[i * 16 : i * 16 + 16, m * 256 : m * 256 + 256]

    loads[0].wait()
    st[...] = s[...].T
    pt[0] = st[pl.ds(pl.multiple_of(x * 32, 32), 32), :].reshape(4, 8, HID)
    work[:, :RANK] = eye
    work[:, RANK:] = eye
    loads[1].wait()
    tokens_part(0)
    loads[2].wait()

    pl.semaphore_wait(barrier, 23)

    def gathered_p(rnd, z2):
        for n, (lo, size) in enumerate(PARTS):
            landed(pt.at[rnd + 1, z2, :, pl.ds(lo, size)], rnd, PG[n] + z2)

    def one_round(rnd, carry):
        send(ysend.at[rnd, o], ycore.at[rnd], rnd, YC, partner)
        landed(ycore.at[rnd], rnd, YC)
        yown[rnd] = ysend[rnd, c] + ycore[rnd]
        for y2 in y_peers:
            send(yown.at[rnd, y2], yrs.at[rnd, y], rnd, YR, dev(z, x, h, y2, c))
        yrs[rnd, y] = yown[rnd, y]
        factor_blocks(6, 9)
        landed(yrs.at[rnd, pl.ds(0, 3)], rnd, YR)
        yt[rnd, mine_xy] = (yrs[rnd, 0] + yrs[rnd, 1]) + (yrs[rnd, 2] + yrs[rnd, 3])
        for x2, y2 in xy_peers:
            piece = yt.at[rnd, mine_xy]
            send(piece, piece, rnd, YG, dev(z, x2, h, y2, c))
        factor_blocks(9, 15)
        landed(yt.at[rnd, pl.ds(0, 15)], rnd, YG)

        rows = [jnp.concatenate([yt[rnd, i * 4 + m] for m in range(4)], axis=1) for i in range(4)]
        lhs = stacked(jnp.concatenate(rows, axis=0))
        for n in range(2):
            span = pl.ds(n * 256, 256)
            part = folded(jnp.dot(lhs, a[:, n * 256 : n * 256 + 256], preferred_element_type=F32))
            for i in range(8):
                ms[rnd, i, :, n * 256 : n * 256 + 256] = part[i * 8 : i * 8 + 8]
            for z2, h2 in zh_peers:
                send(
                    ms.at[rnd, h2 * 4 + z2, :, span], mrs.at[rnd, mine_hz, :, span], rnd, MR[n], dev(z2, x, h2, y, c)
                )
        mrs[rnd, mine_hz] = ms[rnd, mine_hz]
        factor_blocks(15, 16)
        linv[...] = work[:, RANK:]
        for n in range(2):
            span = pl.ds(n * 256, 256)
            landed(mrs.at[rnd, pl.ds(0, 7), :, span], rnd, MR[n])
            got = [mrs[rnd, i, :, n * 256 : n * 256 + 256] for i in range(8)]
            mraw[rnd, c, mine_hz, :, n * 256 : n * 256 + 256] = ((got[0] + got[1]) + (got[2] + got[3])) + (
                (got[4] + got[5]) + (got[6] + got[7])
            )
            for z2, h2 in zh_peers:
                piece = mraw.at[rnd, c, mine_hz, :, span]
                send(piece, piece, rnd, MG[n], dev(z2, x, h2, y, c))
        for n in range(2):
            landed(mraw.at[rnd, c, pl.ds(0, 7), :, pl.ds(n * 256, 256)], rnd, MG[n])
        send(mraw.at[rnd, c], mraw.at[rnd, c], rnd, MC, partner)

        def all_columns():
            landed(mraw.at[rnd, o], rnd, MC)
            for cc in range(2):
                for i in range(8):
                    r0 = (i // 2) * 32 + cc * 16 + (i % 2) * 8
                    mfull[r0 : r0 + 8, :] = mraw[rnd, cc, i]

        @pl.when(rnd == 0)
        def _():
            for i in range(8):
                xl[i * 8 : i * 8 + 8, :] = mraw[rnd, c, i]

        @pl.when(rnd > 0)
        def _():
            all_columns()
            mt[rnd] = jnp.dot(linv[...], mfull[...], precision=HIGHEST, preferred_element_type=F32)
            for i in range(4):
                xl[i * 16 : i * 16 + 16, :] = mt[rnd, pl.ds(pl.multiple_of(i * 32 + c * 16, 16), 16), :]

        part = folded(lax.dot_general(stacked(xl[...]), a[...], NT, preferred_element_type=F32))
        for i in range(4):
            for m in range(4):
                xs[rnd, i * 4 + m] = part[i * 16 : i * 16 + 16, m * 256 : m * 256 + 256]
        for x2, y2 in xy_peers:
            send(xs.at[rnd, x2 * 4 + y2], xrs.at[rnd, mine_xy], rnd, XR, dev(z, x2, h, y2, c))
        xrs[rnd, mine_xy] = xs[rnd, mine_xy]

        @pl.when(rnd == 0)
        def _():
            all_columns()
            mt[rnd] = mfull[...]

        gown[rnd] = lax.dot_general(
            mt[rnd, pl.ds(pl.multiple_of((c * 4 + z) * 16, 16), 16), :],
            mt[rnd], NT, precision=HIGHEST, preferred_element_type=F32,
        )
        for y2 in y_peers:
            send(gown.at[rnd], gys.at[rnd, y], rnd, GY, dev(z, x, h, y2, c))
        gys[rnd, y] = gown[rnd]
        landed(xrs.at[rnd, pl.ds(0, 15)], rnd, XR)
        total = xrs[rnd, 0]
        for i in range(1, 16):
            total = total + xrs[rnd, i]
        xt[rnd, c, y] = total
        for y2 in y_peers:
            piece = xt.at[rnd, c, y]
            send(piece, piece, rnd, XG, dev(z, x, h, y2, c))
        landed(gys.at[rnd, pl.ds(0, 3)], rnd, GY)
        gsum[rnd] = (gys[rnd, 0] + gys[rnd, 1]) + (gys[rnd, 2] + gys[rnd, 3])
        for x2 in x_peers:
            send(gsum.at[rnd], gxs.at[rnd, x], rnd, GX, dev(z, x2, h, y, c))
        gxs[rnd, x] = gsum[rnd]

        landed(xt.at[rnd, c, pl.ds(0, 3)], rnd, XG)
        send(xt.at[rnd, c], xt.at[rnd, c], rnd, XC, partner)

        @pl.when(rnd == ROUNDS - 1)
        def _():
            for y2 in y_peers:
                send(
                    mt.at[rnd, :, pl.ds(pl.multiple_of(c * 256, 256), 256)],
                    mg.at[y, c],
                    0, PHASES,
                    dev(z, x, h, y2, c),
                )

        landed(xt.at[rnd, o], rnd, XC)

        rows = [jnp.concatenate([xt[rnd, i, m] for m in range(4)], axis=1) for i in range(2)]
        lhs = stacked(jnp.concatenate(rows, axis=0))
        for n, (lo, size) in enumerate(PARTS):
            part = folded(jnp.dot(lhs, b[:, lo : lo + size], preferred_element_type=F32))
            ps[rnd, :, :, lo : lo + size] = part.reshape(4, 8, size)
            for z2 in z_peers:
                span = pl.ds(lo, size)
                send(ps.at[rnd, z2, :, span], prs.at[rnd, z, :, span], rnd, PR[n], dev(z2, x, h, y, c))
        prs[rnd, z] = ps[rnd, z]
        landed(gxs.at[rnd, pl.ds(0, 3)], rnd, GX)
        gfull[rnd, c, z] = (gxs[rnd, 0] + gxs[rnd, 1]) + (gxs[rnd, 2] + gxs[rnd, 3])
        for z2 in z_peers:
            piece = gfull.at[rnd, c, z]
            send(piece, piece, rnd, GZ, dev(z2, x, h, y, c))
        for n, (lo, size) in enumerate(PARTS):
            span = pl.ds(lo, size)
            landed(prs.at[rnd, pl.ds(0, 3), :, span], rnd, PR[n])
            got = [prs[rnd, i, :, lo : lo + size] for i in range(4)]
            pt[rnd + 1, z, :, lo : lo + size] = (got[0] + got[1]) + (got[2] + got[3])
            for z2 in z_peers:
                piece = pt.at[rnd + 1, z, :, span]
                send(piece, piece, rnd, PG[n] + z, dev(z2, x, h, y, c))
        landed(gfull.at[rnd, c, pl.ds(0, 3)], rnd, GZ)
        send(gfull.at[rnd, c], gfull.at[rnd, c], rnd, GC, partner)
        landed(gfull.at[rnd, o], rnd, GC)
        factor_start(rnd)
        factor_blocks(0, 6)

        @pl.when(rnd < ROUNDS - 1)
        def _():
            for z2 in z_peers:
                gathered_p(rnd, z2)
            tokens_part(rnd + 1)

        return carry

    lax.fori_loop(0, ROUNDS, one_round, 0)

    last = ROUNDS - 1
    for x2 in x_peers:
        send(pt.at[ROUNDS, z], cf.at[x, z], 2, PHASES, dev(z, x2, h, y, c))
    for k in (1, 3, 2):
        z2 = (z + k) % 4
        gathered_p(last, z2)
        for x2 in x_peers:
            send(pt.at[ROUNDS, z2], cf.at[x, z2], 2, PHASES, dev(z, x2, h, y, c))
    landed(mg.at[pl.ds(0, 3), 0], 0, PHASES)
    for y2 in y_peers:
        piece = mg.at[y2, c]
        send(piece, piece, 1, PHASES, partner)
    for cc in range(2):
        mg[y, cc] = mt[last, :, cc * 256 : cc * 256 + 256]
    cf[x] = pt[ROUNDS]
    factor_blocks(6, 16)
    final = work[:, RANK:]
    scaled = final * math.sqrt(D)
    landed(mg.at[pl.ds(0, 3), 0], 1, PHASES)
    for i in range(4):
        for cc in range(2):
            r0 = i * FEAT + cc * 256
            basis_ref[r0 : r0 + 256, :] = lax.dot_general(
                mg[i, cc].T, scaled, NT, precision=HIGHEST, preferred_element_type=F32
            )
    landed(cf.at[pl.ds(0, 3)], 2, PHASES)
    coef_ref[...] = jnp.dot(final, cf[...].reshape(RANK, HID), precision=HIGHEST, preferred_element_type=F32)

    def drain(rnd, carry):
        left(ycore.at[rnd], rnd, YC)
        left(yrs.at[rnd, pl.ds(0, 3)], rnd, YR)
        left(yt.at[rnd, pl.ds(0, 15)], rnd, YG)
        for n in range(2):
            span = pl.ds(n * 256, 256)
            left(mrs.at[rnd, pl.ds(0, 7), :, span], rnd, MR[n])
            left(mraw.at[rnd, 0, pl.ds(0, 7), :, span], rnd, MG[n])
        left(mraw.at[rnd, 0], rnd, MC)
        left(xrs.at[rnd, pl.ds(0, 15)], rnd, XR)
        left(xt.at[rnd, 0, pl.ds(0, 3)], rnd, XG)
        left(xt.at[rnd, 0], rnd, XC)
        for n, (lo, size) in enumerate(PARTS):
            span = pl.ds(lo, size)
            left(prs.at[rnd, pl.ds(0, 3), :, span], rnd, PR[n])
            left(pt.at[rnd, pl.ds(0, 3), :, span], rnd, PG[n] + z)
        left(gys.at[rnd, pl.ds(0, 3)], rnd, GY)
        left(gxs.at[rnd, pl.ds(0, 3)], rnd, GX)
        left(gfull.at[rnd, 0, pl.ds(0, 3)], rnd, GZ)
        left(gfull.at[rnd, 0], rnd, GC)
        return carry

    lax.fori_loop(0, ROUNDS, drain, 0)
    left(mg.at[pl.ds(0, 3), 0], 0, PHASES)
    left(mg.at[pl.ds(0, 3), 0], 1, PHASES)
    left(cf.at[pl.ds(0, 3)], 2, PHASES)


def body(activations, grad_out, sketch):
    anywhere = pl.BlockSpec(memory_space=pl.ANY)
    inside = pl.BlockSpec(memory_space=pltpu.VMEM)
    vm = pltpu.VMEM
    n = ROUNDS
    return pl.pallas_call(
        kernel,
        name="range_finder",
        out_shape=(
            jax.ShapeDtypeStruct((2048, RANK), F32),
            jax.ShapeDtypeStruct((RANK, HID), F32),
        ),
        in_specs=[anywhere] * 3,
        out_specs=(inside, inside),
        scratch_shapes=[
            vm((TOK, FEAT), BF16),
            vm((TOK, HID), BF16),
            vm((HID, RANK), F32),
            vm((RANK, HID), F32),
            vm((n + 1, 4, 8, HID), F32),
            vm((n, 2, 4, 16, 256), F32),
            vm((n, 4, 16, 256), F32),
            vm((n, 4, 16, 256), F32),
            vm((n, 4, 16, 256), F32),
            vm((n, 16, 16, 256), F32),
            vm((n, 8, 8, FEAT), F32),
            vm((n, 8, 8, FEAT), F32),
            vm((n, 2, 8, 8, FEAT), F32),
            vm((RANK, FEAT), F32),
            vm((n, RANK, FEAT), F32),
            vm((64, FEAT), F32),
            vm((n, 16, 16, 256), F32),
            vm((n, 16, 16, 256), F32),
            vm((n, 2, 4, 16, 256), F32),
            vm((n, 4, 8, HID), F32),
            vm((n, 4, 8, HID), F32),
            vm((n, 16, RANK), F32),
            vm((n, 4, 16, RANK), F32),
            vm((n, 16, RANK), F32),
            vm((n, 4, 16, RANK), F32),
            vm((n, 2, 4, 16, RANK), F32),
            vm((RANK, 2 * RANK), F32),
            vm((RANK, RANK), F32),
            vm((4, 4, 8, HID), F32),
            vm((4, 2, RANK, 256), F32),
            pltpu.SemaphoreType.DMA((3,)),
            pltpu.SemaphoreType.DMA((n, PHASES + 1)),
            pltpu.SemaphoreType.DMA((n, PHASES + 1)),
        ],
        compiler_params=pltpu.CompilerParams(
            collective_id=0, has_side_effects=True, vmem_limit_bytes=60 * 2**20
        ),
    )(activations, grad_out, sketch)


def solution(mesh):
    in_specs = (P("dp", "row"), P("dp", "col"), P("col", None))
    out_specs = (P("row", None), P(None, "col"))
    return jax.shard_map(body, mesh=mesh, in_specs=in_specs, out_specs=out_specs, check_vma=False)
```

```python
import functools
import math

import jax
import jax.numpy as jnp
from jax import lax
from jax.experimental import pallas as pl
from jax.experimental.pallas import tpu as pltpu
from jax.sharding import PartitionSpec as P

MESH = pl.DeviceIdType.MESH
F32 = jnp.float32
BF16 = jnp.bfloat16
HIGHEST = lax.Precision.HIGHEST
D = 8192
RANK = 128
ROUNDS = 3
TOK = 1024
HID = 1664
FEAT = 512
NT = (((1,), (1,)), ((), ()))
TN = (((0,), (0,)), ((), ()))
PARTS = ((0, 896), (896, 768))
YR, YG, MRA, MRB, MGA, MGB, MC, XR, XG, PRA, PRB, GY, GX, GZ, GC = range(15)
MR, MG, PR = (MRA, MRB), (MGA, MGB), (PRA, PRB)
PG = (15, 19)
PHASES = 23
XY = (
    (2, 2), (2, 1), (2, 3), (1, 2), (3, 2), (1, 1), (1, 3), (3, 1), (3, 3),
    (2, 0), (0, 2), (1, 0), (3, 0), (0, 1), (0, 3),
)
ZH = ((2, 1), (1, 1), (3, 1), (0, 1), (2, 0), (1, 0), (3, 0))


def stacked(mat):
    high = mat.astype(BF16)
    rest = mat - high.astype(F32)
    mid = rest.astype(BF16)
    low = (rest - mid.astype(F32)).astype(BF16)
    return jnp.concatenate([high, mid, low], axis=0)


def folded(wide):
    rows = wide.shape[0] // 3
    return wide[:rows] + (wide[rows : 2 * rows] + wide[2 * rows :])


def kernel(
    a_hbm, b_hbm, s_hbm, basis_ref, coef_ref,
    a, b, s, st, pt, ysend, yrs, yt, ms, mrs, mraw, mfull, mt, xl, xs, xrs, xt,
    ps, prs, gown, gys, gsum, gxs, gfull, work, cf, mg,
    load_sem, send_sem, recv_sem,
):
    z, x, j = lax.axis_index("dp"), lax.axis_index("row"), lax.axis_index("col")
    c = j % 2
    y = (j // 2) % 4
    h = j // 8
    o = 1 - c
    mine_xy = x * 4 + y
    mine_hz = h * 4 + z
    mine_cy = c * 4 + y

    def dev(z_, x_, h_, y_, c_):
        return (z_, x_, (h_ * 4 + y_) * 2 + c_)

    partner = dev(z, x, h, y, o)
    xy_peers = [((x + dx) % 4, (y + dy) % 4) for dx, dy in XY]
    zh_peers = [((z + dz) % 4, (h + dh) % 2) for dz, dh in ZH]
    z_peers = [(z + k) % 4 for k in (2, 1, 3)]
    y_peers = [(y + k) % 4 for k in (2, 1, 3)]
    yc_peers = [((y + k) % 4, c2) for k in (2, 1, 3) for c2 in (c, o)] + [(y, o)]
    x_peers = [(x + k) % 4 for k in (2, 1, 3)]

    barrier = pltpu.get_barrier_semaphore()

    def greet(device):
        pl.semaphore_signal(barrier, inc=1, device_id=device, device_id_type=MESH)

    loads = [
        pltpu.make_async_copy(s_hbm, s, load_sem.at[0]),
        pltpu.make_async_copy(b_hbm, b, load_sem.at[1]),
        pltpu.make_async_copy(
            a_hbm.at[:, pl.ds(pl.multiple_of(y * FEAT, FEAT), FEAT)], a, load_sem.at[2]
        ),
    ]
    for load in loads:
        load.start()

    for (x2, y2), (dx, _) in zip(xy_peers, XY):
        if dx:
            greet(dev(z, x2, h, y2, c))
    for z2, h2 in zh_peers:
        greet(dev(z2, x, h2, y, c))
    for y2, c2 in yc_peers:
        greet(dev(z, x, h, y2, c2))

    def send(src, dst, rnd, phase, device):
        pltpu.make_async_remote_copy(
            src_ref=src,
            dst_ref=dst,
            send_sem=send_sem.at[rnd, phase],
            recv_sem=recv_sem.at[rnd, phase],
            device_id=device,
            device_id_type=MESH,
        ).start()

    def landed(like, rnd, phase):
        pltpu.make_async_copy(like, like, recv_sem.at[rnd, phase]).wait()

    def left(like, rnd, phase):
        pltpu.make_async_copy(like, like, send_sem.at[rnd, phase]).wait()

    row_iota = lax.broadcasted_iota(jnp.int32, (RANK, RANK), 0)
    col_iota = lax.broadcasted_iota(jnp.int32, (RANK, RANK), 1)
    eye = jnp.where(row_iota == col_iota, 1.0, 0.0).astype(F32)

    def factor_start(rnd):
        work[:, :RANK] = gfull[rnd].reshape(RANK, RANK)
        work[:, RANK:] = eye

    sub = lax.broadcasted_iota(jnp.int32, (8, RANK), 0)
    lane = lax.broadcasted_iota(jnp.int32, (8, RANK), 1)

    def spread(row):
        return jnp.broadcast_to(row, (8, RANK))

    def factor_block(blk, carry):
        r0 = pl.multiple_of(blk * 8, 8)
        gp = work[pl.ds(r0, 8), :RANK]
        ep = work[pl.ds(r0, 8), RANK:]
        diag = pltpu.roll(gp, RANK - r0, 1)
        cols = [jnp.broadcast_to(diag[:, i : i + 1], (8, RANK)) for i in range(8)]
        inv = [jnp.where(sub == i, 1.0, 0.0).astype(F32) for i in range(8)]
        pivots = jnp.ones((8, RANK), F32)
        for i in range(8):
            pivot = spread(cols[i][i : i + 1])
            pivots = jnp.where(sub == i, pivot, pivots)
            if i == 7:
                break
            scale = jnp.where(sub > i, cols[i] * (1.0 / pivot), 0.0)
            for m in range(i + 1, 8):
                cols[m] = cols[m] - scale * spread(cols[m][i : i + 1])
            for m in range(i + 1):
                inv[m] = inv[m] - scale * spread(inv[m][i : i + 1])
        root = lax.rsqrt(pivots)
        root = root * (1.5 - 0.5 * pivots * root * root)
        ug = jnp.zeros((8, RANK), F32)
        ue = jnp.zeros((8, RANK), F32)
        for m in range(8):
            weight = inv[m] * root
            ug = ug + weight * spread(gp[m : m + 1])
            ue = ue + weight * spread(ep[m : m + 1])
        work[pl.ds(r0, 8), RANK:] = ue
        rest = jnp.where(lane >= r0 + 8, ug, 0.0)
        work[...] -= lax.dot_general(
            rest, jnp.concatenate([ug, ue], axis=1), TN, precision=HIGHEST, preferred_element_type=F32
        )
        return carry

    def factor_blocks(lo, hi):
        lax.fori_loop(lo, hi, factor_block, 0)

    def tokens_part(rnd, ready):
        part = None
        for n, (lo, size) in enumerate(PARTS):
            ready(n)
            lhs = stacked(pt[rnd, :, :, lo : lo + size].reshape(32, size))
            term = folded(lax.dot_general(lhs, b[:, lo : lo + size], NT, preferred_element_type=F32))
            part = term if part is None else part + term
        for i in range(2):
            for m in range(4):
                ysend[rnd, i * 4 + m] = part[i * 16 : i * 16 + 16, m * 256 : m * 256 + 256]

    loads[0].wait()
    st[...] = s[...].T
    pt[0] = st[pl.ds(pl.multiple_of(x * 32, 32), 32), :].reshape(4, 8, HID)
    loads[1].wait()
    tokens_part(0, lambda n: None)
    loads[2].wait()

    pl.semaphore_wait(barrier, 26)

    def gathered_p(rnd, n, z2):
        lo, size = PARTS[n]
        landed(pt.at[rnd + 1, z2, :, pl.ds(lo, size)], rnd, PG[n] + z2)

    def one_round(rnd, carry):
        for y2, c2 in yc_peers:
            send(ysend.at[rnd, c2 * 4 + y2], yrs.at[rnd, mine_cy], rnd, YR, dev(z, x, h, y2, c2))
        yrs[rnd, mine_cy] = ysend[rnd, mine_cy]

        @pl.when(rnd > 0)
        def _():
            landed(gfull.at[rnd - 1, o], rnd - 1, GC)
            factor_start(rnd - 1)
            factor_blocks(0, 4)

        landed(yrs.at[rnd, pl.ds(0, 7)], rnd, YR)
        got = [yrs[rnd, i] for i in range(8)]
        yt[rnd, mine_xy] = ((got[0] + got[1]) + (got[2] + got[3])) + ((got[4] + got[5]) + (got[6] + got[7]))
        for x2, y2 in xy_peers:
            piece = yt.at[rnd, mine_xy]
            send(piece, piece, rnd, YG, dev(z, x2, h, y2, c))

        @pl.when(rnd > 0)
        def _():
            factor_blocks(4, 9)

        landed(yt.at[rnd, pl.ds(0, 15)], rnd, YG)

        rows = [jnp.concatenate([yt[rnd, i * 4 + m] for m in range(4)], axis=1) for i in range(4)]
        lhs = stacked(jnp.concatenate(rows, axis=0))
        for n in range(2):
            span = pl.ds(n * 256, 256)
            part = folded(jnp.dot(lhs, a[:, n * 256 : n * 256 + 256], preferred_element_type=F32))
            for i in range(8):
                ms[rnd, i, :, n * 256 : n * 256 + 256] = part[i * 8 : i * 8 + 8]
            for z2, h2 in zh_peers:
                send(
                    ms.at[rnd, h2 * 4 + z2, :, span], mrs.at[rnd, mine_hz, :, span], rnd, MR[n], dev(z2, x, h2, y, c)
                )
        mrs[rnd, mine_hz] = ms[rnd, mine_hz]

        @pl.when(rnd > 0)
        def _():
            factor_blocks(9, 14)

        for n in range(2):
            span = pl.ds(n * 256, 256)
            landed(mrs.at[rnd, pl.ds(0, 7), :, span], rnd, MR[n])
            got = [mrs[rnd, i, :, n * 256 : n * 256 + 256] for i in range(8)]
            mraw[rnd, c, mine_hz, :, n * 256 : n * 256 + 256] = ((got[0] + got[1]) + (got[2] + got[3])) + (
                (got[4] + got[5]) + (got[6] + got[7])
            )
            for z2, h2 in zh_peers:
                piece = mraw.at[rnd, c, mine_hz, :, span]
                send(piece, piece, rnd, MG[n], dev(z2, x, h2, y, c))

        @pl.when(rnd > 0)
        def _():
            factor_blocks(14, 16)

        for n in range(2):
            landed(mraw.at[rnd, c, pl.ds(0, 7), :, pl.ds(n * 256, 256)], rnd, MG[n])
        send(mraw.at[rnd, c], mraw.at[rnd, c], rnd, MC, partner)

        def all_columns():
            landed(mraw.at[rnd, o], rnd, MC)
            for cc in range(2):
                for i in range(8):
                    r0 = (i // 2) * 32 + cc * 16 + (i % 2) * 8
                    mfull[r0 : r0 + 8, :] = mraw[rnd, cc, i]

        @pl.when(rnd == 0)
        def _():
            for i in range(8):
                xl[i * 8 : i * 8 + 8, :] = mraw[rnd, c, i]

        @pl.when(rnd > 0)
        def _():
            all_columns()
            mt[rnd] = jnp.dot(work[:, RANK:], mfull[...], precision=HIGHEST, preferred_element_type=F32)
            for i in range(4):
                xl[i * 16 : i * 16 + 16, :] = mt[rnd, pl.ds(pl.multiple_of(i * 32 + c * 16, 16), 16), :]

        part = folded(lax.dot_general(stacked(xl[...]), a[...], NT, preferred_element_type=F32))
        for i in range(4):
            for m in range(4):
                xs[rnd, i * 4 + m] = part[i * 16 : i * 16 + 16, m * 256 : m * 256 + 256]
        for x2, y2 in xy_peers:
            send(xs.at[rnd, x2 * 4 + y2], xrs.at[rnd, mine_xy], rnd, XR, dev(z, x2, h, y2, c))
        xrs[rnd, mine_xy] = xs[rnd, mine_xy]

        @pl.when(rnd == 0)
        def _():
            all_columns()
            mt[rnd] = mfull[...]

        gown[rnd] = lax.dot_general(
            mt[rnd, pl.ds(pl.multiple_of((c * 4 + z) * 16, 16), 16), :],
            mt[rnd], NT, precision=HIGHEST, preferred_element_type=F32,
        )
        for y2 in y_peers:
            send(gown.at[rnd], gys.at[rnd, y], rnd, GY, dev(z, x, h, y2, c))
        gys[rnd, y] = gown[rnd]
        landed(xrs.at[rnd, pl.ds(0, 15)], rnd, XR)
        total = xrs[rnd, 0]
        for i in range(1, 16):
            total = total + xrs[rnd, i]
        xt[rnd, mine_cy] = total
        for y2, c2 in yc_peers:
            piece = xt.at[rnd, mine_cy]
            send(piece, piece, rnd, XG, dev(z, x, h, y2, c2))
        landed(gys.at[rnd, pl.ds(0, 3)], rnd, GY)
        gsum[rnd] = (gys[rnd, 0] + gys[rnd, 1]) + (gys[rnd, 2] + gys[rnd, 3])
        for x2 in x_peers:
            send(gsum.at[rnd], gxs.at[rnd, x], rnd, GX, dev(z, x2, h, y, c))
        gxs[rnd, x] = gsum[rnd]

        landed(xt.at[rnd, pl.ds(0, 7)], rnd, XG)

        rows = [jnp.concatenate([xt[rnd, i * 4 + m] for m in range(4)], axis=1) for i in range(2)]
        lhs = stacked(jnp.concatenate(rows, axis=0))
        for n, (lo, size) in enumerate(PARTS):
            part = folded(jnp.dot(lhs, b[:, lo : lo + size], preferred_element_type=F32))
            ps[rnd, :, :, lo : lo + size] = part.reshape(4, 8, size)
            for z2 in z_peers:
                span = pl.ds(lo, size)
                send(ps.at[rnd, z2, :, span], prs.at[rnd, z, :, span], rnd, PR[n], dev(z2, x, h, y, c))
        prs[rnd, z] = ps[rnd, z]

        @pl.when(rnd == ROUNDS - 1)
        def _():
            for y2 in y_peers:
                send(
                    mt.at[rnd, :, pl.ds(pl.multiple_of(c * 256, 256), 256)],
                    mg.at[y, c],
                    0, PHASES,
                    dev(z, x, h, y2, c),
                )

        landed(gxs.at[rnd, pl.ds(0, 3)], rnd, GX)
        gfull[rnd, c, z] = (gxs[rnd, 0] + gxs[rnd, 1]) + (gxs[rnd, 2] + gxs[rnd, 3])
        for z2 in z_peers:
            piece = gfull.at[rnd, c, z]
            send(piece, piece, rnd, GZ, dev(z2, x, h, y, c))
        for n, (lo, size) in enumerate(PARTS):
            span = pl.ds(lo, size)
            landed(prs.at[rnd, pl.ds(0, 3), :, span], rnd, PR[n])
            got = [prs[rnd, i, :, lo : lo + size] for i in range(4)]
            pt[rnd + 1, z, :, lo : lo + size] = (got[0] + got[1]) + (got[2] + got[3])
            for z2 in z_peers:
                piece = pt.at[rnd + 1, z, :, span]
                send(piece, piece, rnd, PG[n] + z, dev(z2, x, h, y, c))
        landed(gfull.at[rnd, c, pl.ds(0, 3)], rnd, GZ)
        send(gfull.at[rnd, c], gfull.at[rnd, c], rnd, GC, partner)

        @pl.when(rnd < ROUNDS - 1)
        def _():
            def ready(n):
                for z2 in z_peers:
                    gathered_p(rnd, n, z2)

            tokens_part(rnd + 1, ready)

        return carry

    lax.fori_loop(0, ROUNDS, one_round, 0)

    last = ROUNDS - 1
    for x2 in x_peers:
        send(pt.at[ROUNDS, z], cf.at[x, z], 2, PHASES, dev(z, x2, h, y, c))
    landed(gfull.at[last, o], last, GC)
    factor_start(last)
    factor_blocks(0, 4)
    for k in (1, 3, 2):
        z2 = (z + k) % 4
        for n in range(2):
            gathered_p(last, n, z2)
        for x2 in x_peers:
            send(pt.at[ROUNDS, z2], cf.at[x, z2], 2, PHASES, dev(z, x2, h, y, c))
    landed(mg.at[pl.ds(0, 3), 0], 0, PHASES)
    for y2 in y_peers:
        piece = mg.at[y2, c]
        send(piece, piece, 1, PHASES, partner)
    for cc in range(2):
        mg[y, cc] = mt[last, :, cc * 256 : cc * 256 + 256]
    cf[x] = pt[ROUNDS]
    factor_blocks(4, 16)
    final = work[:, RANK:]
    scaled = final * math.sqrt(D)
    landed(mg.at[pl.ds(0, 3), 0], 1, PHASES)
    for i in range(4):
        for cc in range(2):
            r0 = i * FEAT + cc * 256
            basis_ref[r0 : r0 + 256, :] = lax.dot_general(
                mg[i, cc].T, scaled, NT, precision=HIGHEST, preferred_element_type=F32
            )
    landed(cf.at[pl.ds(0, 3)], 2, PHASES)
    coef_ref[...] = jnp.dot(final, cf[...].reshape(RANK, HID), precision=HIGHEST, preferred_element_type=F32)

    def drain(rnd, carry):
        left(yrs.at[rnd, pl.ds(0, 7)], rnd, YR)
        left(yt.at[rnd, pl.ds(0, 15)], rnd, YG)
        for n in range(2):
            span = pl.ds(n * 256, 256)
            left(mrs.at[rnd, pl.ds(0, 7), :, span], rnd, MR[n])
            left(mraw.at[rnd, 0, pl.ds(0, 7), :, span], rnd, MG[n])
        left(mraw.at[rnd, 0], rnd, MC)
        left(xrs.at[rnd, pl.ds(0, 15)], rnd, XR)
        left(xt.at[rnd, pl.ds(0, 7)], rnd, XG)
        for n, (lo, size) in enumerate(PARTS):
            span = pl.ds(lo, size)
            left(prs.at[rnd, pl.ds(0, 3), :, span], rnd, PR[n])
            left(pt.at[rnd, pl.ds(0, 3), :, span], rnd, PG[n] + z)
        left(gys.at[rnd, pl.ds(0, 3)], rnd, GY)
        left(gxs.at[rnd, pl.ds(0, 3)], rnd, GX)
        left(gfull.at[rnd, 0, pl.ds(0, 3)], rnd, GZ)
        left(gfull.at[rnd, 0], rnd, GC)
        return carry

    lax.fori_loop(0, ROUNDS, drain, 0)
    left(mg.at[pl.ds(0, 3), 0], 0, PHASES)
    left(mg.at[pl.ds(0, 3), 0], 1, PHASES)
    left(cf.at[pl.ds(0, 3)], 2, PHASES)


def body(activations, grad_out, sketch):
    anywhere = pl.BlockSpec(memory_space=pl.ANY)
    inside = pl.BlockSpec(memory_space=pltpu.VMEM)
    vm = pltpu.VMEM
    n = ROUNDS
    return pl.pallas_call(
        kernel,
        name="range_finder",
        out_shape=(
            jax.ShapeDtypeStruct((2048, RANK), F32),
            jax.ShapeDtypeStruct((RANK, HID), F32),
        ),
        in_specs=[anywhere] * 3,
        out_specs=(inside, inside),
        scratch_shapes=[
            vm((TOK, FEAT), BF16),
            vm((TOK, HID), BF16),
            vm((HID, RANK), F32),
            vm((RANK, HID), F32),
            vm((n + 1, 4, 8, HID), F32),
            vm((n, 8, 16, 256), F32),
            vm((n, 8, 16, 256), F32),
            vm((n, 16, 16, 256), F32),
            vm((n, 8, 8, FEAT), F32),
            vm((n, 8, 8, FEAT), F32),
            vm((n, 2, 8, 8, FEAT), F32),
            vm((RANK, FEAT), F32),
            vm((n, RANK, FEAT), F32),
            vm((64, FEAT), F32),
            vm((n, 16, 16, 256), F32),
            vm((n, 16, 16, 256), F32),
            vm((n, 8, 16, 256), F32),
            vm((n, 4, 8, HID), F32),
            vm((n, 4, 8, HID), F32),
            vm((n, 16, RANK), F32),
            vm((n, 4, 16, RANK), F32),
            vm((n, 16, RANK), F32),
            vm((n, 4, 16, RANK), F32),
            vm((n, 2, 4, 16, RANK), F32),
            vm((RANK, 2 * RANK), F32),
            vm((4, 4, 8, HID), F32),
            vm((4, 2, RANK, 256), F32),
            pltpu.SemaphoreType.DMA((3,)),
            pltpu.SemaphoreType.DMA((n, PHASES + 1)),
            pltpu.SemaphoreType.DMA((n, PHASES + 1)),
        ],
        compiler_params=pltpu.CompilerParams(
            collective_id=0, has_side_effects=True, vmem_limit_bytes=50 * 2**20
        ),
    )(activations, grad_out, sketch)


def solution(mesh):
    in_specs = (P("dp", "row"), P("dp", "col"), P("col", None))
    out_specs = (P("row", None), P(None, "col"))
    return jax.shard_map(body, mesh=mesh, in_specs=in_specs, out_specs=out_specs, check_vma=False)
```

```python
import functools
import math

import jax
import jax.numpy as jnp
from jax import lax
from jax.experimental import pallas as pl
from jax.experimental.pallas import tpu as pltpu
from jax.sharding import PartitionSpec as P

MESH = pl.DeviceIdType.MESH
F32 = jnp.float32
BF16 = jnp.bfloat16
HIGHEST = lax.Precision.HIGHEST
D = 8192
RANK = 128
ROUNDS = 3
TOK = 1024
HID = 1664
FEAT = 512
NT = (((1,), (1,)), ((), ()))
TN = (((0,), (0,)), ((), ()))
PARTS = ((0, 896), (896, 768))
YR, YG, MRA, MRB, MGA, MGB, MC, XR, XG, PRA, PRB, GY, GX, GZ, GC = range(15)
MR, MG, PR = (MRA, MRB), (MGA, MGB), (PRA, PRB)
PG = (15, 19)
PHASES = 23
XY = (
    (2, 2), (2, 1), (2, 3), (1, 2), (3, 2), (1, 1), (1, 3), (3, 1), (3, 3),
    (2, 0), (0, 2), (1, 0), (3, 0), (0, 1), (0, 3),
)
ZH = ((2, 1), (1, 1), (3, 1), (0, 1), (2, 0), (1, 0), (3, 0))


def stacked(mat):
    high = mat.astype(BF16)
    rest = mat - high.astype(F32)
    mid = rest.astype(BF16)
    low = (rest - mid.astype(F32)).astype(BF16)
    return jnp.concatenate([high, mid, low], axis=0)


def outer(left, right):
    def three(mat):
        high = mat.astype(BF16).astype(F32)
        mid = (mat - high).astype(BF16).astype(F32)
        return high, mid, (mat - high - mid).astype(BF16).astype(F32)

    lh, lm, ll = three(left)
    rh, rm, rl = three(right)
    return lax.dot_general(
        jnp.concatenate([lh, lh, lm, lh, ll, lm], axis=0).astype(BF16),
        jnp.concatenate([rh, rm, rh, rl, rh, rm], axis=0).astype(BF16),
        TN, preferred_element_type=F32,
    )


def folded(wide):
    rows = wide.shape[0] // 3
    return wide[:rows] + (wide[rows : 2 * rows] + wide[2 * rows :])


def kernel(
    a_hbm, b_hbm, s_hbm, basis_ref, coef_ref,
    a, b, s, st, pt, yacc, ysend, yrs, yt, ms, mrs, mraw, mfull, mt, xl, xs, xrs, xt,
    ps, prs, gown, gys, gsum, gxs, gfull, work, cf, mg,
    load_sem, send_sem, recv_sem,
):
    z, x, j = lax.axis_index("dp"), lax.axis_index("row"), lax.axis_index("col")
    c = j % 2
    y = (j // 2) % 4
    h = j // 8
    o = 1 - c
    mine_xy = x * 4 + y
    mine_hz = h * 4 + z
    mine_cy = c * 4 + y

    def dev(z_, x_, h_, y_, c_):
        return (z_, x_, (h_ * 4 + y_) * 2 + c_)

    partner = dev(z, x, h, y, o)
    xy_peers = [((x + dx) % 4, (y + dy) % 4) for dx, dy in XY]
    zh_peers = [((z + dz) % 4, (h + dh) % 2) for dz, dh in ZH]
    z_peers = [(z + k) % 4 for k in (2, 1, 3)]
    y_peers = [(y + k) % 4 for k in (2, 1, 3)]
    yc_peers = [((y + k) % 4, c2) for k in (2, 1, 3) for c2 in (c, o)] + [(y, o)]
    x_peers = [(x + k) % 4 for k in (2, 1, 3)]

    barrier = pltpu.get_barrier_semaphore()

    def greet(device):
        pl.semaphore_signal(barrier, inc=1, device_id=device, device_id_type=MESH)

    loads = [
        pltpu.make_async_copy(s_hbm, s, load_sem.at[0]),
        pltpu.make_async_copy(b_hbm, b, load_sem.at[1]),
        pltpu.make_async_copy(
            a_hbm.at[:, pl.ds(pl.multiple_of(y * FEAT, FEAT), FEAT)], a, load_sem.at[2]
        ),
    ]
    for load in loads:
        load.start()

    for (x2, y2), (dx, _) in zip(xy_peers, XY):
        if dx:
            greet(dev(z, x2, h, y2, c))
    for z2, h2 in zh_peers:
        greet(dev(z2, x, h2, y, c))
    for y2, c2 in yc_peers:
        greet(dev(z, x, h, y2, c2))

    def send(src, dst, rnd, phase, device):
        pltpu.make_async_remote_copy(
            src_ref=src,
            dst_ref=dst,
            send_sem=send_sem.at[rnd, phase],
            recv_sem=recv_sem.at[rnd, phase],
            device_id=device,
            device_id_type=MESH,
        ).start()

    def landed(like, rnd, phase):
        pltpu.make_async_copy(like, like, recv_sem.at[rnd, phase]).wait()

    def left(like, rnd, phase):
        pltpu.make_async_copy(like, like, send_sem.at[rnd, phase]).wait()

    row_iota = lax.broadcasted_iota(jnp.int32, (RANK, RANK), 0)
    col_iota = lax.broadcasted_iota(jnp.int32, (RANK, RANK), 1)
    eye = jnp.where(row_iota == col_iota, 1.0, 0.0).astype(F32)

    def factor_start(rnd):
        work[:, :RANK] = gfull[rnd].reshape(RANK, RANK)
        work[:, RANK:] = eye

    sub = lax.broadcasted_iota(jnp.int32, (8, RANK), 0)
    lane = lax.broadcasted_iota(jnp.int32, (8, RANK), 1)

    def spread(row):
        return jnp.broadcast_to(row, (8, RANK))

    def factor_block(blk, carry):
        r0 = pl.multiple_of(blk * 8, 8)
        gp = work[pl.ds(r0, 8), :RANK]
        ep = work[pl.ds(r0, 8), RANK:]
        diag = pltpu.roll(gp, RANK - r0, 1)
        cols = [jnp.broadcast_to(diag[:, i : i + 1], (8, RANK)) for i in range(8)]
        inv = [jnp.where(sub == i, 1.0, 0.0).astype(F32) for i in range(8)]
        pivots = jnp.ones((8, RANK), F32)
        for i in range(8):
            pivot = spread(cols[i][i : i + 1])
            pivots = jnp.where(sub == i, pivot, pivots)
            if i == 7:
                break
            scale = jnp.where(sub > i, cols[i] * (1.0 / pivot), 0.0)
            for m in range(i + 1, 8):
                cols[m] = cols[m] - scale * spread(cols[m][i : i + 1])
            for m in range(i + 1):
                inv[m] = inv[m] - scale * spread(inv[m][i : i + 1])
        root = lax.rsqrt(pivots)
        root = root * (1.5 - 0.5 * pivots * root * root)
        ug = jnp.zeros((8, RANK), F32)
        ue = jnp.zeros((8, RANK), F32)
        for m in range(8):
            weight = inv[m] * root
            ug = ug + weight * spread(gp[m : m + 1])
            ue = ue + weight * spread(ep[m : m + 1])
        work[pl.ds(r0, 8), RANK:] = ue
        rest = jnp.where(lane >= r0 + 8, ug, 0.0)
        work[...] -= outer(rest, jnp.concatenate([ug, ue], axis=1))
        return carry

    def factor_blocks(lo, hi):
        lax.fori_loop(lo, hi, factor_block, 0)

    def tokens_part(rnd, ready):
        sides = []
        for n, (lo, size) in enumerate(PARTS):
            ready(n)
            sides.append(stacked(pt[rnd, :, :, lo : lo + size].reshape(32, size)))
            if n == 0:
                part = folded(lax.dot_general(sides[0], b[:, lo : lo + size], NT, preferred_element_type=F32))
                for m in range(4):
                    yacc[m] = part[:, m * 256 : m * 256 + 256]
        lo, size = PARTS[1]
        for k in (2, 1, 3, 0):
            y2 = (y + k) % 4
            rows = b[pl.ds(pl.multiple_of(y2 * 256, 256), 256), lo : lo + size]
            quarter = yacc[y2] + folded(lax.dot_general(sides[1], rows, NT, preferred_element_type=F32))
            ysend[rnd, y2] = quarter[:16]
            ysend[rnd, 4 + y2] = quarter[16:]
            for c2 in (c, o) if k else (o,):
                send(ysend.at[rnd, c2 * 4 + y2], yrs.at[rnd, mine_cy], rnd, YR, dev(z, x, h, y2, c2))

    loads[0].wait()
    st[...] = s[...].T
    pt[0] = st[pl.ds(pl.multiple_of(x * 32, 32), 32), :].reshape(4, 8, HID)
    loads[1].wait()

    def begin(n):
        if n == 1:
            pl.semaphore_wait(barrier, 26)

    tokens_part(0, begin)
    loads[2].wait()

    def to_row(z2, n):
        span = pl.ds(*PARTS[n])
        for x2 in x_peers:
            send(pt.at[ROUNDS, z2, :, span], cf.at[x, z2, :, span], 2, PHASES, dev(z, x2, h, y, c))

    def gathered_p(rnd, n, z2):
        lo, size = PARTS[n]
        landed(pt.at[rnd + 1, z2, :, pl.ds(lo, size)], rnd, PG[n] + z2)

    def one_round(rnd, carry):
        yrs[rnd, mine_cy] = ysend[rnd, mine_cy]

        @pl.when(rnd > 0)
        def _():
            landed(gfull.at[rnd - 1, o], rnd - 1, GC)
            factor_start(rnd - 1)
            factor_blocks(0, 4)

        landed(yrs.at[rnd, pl.ds(0, 7)], rnd, YR)
        got = [yrs[rnd, i] for i in range(8)]
        yt[rnd, mine_xy] = ((got[0] + got[1]) + (got[2] + got[3])) + ((got[4] + got[5]) + (got[6] + got[7]))
        for x2, y2 in xy_peers:
            piece = yt.at[rnd, mine_xy]
            send(piece, piece, rnd, YG, dev(z, x2, h, y2, c))

        @pl.when(rnd > 0)
        def _():
            factor_blocks(4, 9)

        landed(yt.at[rnd, pl.ds(0, 15)], rnd, YG)

        rows = [jnp.concatenate([yt[rnd, i * 4 + m] for m in range(4)], axis=1) for i in range(4)]
        lhs = stacked(jnp.concatenate(rows, axis=0))
        for n in range(2):
            span = pl.ds(n * 256, 256)
            part = folded(jnp.dot(lhs, a[:, n * 256 : n * 256 + 256], preferred_element_type=F32))
            for i in range(8):
                ms[rnd, i, :, n * 256 : n * 256 + 256] = part[i * 8 : i * 8 + 8]
            for z2, h2 in zh_peers:
                send(
                    ms.at[rnd, h2 * 4 + z2, :, span], mrs.at[rnd, mine_hz, :, span], rnd, MR[n], dev(z2, x, h2, y, c)
                )
        mrs[rnd, mine_hz] = ms[rnd, mine_hz]

        @pl.when(rnd > 0)
        def _():
            factor_blocks(9, 14)

        for n in range(2):
            span = pl.ds(n * 256, 256)
            landed(mrs.at[rnd, pl.ds(0, 7), :, span], rnd, MR[n])
            got = [mrs[rnd, i, :, n * 256 : n * 256 + 256] for i in range(8)]
            mraw[rnd, c, mine_hz, :, n * 256 : n * 256 + 256] = ((got[0] + got[1]) + (got[2] + got[3])) + (
                (got[4] + got[5]) + (got[6] + got[7])
            )
            for z2, h2 in zh_peers:
                piece = mraw.at[rnd, c, mine_hz, :, span]
                send(piece, piece, rnd, MG[n], dev(z2, x, h2, y, c))

        @pl.when(rnd > 0)
        def _():
            factor_blocks(14, 16)

        for n in range(2):
            landed(mraw.at[rnd, c, pl.ds(0, 7), :, pl.ds(n * 256, 256)], rnd, MG[n])
        send(mraw.at[rnd, c], mraw.at[rnd, c], rnd, MC, partner)

        def all_columns():
            landed(mraw.at[rnd, o], rnd, MC)
            for cc in range(2):
                for i in range(8):
                    r0 = (i // 2) * 32 + cc * 16 + (i % 2) * 8
                    mfull[r0 : r0 + 8, :] = mraw[rnd, cc, i]

        @pl.when(rnd == 0)
        def _():
            for i in range(8):
                xl[i * 8 : i * 8 + 8, :] = mraw[rnd, c, i]

        @pl.when(rnd > 0)
        def _():
            all_columns()
            mt[rnd] = jnp.dot(work[:, RANK:], mfull[...], precision=HIGHEST, preferred_element_type=F32)
            for i in range(4):
                xl[i * 16 : i * 16 + 16, :] = mt[rnd, pl.ds(pl.multiple_of(i * 32 + c * 16, 16), 16), :]

        lhs = stacked(xl[...])
        for k in (2, 1, 3, 0):
            y2 = (y + k) % 4
            rows = a[pl.ds(pl.multiple_of(y2 * 256, 256), 256), :]
            part = folded(lax.dot_general(lhs, rows, NT, preferred_element_type=F32))
            for i in range(4):
                xs[rnd, i * 4 + y2] = part[i * 16 : i * 16 + 16]
            for x2 in x_peers + ([x] if k else []):
                send(xs.at[rnd, x2 * 4 + y2], xrs.at[rnd, mine_xy], rnd, XR, dev(z, x2, h, y2, c))
        xrs[rnd, mine_xy] = xs[rnd, mine_xy]

        @pl.when(rnd == 0)
        def _():
            all_columns()
            mt[rnd] = mfull[...]

        gown[rnd] = lax.dot_general(
            mt[rnd, pl.ds(pl.multiple_of((c * 4 + z) * 16, 16), 16), :],
            mt[rnd], NT, precision=HIGHEST, preferred_element_type=F32,
        )
        for y2 in y_peers:
            send(gown.at[rnd], gys.at[rnd, y], rnd, GY, dev(z, x, h, y2, c))
        gys[rnd, y] = gown[rnd]
        landed(xrs.at[rnd, pl.ds(0, 15)], rnd, XR)
        total = xrs[rnd, 0]
        for i in range(1, 16):
            total = total + xrs[rnd, i]
        xt[rnd, mine_cy] = total
        for y2, c2 in yc_peers:
            piece = xt.at[rnd, mine_cy]
            send(piece, piece, rnd, XG, dev(z, x, h, y2, c2))
        landed(gys.at[rnd, pl.ds(0, 3)], rnd, GY)
        gsum[rnd] = (gys[rnd, 0] + gys[rnd, 1]) + (gys[rnd, 2] + gys[rnd, 3])
        for x2 in x_peers:
            send(gsum.at[rnd], gxs.at[rnd, x], rnd, GX, dev(z, x2, h, y, c))
        gxs[rnd, x] = gsum[rnd]

        landed(xt.at[rnd, pl.ds(0, 7)], rnd, XG)

        rows = [jnp.concatenate([xt[rnd, i * 4 + m] for m in range(4)], axis=1) for i in range(2)]
        lhs = stacked(jnp.concatenate(rows, axis=0))
        for n, (lo, size) in enumerate(PARTS):
            part = folded(jnp.dot(lhs, b[:, lo : lo + size], preferred_element_type=F32))
            ps[rnd, :, :, lo : lo + size] = part.reshape(4, 8, size)
            for z2 in z_peers:
                span = pl.ds(lo, size)
                send(ps.at[rnd, z2, :, span], prs.at[rnd, z, :, span], rnd, PR[n], dev(z2, x, h, y, c))
            if n == 0:
                landed(gxs.at[rnd, pl.ds(0, 3)], rnd, GX)
                gfull[rnd, c, z] = (gxs[rnd, 0] + gxs[rnd, 1]) + (gxs[rnd, 2] + gxs[rnd, 3])
                for z2 in z_peers:
                    piece = gfull.at[rnd, c, z]
                    send(piece, piece, rnd, GZ, dev(z2, x, h, y, c))
        prs[rnd, z] = ps[rnd, z]

        @pl.when(rnd == ROUNDS - 1)
        def _():
            for y2 in y_peers:
                send(
                    mt.at[rnd, :, pl.ds(pl.multiple_of(c * 256, 256), 256)],
                    mg.at[y, c],
                    0, PHASES,
                    dev(z, x, h, y2, c),
                )

        for n, (lo, size) in enumerate(PARTS):
            span = pl.ds(lo, size)
            landed(prs.at[rnd, pl.ds(0, 3), :, span], rnd, PR[n])
            got = [prs[rnd, i, :, lo : lo + size] for i in range(4)]
            pt[rnd + 1, z, :, lo : lo + size] = (got[0] + got[1]) + (got[2] + got[3])
            for z2 in z_peers:
                piece = pt.at[rnd + 1, z, :, span]
                send(piece, piece, rnd, PG[n] + z, dev(z2, x, h, y, c))

            @pl.when(rnd == ROUNDS - 1)
            def _():
                to_row(z, n)

        landed(gfull.at[rnd, c, pl.ds(0, 3)], rnd, GZ)
        send(gfull.at[rnd, c], gfull.at[rnd, c], rnd, GC, partner)

        @pl.when(rnd < ROUNDS - 1)
        def _():
            def ready(n):
                for z2 in z_peers:
                    gathered_p(rnd, n, z2)

            tokens_part(rnd + 1, ready)

        return carry

    lax.fori_loop(0, ROUNDS, one_round, 0)

    last = ROUNDS - 1
    landed(gfull.at[last, o], last, GC)
    factor_start(last)
    factor_blocks(0, 2)
    for n in range(2):
        for k in (1, 3, 2):
            z2 = (z + k) % 4
            gathered_p(last, n, z2)
            to_row(z2, n)
        factor_blocks(2 + n * 2, 4 + n * 2)
    landed(mg.at[pl.ds(0, 3), 0], 0, PHASES)
    for y2 in y_peers:
        piece = mg.at[y2, c]
        send(piece, piece, 1, PHASES, partner)
    for cc in range(2):
        mg[y, cc] = mt[last, :, cc * 256 : cc * 256 + 256]
    cf[x] = pt[ROUNDS]
    factor_blocks(6, 16)
    final = work[:, RANK:]
    scaled = final * math.sqrt(D)
    landed(mg.at[pl.ds(0, 3), 0], 1, PHASES)
    for i in range(4):
        for cc in range(2):
            r0 = i * FEAT + cc * 256
            basis_ref[r0 : r0 + 256, :] = lax.dot_general(
                mg[i, cc].T, scaled, NT, precision=HIGHEST, preferred_element_type=F32
            )
    landed(cf.at[pl.ds(0, 3)], 2, PHASES)
    coef_ref[...] = jnp.dot(final, cf[...].reshape(RANK, HID), precision=HIGHEST, preferred_element_type=F32)

    def drain(rnd, carry):
        left(yrs.at[rnd, pl.ds(0, 7)], rnd, YR)
        left(yt.at[rnd, pl.ds(0, 15)], rnd, YG)
        for n in range(2):
            span = pl.ds(n * 256, 256)
            left(mrs.at[rnd, pl.ds(0, 7), :, span], rnd, MR[n])
            left(mraw.at[rnd, 0, pl.ds(0, 7), :, span], rnd, MG[n])
        left(mraw.at[rnd, 0], rnd, MC)
        left(xrs.at[rnd, pl.ds(0, 15)], rnd, XR)
        left(xt.at[rnd, pl.ds(0, 7)], rnd, XG)
        for n, (lo, size) in enumerate(PARTS):
            span = pl.ds(lo, size)
            left(prs.at[rnd, pl.ds(0, 3), :, span], rnd, PR[n])
            left(pt.at[rnd, pl.ds(0, 3), :, span], rnd, PG[n] + z)
        left(gys.at[rnd, pl.ds(0, 3)], rnd, GY)
        left(gxs.at[rnd, pl.ds(0, 3)], rnd, GX)
        left(gfull.at[rnd, 0, pl.ds(0, 3)], rnd, GZ)
        left(gfull.at[rnd, 0], rnd, GC)
        return carry

    lax.fori_loop(0, ROUNDS, drain, 0)
    left(mg.at[pl.ds(0, 3), 0], 0, PHASES)
    left(mg.at[pl.ds(0, 3), 0], 1, PHASES)
    left(cf.at[pl.ds(0, 3)], 2, PHASES)


def body(activations, grad_out, sketch):
    anywhere = pl.BlockSpec(memory_space=pl.ANY)
    inside = pl.BlockSpec(memory_space=pltpu.VMEM)
    vm = pltpu.VMEM
    n = ROUNDS
    return pl.pallas_call(
        kernel,
        name="range_finder",
        out_shape=(
            jax.ShapeDtypeStruct((2048, RANK), F32),
            jax.ShapeDtypeStruct((RANK, HID), F32),
        ),
        in_specs=[anywhere] * 3,
        out_specs=(inside, inside),
        scratch_shapes=[
            vm((TOK, FEAT), BF16),
            vm((TOK, HID), BF16),
            vm((HID, RANK), F32),
            vm((RANK, HID), F32),
            vm((n + 1, 4, 8, HID), F32),
            vm((4, 32, 256), F32),
            vm((n, 8, 16, 256), F32),
            vm((n, 8, 16, 256), F32),
            vm((n, 16, 16, 256), F32),
            vm((n, 8, 8, FEAT), F32),
            vm((n, 8, 8, FEAT), F32),
            vm((n, 2, 8, 8, FEAT), F32),
            vm((RANK, FEAT), F32),
            vm((n, RANK, FEAT), F32),
            vm((64, FEAT), F32),
            vm((n, 16, 16, 256), F32),
            vm((n, 16, 16, 256), F32),
            vm((n, 8, 16, 256), F32),
            vm((n, 4, 8, HID), F32),
            vm((n, 4, 8, HID), F32),
            vm((n, 16, RANK), F32),
            vm((n, 4, 16, RANK), F32),
            vm((n, 16, RANK), F32),
            vm((n, 4, 16, RANK), F32),
            vm((n, 2, 4, 16, RANK), F32),
            vm((RANK, 2 * RANK), F32),
            vm((4, 4, 8, HID), F32),
            vm((4, 2, RANK, 256), F32),
            pltpu.SemaphoreType.DMA((3,)),
            pltpu.SemaphoreType.DMA((n, PHASES + 1)),
            pltpu.SemaphoreType.DMA((n, PHASES + 1)),
        ],
        compiler_params=pltpu.CompilerParams(
            collective_id=0, has_side_effects=True, vmem_limit_bytes=50 * 2**20
        ),
    )(activations, grad_out, sketch)


def solution(mesh):
    in_specs = (P("dp", "row"), P("dp", "col"), P("col", None))
    out_specs = (P("row", None), P(None, "col"))
    return jax.shard_map(body, mesh=mesh, in_specs=in_specs, out_specs=out_specs, check_vma=False)
```

```python
import functools
import math

import jax
import jax.numpy as jnp
from jax import lax
from jax.experimental import pallas as pl
from jax.experimental.pallas import tpu as pltpu
from jax.sharding import PartitionSpec as P

MESH = pl.DeviceIdType.MESH
F32 = jnp.float32
BF16 = jnp.bfloat16
HIGHEST = lax.Precision.HIGHEST
D = 8192
RANK = 128
ROUNDS = 3
TOK = 1024
HID = 1664
FEAT = 512
NT = (((1,), (1,)), ((), ()))
TN = (((0,), (0,)), ((), ()))
PARTS = ((0, 640), (640, 512), (1152, 512))
HALVES = ((0, 256), (256, 256))
YR, YG, MC, XR, XG, GY, GX, GZ, GC = range(9)
MR, MG, PR = range(9, 12), range(12, 15), range(15, 18)
PG = range(18, 30, 4)
PHASES = 30
XY = (
    (2, 2), (2, 1), (2, 3), (1, 2), (3, 2), (1, 1), (1, 3), (3, 1), (3, 3),
    (2, 0), (0, 2), (1, 0), (3, 0), (0, 1), (0, 3),
)
ZH = ((2, 1), (1, 1), (3, 1), (0, 1), (2, 0), (1, 0), (3, 0))


def stacked(mat):
    high = mat.astype(BF16)
    rest = mat - high.astype(F32)
    mid = rest.astype(BF16)
    low = (rest - mid.astype(F32)).astype(BF16)
    return jnp.concatenate([high, mid, low], axis=0)


def outer(left, right):
    def three(mat):
        high = mat.astype(BF16).astype(F32)
        mid = (mat - high).astype(BF16).astype(F32)
        return high, mid, (mat - high - mid).astype(BF16).astype(F32)

    lh, lm, ll = three(left)
    rh, rm, rl = three(right)
    return lax.dot_general(
        jnp.concatenate([lh, lh, lm, lh, ll, lm], axis=0).astype(BF16),
        jnp.concatenate([rh, rm, rh, rl, rh, rm], axis=0).astype(BF16),
        TN, preferred_element_type=F32,
    )


def folded(wide):
    rows = wide.shape[0] // 3
    return wide[:rows] + (wide[rows : 2 * rows] + wide[2 * rows :])


def kernel(
    a_hbm, b_hbm, s_hbm, basis_ref, coef_ref,
    a, b, s, st, pt, yacc, ysend, yrs, yt, ms, mrs, mraw, mfull, mt, xl, xs, xrs, xt,
    ps, prs, gown, gys, gsum, gxs, gfull, work, cf, mg,
    load_sem, send_sem, recv_sem,
):
    z, x, j = lax.axis_index("dp"), lax.axis_index("row"), lax.axis_index("col")
    c = j % 2
    y = (j // 2) % 4
    h = j // 8
    o = 1 - c
    mine_xy = x * 4 + y
    mine_hz = h * 4 + z
    mine_cy = c * 4 + y

    def dev(z_, x_, h_, y_, c_):
        return (z_, x_, (h_ * 4 + y_) * 2 + c_)

    partner = dev(z, x, h, y, o)
    xy_peers = [((x + dx) % 4, (y + dy) % 4) for dx, dy in XY]
    zh_peers = [((z + dz) % 4, (h + dh) % 2) for dz, dh in ZH]
    z_peers = [(z + k) % 4 for k in (2, 1, 3)]
    y_peers = [(y + k) % 4 for k in (2, 1, 3)]
    yc_peers = [((y + k) % 4, c2) for k in (2, 1, 3) for c2 in (c, o)] + [(y, o)]
    x_peers = [(x + k) % 4 for k in (2, 1, 3)]

    barrier = pltpu.get_barrier_semaphore()

    def greet(device):
        pl.semaphore_signal(barrier, inc=1, device_id=device, device_id_type=MESH)

    loads = [
        pltpu.make_async_copy(s_hbm, s, load_sem.at[0]),
    ]
    for n, (lo, size) in enumerate(PARTS):
        span = pl.ds(lo, size)
        loads.append(pltpu.make_async_copy(b_hbm.at[:, span], b.at[:, span], load_sem.at[1 + n]))
    loads.append(
        pltpu.make_async_copy(
            a_hbm.at[:, pl.ds(pl.multiple_of(y * FEAT, FEAT), FEAT)], a, load_sem.at[1 + len(PARTS)]
        )
    )
    for load in loads:
        load.start()

    for (x2, y2), (dx, _) in zip(xy_peers, XY):
        if dx:
            greet(dev(z, x2, h, y2, c))
    for z2, h2 in zh_peers:
        greet(dev(z2, x, h2, y, c))
    for y2, c2 in yc_peers:
        greet(dev(z, x, h, y2, c2))

    def send(src, dst, rnd, phase, device):
        pltpu.make_async_remote_copy(
            src_ref=src,
            dst_ref=dst,
            send_sem=send_sem.at[rnd, phase],
            recv_sem=recv_sem.at[rnd, phase],
            device_id=device,
            device_id_type=MESH,
        ).start()

    def landed(like, rnd, phase):
        pltpu.make_async_copy(like, like, recv_sem.at[rnd, phase]).wait()

    def left(like, rnd, phase):
        pltpu.make_async_copy(like, like, send_sem.at[rnd, phase]).wait()

    row_iota = lax.broadcasted_iota(jnp.int32, (RANK, RANK), 0)
    col_iota = lax.broadcasted_iota(jnp.int32, (RANK, RANK), 1)
    eye = jnp.where(row_iota == col_iota, 1.0, 0.0).astype(F32)

    def factor_start(rnd):
        work[:, :RANK] = gfull[rnd].reshape(RANK, RANK)
        work[:, RANK:] = eye

    sub = lax.broadcasted_iota(jnp.int32, (8, RANK), 0)
    lane = lax.broadcasted_iota(jnp.int32, (8, RANK), 1)

    def spread(row):
        return jnp.broadcast_to(row, (8, RANK))

    def factor_block(blk, carry):
        r0 = pl.multiple_of(blk * 8, 8)
        gp = work[pl.ds(r0, 8), :RANK]
        ep = work[pl.ds(r0, 8), RANK:]
        diag = pltpu.roll(gp, RANK - r0, 1)
        cols = [jnp.broadcast_to(diag[:, i : i + 1], (8, RANK)) for i in range(8)]
        inv = [jnp.where(sub == i, 1.0, 0.0).astype(F32) for i in range(8)]
        pivots = jnp.ones((8, RANK), F32)
        for i in range(8):
            pivot = spread(cols[i][i : i + 1])
            pivots = jnp.where(sub == i, pivot, pivots)
            if i == 7:
                break
            scale = jnp.where(sub > i, cols[i] * (1.0 / pivot), 0.0)
            for m in range(i + 1, 8):
                cols[m] = cols[m] - scale * spread(cols[m][i : i + 1])
            for m in range(i + 1):
                inv[m] = inv[m] - scale * spread(inv[m][i : i + 1])
        root = lax.rsqrt(pivots)
        root = root * (1.5 - 0.5 * pivots * root * root)
        ug = jnp.zeros((8, RANK), F32)
        ue = jnp.zeros((8, RANK), F32)
        for m in range(8):
            weight = inv[m] * root
            ug = ug + weight * spread(gp[m : m + 1])
            ue = ue + weight * spread(ep[m : m + 1])
        work[pl.ds(r0, 8), RANK:] = ue
        rest = jnp.where(lane >= r0 + 8, ug, 0.0)
        work[...] -= outer(rest, jnp.concatenate([ug, ue], axis=1))
        return carry

    def factor_blocks(lo, hi):
        lax.fori_loop(lo, hi, factor_block, 0)

    def tokens_part(rnd, ready):
        for n, (lo, size) in enumerate(PARTS):
            ready(n)
            lhs = stacked(pt[rnd, :, :, lo : lo + size].reshape(32, size))
            if n < len(PARTS) - 1:
                part = folded(lax.dot_general(lhs, b[:, lo : lo + size], NT, preferred_element_type=F32))
                for m in range(4):
                    quarter = part[:, m * 256 : m * 256 + 256]
                    yacc[m] = yacc[m] + quarter if n else quarter
        for k in (2, 1, 3, 0):
            y2 = (y + k) % 4
            rows = b[pl.ds(pl.multiple_of(y2 * 256, 256), 256), lo : lo + size]
            quarter = folded(lax.dot_general(lhs, rows, NT, preferred_element_type=F32))
            if len(PARTS) > 1:
                quarter = yacc[y2] + quarter
            ysend[rnd, y2] = quarter[:16]
            ysend[rnd, 4 + y2] = quarter[16:]
            for c2 in (c, o) if k else (o,):
                send(ysend.at[rnd, c2 * 4 + y2], yrs.at[rnd, mine_cy], rnd, YR, dev(z, x, h, y2, c2))

    loads[0].wait()
    st[...] = s[...].T
    pt[0] = st[pl.ds(pl.multiple_of(x * 32, 32), 32), :].reshape(4, 8, HID)

    def begin(n):
        loads[1 + n].wait()
        if n == len(PARTS) - 1:
            pl.semaphore_wait(barrier, 26)

    tokens_part(0, begin)
    loads[-1].wait()

    def to_row(z2, n):
        span = pl.ds(*PARTS[n])
        for x2 in x_peers:
            send(pt.at[ROUNDS, z2, :, span], cf.at[x, z2, :, span], 2, PHASES, dev(z, x2, h, y, c))

    def gathered_p(rnd, n, z2):
        lo, size = PARTS[n]
        landed(pt.at[rnd + 1, z2, :, pl.ds(lo, size)], rnd, PG[n] + z2)

    def one_round(rnd, carry):
        yrs[rnd, mine_cy] = ysend[rnd, mine_cy]

        @pl.when(rnd > 0)
        def _():
            landed(gfull.at[rnd - 1, o], rnd - 1, GC)
            factor_start(rnd - 1)
            factor_blocks(0, 4)

        landed(yrs.at[rnd, pl.ds(0, 7)], rnd, YR)
        got = [yrs[rnd, i] for i in range(8)]
        yt[rnd, mine_xy] = ((got[0] + got[1]) + (got[2] + got[3])) + ((got[4] + got[5]) + (got[6] + got[7]))
        for x2, y2 in xy_peers:
            piece = yt.at[rnd, mine_xy]
            send(piece, piece, rnd, YG, dev(z, x2, h, y2, c))

        @pl.when(rnd > 0)
        def _():
            factor_blocks(4, 9)

        landed(yt.at[rnd, pl.ds(0, 15)], rnd, YG)

        rows = [jnp.concatenate([yt[rnd, i * 4 + m] for m in range(4)], axis=1) for i in range(4)]
        lhs = stacked(jnp.concatenate(rows, axis=0))
        for n, (lo, size) in enumerate(HALVES):
            span = pl.ds(lo, size)
            part = folded(jnp.dot(lhs, a[:, lo : lo + size], preferred_element_type=F32))
            for i in range(8):
                ms[rnd, i, :, lo : lo + size] = part[i * 8 : i * 8 + 8]
            for z2, h2 in zh_peers:
                send(
                    ms.at[rnd, h2 * 4 + z2, :, span], mrs.at[rnd, mine_hz, :, span], rnd, MR[n], dev(z2, x, h2, y, c)
                )
        mrs[rnd, mine_hz] = ms[rnd, mine_hz]

        @pl.when(rnd > 0)
        def _():
            factor_blocks(9, 14)

        for n, (lo, size) in enumerate(HALVES):
            span = pl.ds(lo, size)
            landed(mrs.at[rnd, pl.ds(0, 7), :, span], rnd, MR[n])
            got = [mrs[rnd, i, :, lo : lo + size] for i in range(8)]
            mraw[rnd, c, mine_hz, :, lo : lo + size] = ((got[0] + got[1]) + (got[2] + got[3])) + (
                (got[4] + got[5]) + (got[6] + got[7])
            )
            for z2, h2 in zh_peers:
                piece = mraw.at[rnd, c, mine_hz, :, span]
                send(piece, piece, rnd, MG[n], dev(z2, x, h2, y, c))

        @pl.when(rnd > 0)
        def _():
            factor_blocks(14, 16)

        for n, (lo, size) in enumerate(HALVES):
            landed(mraw.at[rnd, c, pl.ds(0, 7), :, pl.ds(lo, size)], rnd, MG[n])
        send(mraw.at[rnd, c], mraw.at[rnd, c], rnd, MC, partner)

        def all_columns():
            landed(mraw.at[rnd, o], rnd, MC)
            for cc in range(2):
                for i in range(8):
                    r0 = (i // 2) * 32 + cc * 16 + (i % 2) * 8
                    mfull[r0 : r0 + 8, :] = mraw[rnd, cc, i]

        @pl.when(rnd == 0)
        def _():
            for i in range(8):
                xl[i * 8 : i * 8 + 8, :] = mraw[rnd, c, i]

        @pl.when(rnd > 0)
        def _():
            all_columns()
            mt[rnd] = jnp.dot(work[:, RANK:], mfull[...], precision=HIGHEST, preferred_element_type=F32)
            for i in range(4):
                xl[i * 16 : i * 16 + 16, :] = mt[rnd, pl.ds(pl.multiple_of(i * 32 + c * 16, 16), 16), :]

        lhs = stacked(xl[...])
        for k in (2, 1, 3, 0):
            y2 = (y + k) % 4
            rows = a[pl.ds(pl.multiple_of(y2 * 256, 256), 256), :]
            part = folded(lax.dot_general(lhs, rows, NT, preferred_element_type=F32))
            for i in range(4):
                xs[rnd, i * 4 + y2] = part[i * 16 : i * 16 + 16]
            for x2 in x_peers + ([x] if k else []):
                send(xs.at[rnd, x2 * 4 + y2], xrs.at[rnd, mine_xy], rnd, XR, dev(z, x2, h, y2, c))
        xrs[rnd, mine_xy] = xs[rnd, mine_xy]

        @pl.when(rnd == 0)
        def _():
            all_columns()
            mt[rnd] = mfull[...]

        gown[rnd] = lax.dot_general(
            mt[rnd, pl.ds(pl.multiple_of((c * 4 + z) * 16, 16), 16), :],
            mt[rnd], NT, precision=HIGHEST, preferred_element_type=F32,
        )
        for y2 in y_peers:
            send(gown.at[rnd], gys.at[rnd, y], rnd, GY, dev(z, x, h, y2, c))
        gys[rnd, y] = gown[rnd]
        landed(xrs.at[rnd, pl.ds(0, 15)], rnd, XR)
        total = xrs[rnd, 0]
        for i in range(1, 16):
            total = total + xrs[rnd, i]
        xt[rnd, mine_cy] = total
        for y2, c2 in yc_peers:
            piece = xt.at[rnd, mine_cy]
            send(piece, piece, rnd, XG, dev(z, x, h, y2, c2))
        landed(gys.at[rnd, pl.ds(0, 3)], rnd, GY)
        gsum[rnd] = (gys[rnd, 0] + gys[rnd, 1]) + (gys[rnd, 2] + gys[rnd, 3])
        for x2 in x_peers:
            send(gsum.at[rnd], gxs.at[rnd, x], rnd, GX, dev(z, x2, h, y, c))
        gxs[rnd, x] = gsum[rnd]

        landed(xt.at[rnd, pl.ds(0, 7)], rnd, XG)

        rows = [jnp.concatenate([xt[rnd, i * 4 + m] for m in range(4)], axis=1) for i in range(2)]
        lhs = stacked(jnp.concatenate(rows, axis=0))
        for n, (lo, size) in enumerate(PARTS):
            part = folded(jnp.dot(lhs, b[:, lo : lo + size], preferred_element_type=F32))
            ps[rnd, :, :, lo : lo + size] = part.reshape(4, 8, size)
            for z2 in z_peers:
                span = pl.ds(lo, size)
                send(ps.at[rnd, z2, :, span], prs.at[rnd, z, :, span], rnd, PR[n], dev(z2, x, h, y, c))
            if n == 0:
                landed(gxs.at[rnd, pl.ds(0, 3)], rnd, GX)
                gfull[rnd, c, z] = (gxs[rnd, 0] + gxs[rnd, 1]) + (gxs[rnd, 2] + gxs[rnd, 3])
                for z2 in z_peers:
                    piece = gfull.at[rnd, c, z]
                    send(piece, piece, rnd, GZ, dev(z2, x, h, y, c))
        prs[rnd, z] = ps[rnd, z]

        @pl.when(rnd == ROUNDS - 1)
        def _():
            for y2 in y_peers:
                send(
                    mt.at[rnd, :, pl.ds(pl.multiple_of(c * 256, 256), 256)],
                    mg.at[y, c],
                    0, PHASES,
                    dev(z, x, h, y2, c),
                )

        for n, (lo, size) in enumerate(PARTS):
            span = pl.ds(lo, size)
            landed(prs.at[rnd, pl.ds(0, 3), :, span], rnd, PR[n])
            got = [prs[rnd, i, :, lo : lo + size] for i in range(4)]
            pt[rnd + 1, z, :, lo : lo + size] = (got[0] + got[1]) + (got[2] + got[3])
            for z2 in z_peers:
                piece = pt.at[rnd + 1, z, :, span]
                send(piece, piece, rnd, PG[n] + z, dev(z2, x, h, y, c))

            @pl.when(rnd == ROUNDS - 1)
            def _():
                to_row(z, n)

        landed(gfull.at[rnd, c, pl.ds(0, 3)], rnd, GZ)
        send(gfull.at[rnd, c], gfull.at[rnd, c], rnd, GC, partner)

        @pl.when(rnd < ROUNDS - 1)
        def _():
            def ready(n):
                for z2 in z_peers:
                    gathered_p(rnd, n, z2)

            tokens_part(rnd + 1, ready)

        return carry

    lax.fori_loop(0, ROUNDS, one_round, 0)

    last = ROUNDS - 1
    landed(gfull.at[last, o], last, GC)
    factor_start(last)
    factor_blocks(0, 2)
    for n in range(len(PARTS)):
        for k in (1, 3, 2):
            z2 = (z + k) % 4
            gathered_p(last, n, z2)
            to_row(z2, n)
        if n == 0:
            factor_blocks(2, 4)
    landed(mg.at[pl.ds(0, 3), 0], 0, PHASES)
    for y2 in y_peers:
        piece = mg.at[y2, c]
        send(piece, piece, 1, PHASES, partner)
    for cc in range(2):
        mg[y, cc] = mt[last, :, cc * 256 : cc * 256 + 256]
    cf[x] = pt[ROUNDS]
    factor_blocks(4, 16)
    final = work[:, RANK:]
    scaled = final * math.sqrt(D)
    landed(mg.at[pl.ds(0, 3), 0], 1, PHASES)
    for i in range(4):
        for cc in range(2):
            r0 = i * FEAT + cc * 256
            basis_ref[r0 : r0 + 256, :] = lax.dot_general(
                mg[i, cc].T, scaled, NT, precision=HIGHEST, preferred_element_type=F32
            )
    landed(cf.at[pl.ds(0, 3)], 2, PHASES)
    coef_ref[...] = jnp.dot(final, cf[...].reshape(RANK, HID), precision=HIGHEST, preferred_element_type=F32)

    def drain(rnd, carry):
        left(yrs.at[rnd, pl.ds(0, 7)], rnd, YR)
        left(yt.at[rnd, pl.ds(0, 15)], rnd, YG)
        for n, (lo, size) in enumerate(HALVES):
            span = pl.ds(lo, size)
            left(mrs.at[rnd, pl.ds(0, 7), :, span], rnd, MR[n])
            left(mraw.at[rnd, 0, pl.ds(0, 7), :, span], rnd, MG[n])
        left(mraw.at[rnd, 0], rnd, MC)
        left(xrs.at[rnd, pl.ds(0, 15)], rnd, XR)
        left(xt.at[rnd, pl.ds(0, 7)], rnd, XG)
        for n, (lo, size) in enumerate(PARTS):
            span = pl.ds(lo, size)
            left(prs.at[rnd, pl.ds(0, 3), :, span], rnd, PR[n])
            left(pt.at[rnd, pl.ds(0, 3), :, span], rnd, PG[n] + z)
        left(gys.at[rnd, pl.ds(0, 3)], rnd, GY)
        left(gxs.at[rnd, pl.ds(0, 3)], rnd, GX)
        left(gfull.at[rnd, 0, pl.ds(0, 3)], rnd, GZ)
        left(gfull.at[rnd, 0], rnd, GC)
        return carry

    lax.fori_loop(0, ROUNDS, drain, 0)
    left(mg.at[pl.ds(0, 3), 0], 0, PHASES)
    left(mg.at[pl.ds(0, 3), 0], 1, PHASES)
    left(cf.at[pl.ds(0, 3)], 2, PHASES)


def body(activations, grad_out, sketch):
    anywhere = pl.BlockSpec(memory_space=pl.ANY)
    inside = pl.BlockSpec(memory_space=pltpu.VMEM)
    vm = pltpu.VMEM
    n = ROUNDS
    return pl.pallas_call(
        kernel,
        name="range_finder",
        out_shape=(
            jax.ShapeDtypeStruct((2048, RANK), F32),
            jax.ShapeDtypeStruct((RANK, HID), F32),
        ),
        in_specs=[anywhere] * 3,
        out_specs=(inside, inside),
        scratch_shapes=[
            vm((TOK, FEAT), BF16),
            vm((TOK, HID), BF16),
            vm((HID, RANK), F32),
            vm((RANK, HID), F32),
            vm((n + 1, 4, 8, HID), F32),
            vm((4, 32, 256), F32),
            vm((n, 8, 16, 256), F32),
            vm((n, 8, 16, 256), F32),
            vm((n, 16, 16, 256), F32),
            vm((n, 8, 8, FEAT), F32),
            vm((n, 8, 8, FEAT), F32),
            vm((n, 2, 8, 8, FEAT), F32),
            vm((RANK, FEAT), F32),
            vm((n, RANK, FEAT), F32),
            vm((64, FEAT), F32),
            vm((n, 16, 16, 256), F32),
            vm((n, 16, 16, 256), F32),
            vm((n, 8, 16, 256), F32),
            vm((n, 4, 8, HID), F32),
            vm((n, 4, 8, HID), F32),
            vm((n, 16, RANK), F32),
            vm((n, 4, 16, RANK), F32),
            vm((n, 16, RANK), F32),
            vm((n, 4, 16, RANK), F32),
            vm((n, 2, 4, 16, RANK), F32),
            vm((RANK, 2 * RANK), F32),
            vm((4, 4, 8, HID), F32),
            vm((4, 2, RANK, 256), F32),
            pltpu.SemaphoreType.DMA((2 + len(PARTS),)),
            pltpu.SemaphoreType.DMA((n, PHASES + 1)),
            pltpu.SemaphoreType.DMA((n, PHASES + 1)),
        ],
        compiler_params=pltpu.CompilerParams(
            collective_id=0, has_side_effects=True, vmem_limit_bytes=50 * 2**20
        ),
    )(activations, grad_out, pltpu.with_memory_space_constraint(sketch, pltpu.HBM))


def solution(mesh):
    in_specs = (P("dp", "row"), P("dp", "col"), P("col", None))
    out_specs = (P("row", None), P(None, "col"))
    return jax.shard_map(body, mesh=mesh, in_specs=in_specs, out_specs=out_specs, check_vma=False)
```

```python
import functools
import math

import jax
import jax.numpy as jnp
from jax import lax
from jax.experimental import pallas as pl
from jax.experimental.pallas import tpu as pltpu
from jax.sharding import PartitionSpec as P

MESH = pl.DeviceIdType.MESH
F32 = jnp.float32
BF16 = jnp.bfloat16
HIGHEST = lax.Precision.HIGHEST
D = 8192
RANK = 128
ROUNDS = 3
TOK = 1024
HID = 1664
FEAT = 512
NT = (((1,), (1,)), ((), ()))
TN = (((0,), (0,)), ((), ()))
PARTS = ((0, 256), (256, 384), (640, 384), (1024, 384), (1408, 256))
HALVES = ((0, 256), (256, 256))
YR, YG, MC, XR, XG, GY, GX, GZ, GC = range(9)
MR = range(9, 9 + len(HALVES))
MG = range(MR.stop, MR.stop + len(HALVES))
PR = range(MG.stop, MG.stop + len(PARTS))
PG = range(PR.stop, PR.stop + 4 * len(PARTS), 4)
PHASES = PG.stop
XY = (
    (2, 2), (2, 1), (2, 3), (1, 2), (3, 2), (1, 1), (1, 3), (3, 1), (3, 3),
    (2, 0), (0, 2), (1, 0), (3, 0), (0, 1), (0, 3),
)
ZH = ((2, 1), (1, 1), (3, 1), (0, 1), (2, 0), (1, 0), (3, 0))


def stacked(mat):
    high = mat.astype(BF16)
    rest = mat - high.astype(F32)
    mid = rest.astype(BF16)
    low = (rest - mid.astype(F32)).astype(BF16)
    return jnp.concatenate([high, mid, low], axis=0)


def outer(left, right):
    def three(mat):
        high = mat.astype(BF16).astype(F32)
        mid = (mat - high).astype(BF16).astype(F32)
        return high, mid, (mat - high - mid).astype(BF16).astype(F32)

    lh, lm, ll = three(left)
    rh, rm, rl = three(right)
    return lax.dot_general(
        jnp.concatenate([lh, lh, lm, lh, ll, lm], axis=0).astype(BF16),
        jnp.concatenate([rh, rm, rh, rl, rh, rm], axis=0).astype(BF16),
        TN, preferred_element_type=F32,
    )


def folded(wide):
    rows = wide.shape[0] // 3
    return wide[:rows] + (wide[rows : 2 * rows] + wide[2 * rows :])


def kernel(
    a_hbm, b_hbm, s_hbm, basis_ref, coef_ref,
    a, b, s, st, pt, yacc, ysend, yrs, yt, ms, mrs, mraw, mfull, mt, xl, xs, xrs, xt,
    ps, prs, gown, gys, gsum, gxs, gfull, work, cf, mg,
    load_sem, send_sem, recv_sem,
):
    z, x, j = lax.axis_index("dp"), lax.axis_index("row"), lax.axis_index("col")
    c = j % 2
    y = (j // 2) % 4
    h = j // 8
    o = 1 - c
    mine_xy = x * 4 + y
    mine_hz = h * 4 + z
    mine_cy = c * 4 + y

    def dev(z_, x_, h_, y_, c_):
        return (z_, x_, (h_ * 4 + y_) * 2 + c_)

    partner = dev(z, x, h, y, o)
    xy_peers = [((x + dx) % 4, (y + dy) % 4) for dx, dy in XY]
    zh_peers = [((z + dz) % 4, (h + dh) % 2) for dz, dh in ZH]
    z_peers = [(z + k) % 4 for k in (2, 1, 3)]
    y_peers = [(y + k) % 4 for k in (2, 1, 3)]
    yc_peers = [((y + k) % 4, c2) for k in (2, 1, 3) for c2 in (c, o)] + [(y, o)]
    x_peers = [(x + k) % 4 for k in (2, 1, 3)]

    barrier = pltpu.get_barrier_semaphore()

    def greet(device):
        pl.semaphore_signal(barrier, inc=1, device_id=device, device_id_type=MESH)

    loads = [
        pltpu.make_async_copy(s_hbm, s, load_sem.at[0]),
    ]
    for n, (lo, size) in enumerate(PARTS):
        span = pl.ds(lo, size)
        loads.append(pltpu.make_async_copy(b_hbm.at[:, span], b.at[:, span], load_sem.at[1 + n]))
    loads.append(
        pltpu.make_async_copy(
            a_hbm.at[:, pl.ds(pl.multiple_of(y * FEAT, FEAT), FEAT)], a, load_sem.at[1 + len(PARTS)]
        )
    )
    for load in loads:
        load.start()

    for (x2, y2), (dx, _) in zip(xy_peers, XY):
        if dx:
            greet(dev(z, x2, h, y2, c))
    for z2, h2 in zh_peers:
        greet(dev(z2, x, h2, y, c))
    for y2, c2 in yc_peers:
        greet(dev(z, x, h, y2, c2))

    def send(src, dst, rnd, phase, device):
        pltpu.make_async_remote_copy(
            src_ref=src,
            dst_ref=dst,
            send_sem=send_sem.at[rnd, phase],
            recv_sem=recv_sem.at[rnd, phase],
            device_id=device,
            device_id_type=MESH,
        ).start()

    def landed(like, rnd, phase):
        pltpu.make_async_copy(like, like, recv_sem.at[rnd, phase]).wait()

    def left(like, rnd, phase):
        pltpu.make_async_copy(like, like, send_sem.at[rnd, phase]).wait()

    row_iota = lax.broadcasted_iota(jnp.int32, (RANK, RANK), 0)
    col_iota = lax.broadcasted_iota(jnp.int32, (RANK, RANK), 1)
    eye = jnp.where(row_iota == col_iota, 1.0, 0.0).astype(F32)

    def factor_start(rnd):
        work[:, :RANK] = gfull[rnd].reshape(RANK, RANK)
        work[:, RANK:] = eye

    sub = lax.broadcasted_iota(jnp.int32, (8, RANK), 0)
    lane = lax.broadcasted_iota(jnp.int32, (8, RANK), 1)

    def spread(row):
        return jnp.broadcast_to(row, (8, RANK))

    def factor_block(blk, carry):
        r0 = pl.multiple_of(blk * 8, 8)
        gp = work[pl.ds(r0, 8), :RANK]
        ep = work[pl.ds(r0, 8), RANK:]
        diag = pltpu.roll(gp, RANK - r0, 1)
        cols = [jnp.broadcast_to(diag[:, i : i + 1], (8, RANK)) for i in range(8)]
        inv = [jnp.where(sub == i, 1.0, 0.0).astype(F32) for i in range(8)]
        pivots = jnp.ones((8, RANK), F32)
        for i in range(8):
            pivot = spread(cols[i][i : i + 1])
            pivots = jnp.where(sub == i, pivot, pivots)
            if i == 7:
                break
            scale = jnp.where(sub > i, cols[i] * (1.0 / pivot), 0.0)
            for m in range(i + 1, 8):
                cols[m] = cols[m] - scale * spread(cols[m][i : i + 1])
            for m in range(i + 1):
                inv[m] = inv[m] - scale * spread(inv[m][i : i + 1])
        root = lax.rsqrt(pivots)
        root = root * (1.5 - 0.5 * pivots * root * root)
        ug = jnp.zeros((8, RANK), F32)
        ue = jnp.zeros((8, RANK), F32)
        for m in range(8):
            weight = inv[m] * root
            ug = ug + weight * spread(gp[m : m + 1])
            ue = ue + weight * spread(ep[m : m + 1])
        work[pl.ds(r0, 8), RANK:] = ue
        rest = jnp.where(lane >= r0 + 8, ug, 0.0)
        work[...] -= outer(rest, jnp.concatenate([ug, ue], axis=1))
        return carry

    def factor_blocks(lo, hi):
        lax.fori_loop(lo, hi, factor_block, 0)

    def tokens_part(rnd, ready):
        for n, (lo, size) in enumerate(PARTS):
            ready(n)
            lhs = stacked(pt[rnd, :, :, lo : lo + size].reshape(32, size))
            if n < len(PARTS) - 1:
                part = folded(lax.dot_general(lhs, b[:, lo : lo + size], NT, preferred_element_type=F32))
                for m in range(4):
                    quarter = part[:, m * 256 : m * 256 + 256]
                    yacc[m] = yacc[m] + quarter if n else quarter
        for k in (2, 1, 3, 0):
            y2 = (y + k) % 4
            rows = b[pl.ds(pl.multiple_of(y2 * 256, 256), 256), lo : lo + size]
            quarter = folded(lax.dot_general(lhs, rows, NT, preferred_element_type=F32))
            if len(PARTS) > 1:
                quarter = yacc[y2] + quarter
            ysend[rnd, y2] = quarter[:16]
            ysend[rnd, 4 + y2] = quarter[16:]
            for c2 in (c, o) if k else (o,):
                send(ysend.at[rnd, c2 * 4 + y2], yrs.at[rnd, mine_cy], rnd, YR, dev(z, x, h, y2, c2))

    loads[0].wait()
    st[...] = s[...].T
    pt[0] = st[pl.ds(pl.multiple_of(x * 32, 32), 32), :].reshape(4, 8, HID)

    def begin(n):
        loads[1 + n].wait()
        if n == len(PARTS) - 1:
            pl.semaphore_wait(barrier, 26)

    tokens_part(0, begin)
    loads[-1].wait()

    def to_row(z2, n):
        span = pl.ds(*PARTS[n])
        for x2 in x_peers:
            send(pt.at[ROUNDS, z2, :, span], cf.at[x, z2, :, span], 2, PHASES, dev(z, x2, h, y, c))

    def gathered_p(rnd, n, z2):
        lo, size = PARTS[n]
        landed(pt.at[rnd + 1, z2, :, pl.ds(lo, size)], rnd, PG[n] + z2)

    def share_gram(rnd):
        landed(gfull.at[rnd, c, pl.ds(0, 3)], rnd, GZ)
        send(gfull.at[rnd, c], gfull.at[rnd, c], rnd, GC, partner)

    def one_round(rnd, carry):
        yrs[rnd, mine_cy] = ysend[rnd, mine_cy]

        @pl.when(rnd > 0)
        def _():
            landed(gfull.at[rnd - 1, o], rnd - 1, GC)
            factor_start(rnd - 1)
            factor_blocks(0, 4)

        landed(yrs.at[rnd, pl.ds(0, 7)], rnd, YR)
        got = [yrs[rnd, i] for i in range(8)]
        yt[rnd, mine_xy] = ((got[0] + got[1]) + (got[2] + got[3])) + ((got[4] + got[5]) + (got[6] + got[7]))
        for x2, y2 in xy_peers:
            piece = yt.at[rnd, mine_xy]
            send(piece, piece, rnd, YG, dev(z, x2, h, y2, c))

        @pl.when(rnd > 0)
        def _():
            factor_blocks(4, 9)

        landed(yt.at[rnd, pl.ds(0, 15)], rnd, YG)

        rows = [jnp.concatenate([yt[rnd, i * 4 + m] for m in range(4)], axis=1) for i in range(4)]
        lhs = stacked(jnp.concatenate(rows, axis=0))
        for n, (lo, size) in enumerate(HALVES):
            span = pl.ds(lo, size)
            part = folded(jnp.dot(lhs, a[:, lo : lo + size], preferred_element_type=F32))
            for i in range(8):
                ms[rnd, i, :, lo : lo + size] = part[i * 8 : i * 8 + 8]
            for z2, h2 in zh_peers:
                send(
                    ms.at[rnd, h2 * 4 + z2, :, span], mrs.at[rnd, mine_hz, :, span], rnd, MR[n], dev(z2, x, h2, y, c)
                )
        mrs[rnd, mine_hz] = ms[rnd, mine_hz]

        @pl.when(rnd > 0)
        def _():
            factor_blocks(9, 14)

        for n, (lo, size) in enumerate(HALVES):
            span = pl.ds(lo, size)
            landed(mrs.at[rnd, pl.ds(0, 7), :, span], rnd, MR[n])
            got = [mrs[rnd, i, :, lo : lo + size] for i in range(8)]
            mraw[rnd, c, mine_hz, :, lo : lo + size] = ((got[0] + got[1]) + (got[2] + got[3])) + (
                (got[4] + got[5]) + (got[6] + got[7])
            )
            for z2, h2 in zh_peers:
                piece = mraw.at[rnd, c, mine_hz, :, span]
                send(piece, piece, rnd, MG[n], dev(z2, x, h2, y, c))

        @pl.when(rnd > 0)
        def _():
            factor_blocks(14, 16)

        for n, (lo, size) in enumerate(HALVES):
            landed(mraw.at[rnd, c, pl.ds(0, 7), :, pl.ds(lo, size)], rnd, MG[n])
        send(mraw.at[rnd, c], mraw.at[rnd, c], rnd, MC, partner)

        def all_columns():
            landed(mraw.at[rnd, o], rnd, MC)
            for cc in range(2):
                for i in range(8):
                    r0 = (i // 2) * 32 + cc * 16 + (i % 2) * 8
                    mfull[r0 : r0 + 8, :] = mraw[rnd, cc, i]

        @pl.when(rnd == 0)
        def _():
            for i in range(8):
                xl[i * 8 : i * 8 + 8, :] = mraw[rnd, c, i]

        @pl.when(rnd > 0)
        def _():
            all_columns()
            mt[rnd] = jnp.dot(work[:, RANK:], mfull[...], precision=HIGHEST, preferred_element_type=F32)
            for i in range(4):
                xl[i * 16 : i * 16 + 16, :] = mt[rnd, pl.ds(pl.multiple_of(i * 32 + c * 16, 16), 16), :]

        lhs = stacked(xl[...])
        for k in (2, 1, 3, 0):
            y2 = (y + k) % 4
            rows = a[pl.ds(pl.multiple_of(y2 * 256, 256), 256), :]
            part = folded(lax.dot_general(lhs, rows, NT, preferred_element_type=F32))
            for i in range(4):
                xs[rnd, i * 4 + y2] = part[i * 16 : i * 16 + 16]
            for x2 in x_peers + ([x] if k else []):
                send(xs.at[rnd, x2 * 4 + y2], xrs.at[rnd, mine_xy], rnd, XR, dev(z, x2, h, y2, c))
        xrs[rnd, mine_xy] = xs[rnd, mine_xy]

        @pl.when(rnd == 0)
        def _():
            all_columns()
            mt[rnd] = mfull[...]

        gown[rnd] = lax.dot_general(
            mt[rnd, pl.ds(pl.multiple_of((c * 4 + z) * 16, 16), 16), :],
            mt[rnd], NT, precision=HIGHEST, preferred_element_type=F32,
        )
        for y2 in y_peers:
            send(gown.at[rnd], gys.at[rnd, y], rnd, GY, dev(z, x, h, y2, c))
        gys[rnd, y] = gown[rnd]
        landed(xrs.at[rnd, pl.ds(0, 15)], rnd, XR)
        total = xrs[rnd, 0]
        for i in range(1, 16):
            total = total + xrs[rnd, i]
        xt[rnd, mine_cy] = total
        for y2, c2 in yc_peers:
            piece = xt.at[rnd, mine_cy]
            send(piece, piece, rnd, XG, dev(z, x, h, y2, c2))
        landed(gys.at[rnd, pl.ds(0, 3)], rnd, GY)
        gsum[rnd] = (gys[rnd, 0] + gys[rnd, 1]) + (gys[rnd, 2] + gys[rnd, 3])
        for x2 in x_peers:
            send(gsum.at[rnd], gxs.at[rnd, x], rnd, GX, dev(z, x2, h, y, c))
        gxs[rnd, x] = gsum[rnd]

        landed(xt.at[rnd, pl.ds(0, 7)], rnd, XG)

        rows = [jnp.concatenate([xt[rnd, i * 4 + m] for m in range(4)], axis=1) for i in range(2)]
        lhs = stacked(jnp.concatenate(rows, axis=0))
        for n, (lo, size) in enumerate(PARTS):
            part = folded(jnp.dot(lhs, b[:, lo : lo + size], preferred_element_type=F32))
            ps[rnd, :, :, lo : lo + size] = part.reshape(4, 8, size)
            for z2 in z_peers:
                span = pl.ds(lo, size)
                send(ps.at[rnd, z2, :, span], prs.at[rnd, z, :, span], rnd, PR[n], dev(z2, x, h, y, c))
            if n == 0:
                landed(gxs.at[rnd, pl.ds(0, 3)], rnd, GX)
                gfull[rnd, c, z] = (gxs[rnd, 0] + gxs[rnd, 1]) + (gxs[rnd, 2] + gxs[rnd, 3])
                for z2 in z_peers:
                    piece = gfull.at[rnd, c, z]
                    send(piece, piece, rnd, GZ, dev(z2, x, h, y, c))
        prs[rnd, z] = ps[rnd, z]

        @pl.when(rnd == ROUNDS - 1)
        def _():
            for y2 in y_peers:
                send(
                    mt.at[rnd, :, pl.ds(pl.multiple_of(c * 256, 256), 256)],
                    mg.at[y, c],
                    0, PHASES,
                    dev(z, x, h, y2, c),
                )

        @pl.when(rnd == ROUNDS - 1)
        def _():
            share_gram(rnd)
            landed(gfull.at[rnd, o], rnd, GC)
            factor_start(rnd)

        for n, (lo, size) in enumerate(PARTS):
            span = pl.ds(lo, size)
            landed(prs.at[rnd, pl.ds(0, 3), :, span], rnd, PR[n])
            got = [prs[rnd, i, :, lo : lo + size] for i in range(4)]
            pt[rnd + 1, z, :, lo : lo + size] = (got[0] + got[1]) + (got[2] + got[3])
            for z2 in z_peers:
                piece = pt.at[rnd + 1, z, :, span]
                send(piece, piece, rnd, PG[n] + z, dev(z2, x, h, y, c))

            @pl.when(rnd == ROUNDS - 1)
            def _():
                to_row(z, n)
                factor_blocks(n * 6 // len(PARTS), (n + 1) * 6 // len(PARTS))


        @pl.when(rnd < ROUNDS - 1)
        def _():
            share_gram(rnd)

            def ready(n):
                for z2 in z_peers:
                    gathered_p(rnd, n, z2)

            tokens_part(rnd + 1, ready)

        return carry

    lax.fori_loop(0, ROUNDS, one_round, 0)

    last = ROUNDS - 1
    done = 6
    for n in range(len(PARTS)):
        for k in (1, 3, 2):
            z2 = (z + k) % 4
            gathered_p(last, n, z2)
            to_row(z2, n)
        if n < len(PARTS) - 1:
            factor_blocks(done, done + 1)
            done += 1
    landed(mg.at[pl.ds(0, 3), 0], 0, PHASES)
    for y2 in y_peers:
        piece = mg.at[y2, c]
        send(piece, piece, 1, PHASES, partner)
    for cc in range(2):
        mg[y, cc] = mt[last, :, cc * 256 : cc * 256 + 256]
    cf[x] = pt[ROUNDS]
    factor_blocks(done, 16)
    final = work[:, RANK:]
    scaled = final * math.sqrt(D)
    landed(mg.at[pl.ds(0, 3), 0], 1, PHASES)
    for i in range(4):
        for cc in range(2):
            r0 = i * FEAT + cc * 256
            basis_ref[r0 : r0 + 256, :] = lax.dot_general(
                mg[i, cc].T, scaled, NT, precision=HIGHEST, preferred_element_type=F32
            )
    landed(cf.at[pl.ds(0, 3)], 2, PHASES)
    coef_ref[...] = jnp.dot(final, cf[...].reshape(RANK, HID), precision=HIGHEST, preferred_element_type=F32)

    def drain(rnd, carry):
        left(yrs.at[rnd, pl.ds(0, 7)], rnd, YR)
        left(yt.at[rnd, pl.ds(0, 15)], rnd, YG)
        for n, (lo, size) in enumerate(HALVES):
            span = pl.ds(lo, size)
            left(mrs.at[rnd, pl.ds(0, 7), :, span], rnd, MR[n])
            left(mraw.at[rnd, 0, pl.ds(0, 7), :, span], rnd, MG[n])
        left(mraw.at[rnd, 0], rnd, MC)
        left(xrs.at[rnd, pl.ds(0, 15)], rnd, XR)
        left(xt.at[rnd, pl.ds(0, 7)], rnd, XG)
        for n, (lo, size) in enumerate(PARTS):
            span = pl.ds(lo, size)
            left(prs.at[rnd, pl.ds(0, 3), :, span], rnd, PR[n])
            left(pt.at[rnd, pl.ds(0, 3), :, span], rnd, PG[n] + z)
        left(gys.at[rnd, pl.ds(0, 3)], rnd, GY)
        left(gxs.at[rnd, pl.ds(0, 3)], rnd, GX)
        left(gfull.at[rnd, 0, pl.ds(0, 3)], rnd, GZ)
        left(gfull.at[rnd, 0], rnd, GC)
        return carry

    lax.fori_loop(0, ROUNDS, drain, 0)
    left(mg.at[pl.ds(0, 3), 0], 0, PHASES)
    left(mg.at[pl.ds(0, 3), 0], 1, PHASES)
    left(cf.at[pl.ds(0, 3)], 2, PHASES)


def body(activations, grad_out, sketch):
    anywhere = pl.BlockSpec(memory_space=pl.ANY)
    inside = pl.BlockSpec(memory_space=pltpu.VMEM)
    vm = pltpu.VMEM
    n = ROUNDS
    return pl.pallas_call(
        kernel,
        name="range_finder",
        out_shape=(
            jax.ShapeDtypeStruct((2048, RANK), F32),
            jax.ShapeDtypeStruct((RANK, HID), F32),
        ),
        in_specs=[anywhere] * 3,
        out_specs=(inside, inside),
        scratch_shapes=[
            vm((TOK, FEAT), BF16),
            vm((TOK, HID), BF16),
            vm((HID, RANK), F32),
            vm((RANK, HID), F32),
            vm((n + 1, 4, 8, HID), F32),
            vm((4, 32, 256), F32),
            vm((n, 8, 16, 256), F32),
            vm((n, 8, 16, 256), F32),
            vm((n, 16, 16, 256), F32),
            vm((n, 8, 8, FEAT), F32),
            vm((n, 8, 8, FEAT), F32),
            vm((n, 2, 8, 8, FEAT), F32),
            vm((RANK, FEAT), F32),
            vm((n, RANK, FEAT), F32),
            vm((64, FEAT), F32),
            vm((n, 16, 16, 256), F32),
            vm((n, 16, 16, 256), F32),
            vm((n, 8, 16, 256), F32),
            vm((n, 4, 8, HID), F32),
            vm((n, 4, 8, HID), F32),
            vm((n, 16, RANK), F32),
            vm((n, 4, 16, RANK), F32),
            vm((n, 16, RANK), F32),
            vm((n, 4, 16, RANK), F32),
            vm((n, 2, 4, 16, RANK), F32),
            vm((RANK, 2 * RANK), F32),
            vm((4, 4, 8, HID), F32),
            vm((4, 2, RANK, 256), F32),
            pltpu.SemaphoreType.DMA((2 + len(PARTS),)),
            pltpu.SemaphoreType.DMA((n, PHASES + 1)),
            pltpu.SemaphoreType.DMA((n, PHASES + 1)),
        ],
        compiler_params=pltpu.CompilerParams(
            collective_id=0, has_side_effects=True, vmem_limit_bytes=50 * 2**20
        ),
    )(activations, grad_out, pltpu.with_memory_space_constraint(sketch, pltpu.HBM))


def solution(mesh):
    in_specs = (P("dp", "row"), P("dp", "col"), P("col", None))
    out_specs = (P("row", None), P(None, "col"))
    return jax.shard_map(body, mesh=mesh, in_specs=in_specs, out_specs=out_specs, check_vma=False)
```

```python
import functools
import math

import jax
import jax.numpy as jnp
from jax import lax
from jax.experimental import pallas as pl
from jax.experimental.pallas import tpu as pltpu
from jax.sharding import PartitionSpec as P

MESH = pl.DeviceIdType.MESH
F32 = jnp.float32
BF16 = jnp.bfloat16
HIGHEST = lax.Precision.HIGHEST
D = 8192
RANK = 128
ROUNDS = 3
TOK = 1024
HID = 1664
FEAT = 512
NT = (((1,), (1,)), ((), ()))
TN = (((0,), (0,)), ((), ()))
PARTS = ((0, 256), (256, 384), (640, 384), (1024, 384), (1408, 256))
HALVES = ((0, 256), (256, 256))
YR, YG, MC, XR, XG, GY, GX, GZ, GC = range(9)
MR = range(9, 9 + len(HALVES))
MG = range(MR.stop, MR.stop + len(HALVES))
PR = range(MG.stop, MG.stop + len(PARTS))
PG = range(PR.stop, PR.stop + 4 * len(PARTS), 4)
PHASES = PG.stop
XY = (
    (2, 2), (2, 1), (2, 3), (1, 2), (3, 2), (1, 1), (1, 3), (3, 1), (3, 3),
    (2, 0), (0, 2), (1, 0), (3, 0), (0, 1), (0, 3),
)
ZH = ((2, 1), (1, 1), (3, 1), (0, 1), (2, 0), (1, 0), (3, 0))


def stacked(mat):
    high = mat.astype(BF16)
    rest = mat - high.astype(F32)
    mid = rest.astype(BF16)
    low = (rest - mid.astype(F32)).astype(BF16)
    return jnp.concatenate([high, mid, low], axis=0)


def outer(left, right):
    def three(mat):
        high = mat.astype(BF16).astype(F32)
        mid = (mat - high).astype(BF16).astype(F32)
        return high, mid, (mat - high - mid).astype(BF16).astype(F32)

    lh, lm, ll = three(left)
    rh, rm, rl = three(right)
    return lax.dot_general(
        jnp.concatenate([lh, lh, lm, lh, ll, lm], axis=0).astype(BF16),
        jnp.concatenate([rh, rm, rh, rl, rh, rm], axis=0).astype(BF16),
        TN, preferred_element_type=F32,
    )


def folded(wide):
    rows = wide.shape[0] // 3
    return wide[:rows] + (wide[rows : 2 * rows] + wide[2 * rows :])


def kernel(
    a_hbm, b_hbm, s_hbm, basis_ref, coef_ref,
    a, b, s, st, pt, yacc, ysend, yrs, yt, ms, mrs, mraw, mfull, mt, xl, xs, xrs, xt,
    ps, prs, gown, gys, gsum, gxs, gfull, work, cf, mg,
    load_sem, send_sem, recv_sem,
):
    z, x, j = lax.axis_index("dp"), lax.axis_index("row"), lax.axis_index("col")
    c = j % 2
    y = (j // 2) % 4
    h = j // 8
    o = 1 - c
    mine_xy = x * 4 + y
    mine_hz = h * 4 + z
    mine_cy = c * 4 + y

    def dev(z_, x_, h_, y_, c_):
        return (z_, x_, (h_ * 4 + y_) * 2 + c_)

    partner = dev(z, x, h, y, o)
    xy_peers = [((x + dx) % 4, (y + dy) % 4) for dx, dy in XY]
    zh_peers = [((z + dz) % 4, (h + dh) % 2) for dz, dh in ZH]
    z_peers = [(z + k) % 4 for k in (2, 1, 3)]
    y_peers = [(y + k) % 4 for k in (2, 1, 3)]
    yc_peers = [((y + k) % 4, c2) for k in (2, 1, 3) for c2 in (c, o)] + [(y, o)]
    x_peers = [(x + k) % 4 for k in (2, 1, 3)]

    barrier = pltpu.get_barrier_semaphore()

    def greet(device):
        pl.semaphore_signal(barrier, inc=1, device_id=device, device_id_type=MESH)

    loads = [
        pltpu.make_async_copy(s_hbm, s, load_sem.at[0]),
    ]
    for n, (lo, size) in enumerate(PARTS):
        span = pl.ds(lo, size)
        loads.append(pltpu.make_async_copy(b_hbm.at[:, span], b.at[:, span], load_sem.at[1 + n]))
    loads.append(
        pltpu.make_async_copy(
            a_hbm.at[:, pl.ds(pl.multiple_of(y * FEAT, FEAT), FEAT)], a, load_sem.at[1 + len(PARTS)]
        )
    )
    for load in loads:
        load.start()

    for (x2, y2), (dx, _) in zip(xy_peers, XY):
        if dx:
            greet(dev(z, x2, h, y2, c))
    for z2, h2 in zh_peers:
        greet(dev(z2, x, h2, y, c))
    for y2, c2 in yc_peers:
        greet(dev(z, x, h, y2, c2))

    def send(src, dst, rnd, phase, device):
        pltpu.make_async_remote_copy(
            src_ref=src,
            dst_ref=dst,
            send_sem=send_sem.at[rnd, phase],
            recv_sem=recv_sem.at[rnd, phase],
            device_id=device,
            device_id_type=MESH,
        ).start()

    def landed(like, rnd, phase):
        pltpu.make_async_copy(like, like, recv_sem.at[rnd, phase]).wait()

    def left(like, rnd, phase):
        pltpu.make_async_copy(like, like, send_sem.at[rnd, phase]).wait()

    row_iota = lax.broadcasted_iota(jnp.int32, (RANK, RANK), 0)
    col_iota = lax.broadcasted_iota(jnp.int32, (RANK, RANK), 1)
    eye = jnp.where(row_iota == col_iota, 1.0, 0.0).astype(F32)

    def factor_start(rnd):
        work[:, :RANK] = gfull[rnd].reshape(RANK, RANK)
        work[:, RANK:] = eye

    sub = lax.broadcasted_iota(jnp.int32, (8, RANK), 0)
    lane = lax.broadcasted_iota(jnp.int32, (8, RANK), 1)

    def spread(row):
        return jnp.broadcast_to(row, (8, RANK))

    def factor_block(blk, carry):
        r0 = pl.multiple_of(blk * 8, 8)
        gp = work[pl.ds(r0, 8), :RANK]
        ep = work[pl.ds(r0, 8), RANK:]
        diag = pltpu.roll(gp, RANK - r0, 1)
        cols = [jnp.broadcast_to(diag[:, i : i + 1], (8, RANK)) for i in range(8)]
        inv = [jnp.where(sub == i, 1.0, 0.0).astype(F32) for i in range(8)]
        pivots = jnp.ones((8, RANK), F32)
        for i in range(8):
            pivot = spread(cols[i][i : i + 1])
            pivots = jnp.where(sub == i, pivot, pivots)
            if i == 7:
                break
            scale = jnp.where(sub > i, cols[i] * (1.0 / pivot), 0.0)
            for m in range(i + 1, 8):
                cols[m] = cols[m] - scale * spread(cols[m][i : i + 1])
            for m in range(i + 1):
                inv[m] = inv[m] - scale * spread(inv[m][i : i + 1])
        root = lax.rsqrt(pivots)
        root = root * (1.5 - 0.5 * pivots * root * root)
        ug = jnp.zeros((8, RANK), F32)
        ue = jnp.zeros((8, RANK), F32)
        for m in range(8):
            weight = inv[m] * root
            ug = ug + weight * spread(gp[m : m + 1])
            ue = ue + weight * spread(ep[m : m + 1])
        work[pl.ds(r0, 8), RANK:] = ue
        rest = jnp.where(lane >= r0 + 8, ug, 0.0)
        work[...] -= outer(rest, jnp.concatenate([ug, ue], axis=1))
        return carry

    def factor_blocks(lo, hi):
        lax.fori_loop(lo, hi, factor_block, 0)

    def tokens_part(rnd, ready):
        for n, (lo, size) in enumerate(PARTS):
            ready(n)
            lhs = stacked(pt[rnd, :, :, lo : lo + size].reshape(32, size))
            if n < len(PARTS) - 1:
                part = folded(lax.dot_general(lhs, b[:, lo : lo + size], NT, preferred_element_type=F32))
                for m in range(4):
                    quarter = part[:, m * 256 : m * 256 + 256]
                    yacc[m] = yacc[m] + quarter if n else quarter
        for k in (2, 1, 3, 0):
            y2 = (y + k) % 4
            rows = b[pl.ds(pl.multiple_of(y2 * 256, 256), 256), lo : lo + size]
            quarter = folded(lax.dot_general(lhs, rows, NT, preferred_element_type=F32))
            if len(PARTS) > 1:
                quarter = yacc[y2] + quarter
            ysend[rnd, y2] = quarter[:16]
            ysend[rnd, 4 + y2] = quarter[16:]
            for c2 in (c, o) if k else (o,):
                send(ysend.at[rnd, c2 * 4 + y2], yrs.at[rnd, mine_cy], rnd, YR, dev(z, x, h, y2, c2))

    loads[0].wait()
    st[...] = s[...].T
    pt[0] = st[pl.ds(pl.multiple_of(x * 32, 32), 32), :].reshape(4, 8, HID)

    def begin(n):
        loads[1 + n].wait()
        if n == len(PARTS) - 1:
            pl.semaphore_wait(barrier, 26)

    tokens_part(0, begin)
    loads[-1].wait()

    def to_row(z2, n):
        span = pl.ds(*PARTS[n])
        for x2 in x_peers:
            send(pt.at[ROUNDS, z2, :, span], cf.at[x, z2, :, span], 2, PHASES + 1 + n, dev(z, x2, h, y, c))

    def gathered_p(rnd, n, z2):
        lo, size = PARTS[n]
        landed(pt.at[rnd + 1, z2, :, pl.ds(lo, size)], rnd, PG[n] + z2)

    def share_gram(rnd):
        landed(gfull.at[rnd, c, pl.ds(0, 3)], rnd, GZ)
        send(gfull.at[rnd, c], gfull.at[rnd, c], rnd, GC, partner)

    def one_round(rnd, carry):
        yrs[rnd, mine_cy] = ysend[rnd, mine_cy]

        @pl.when(rnd > 0)
        def _():
            landed(gfull.at[rnd - 1, o], rnd - 1, GC)
            factor_start(rnd - 1)
            factor_blocks(0, 4)

        landed(yrs.at[rnd, pl.ds(0, 7)], rnd, YR)
        got = [yrs[rnd, i] for i in range(8)]
        yt[rnd, mine_xy] = ((got[0] + got[1]) + (got[2] + got[3])) + ((got[4] + got[5]) + (got[6] + got[7]))
        for x2, y2 in xy_peers:
            piece = yt.at[rnd, mine_xy]
            send(piece, piece, rnd, YG, dev(z, x2, h, y2, c))

        @pl.when(rnd > 0)
        def _():
            factor_blocks(4, 9)

        landed(yt.at[rnd, pl.ds(0, 15)], rnd, YG)

        rows = [jnp.concatenate([yt[rnd, i * 4 + m] for m in range(4)], axis=1) for i in range(4)]
        lhs = stacked(jnp.concatenate(rows, axis=0))
        for n, (lo, size) in enumerate(HALVES):
            span = pl.ds(lo, size)
            part = folded(jnp.dot(lhs, a[:, lo : lo + size], preferred_element_type=F32))
            for i in range(8):
                ms[rnd, i, :, lo : lo + size] = part[i * 8 : i * 8 + 8]
            for z2, h2 in zh_peers:
                send(
                    ms.at[rnd, h2 * 4 + z2, :, span], mrs.at[rnd, mine_hz, :, span], rnd, MR[n], dev(z2, x, h2, y, c)
                )
        mrs[rnd, mine_hz] = ms[rnd, mine_hz]

        @pl.when(rnd > 0)
        def _():
            factor_blocks(9, 14)

        for n, (lo, size) in enumerate(HALVES):
            span = pl.ds(lo, size)
            landed(mrs.at[rnd, pl.ds(0, 7), :, span], rnd, MR[n])
            got = [mrs[rnd, i, :, lo : lo + size] for i in range(8)]
            mraw[rnd, c, mine_hz, :, lo : lo + size] = ((got[0] + got[1]) + (got[2] + got[3])) + (
                (got[4] + got[5]) + (got[6] + got[7])
            )
            for z2, h2 in zh_peers:
                piece = mraw.at[rnd, c, mine_hz, :, span]
                send(piece, piece, rnd, MG[n], dev(z2, x, h2, y, c))

        @pl.when(rnd > 0)
        def _():
            factor_blocks(14, 16)

        for n, (lo, size) in enumerate(HALVES):
            landed(mraw.at[rnd, c, pl.ds(0, 7), :, pl.ds(lo, size)], rnd, MG[n])
        send(mraw.at[rnd, c], mraw.at[rnd, c], rnd, MC, partner)

        def all_columns():
            landed(mraw.at[rnd, o], rnd, MC)
            for cc in range(2):
                for i in range(8):
                    r0 = (i // 2) * 32 + cc * 16 + (i % 2) * 8
                    mfull[r0 : r0 + 8, :] = mraw[rnd, cc, i]

        @pl.when(rnd == 0)
        def _():
            for i in range(8):
                xl[i * 8 : i * 8 + 8, :] = mraw[rnd, c, i]

        @pl.when(rnd > 0)
        def _():
            all_columns()
            mt[rnd] = jnp.dot(work[:, RANK:], mfull[...], precision=HIGHEST, preferred_element_type=F32)
            for i in range(4):
                xl[i * 16 : i * 16 + 16, :] = mt[rnd, pl.ds(pl.multiple_of(i * 32 + c * 16, 16), 16), :]

        lhs = stacked(xl[...])
        for k in (2, 1, 3, 0):
            y2 = (y + k) % 4
            rows = a[pl.ds(pl.multiple_of(y2 * 256, 256), 256), :]
            part = folded(lax.dot_general(lhs, rows, NT, preferred_element_type=F32))
            for i in range(4):
                xs[rnd, i * 4 + y2] = part[i * 16 : i * 16 + 16]
            for x2 in x_peers + ([x] if k else []):
                send(xs.at[rnd, x2 * 4 + y2], xrs.at[rnd, mine_xy], rnd, XR, dev(z, x2, h, y2, c))
        xrs[rnd, mine_xy] = xs[rnd, mine_xy]

        @pl.when(rnd == 0)
        def _():
            all_columns()
            mt[rnd] = mfull[...]

        gown[rnd] = lax.dot_general(
            mt[rnd, pl.ds(pl.multiple_of((c * 4 + z) * 16, 16), 16), :],
            mt[rnd], NT, precision=HIGHEST, preferred_element_type=F32,
        )
        for y2 in y_peers:
            send(gown.at[rnd], gys.at[rnd, y], rnd, GY, dev(z, x, h, y2, c))
        gys[rnd, y] = gown[rnd]
        landed(xrs.at[rnd, pl.ds(0, 15)], rnd, XR)
        total = xrs[rnd, 0]
        for i in range(1, 16):
            total = total + xrs[rnd, i]
        xt[rnd, mine_cy] = total
        for y2, c2 in yc_peers:
            piece = xt.at[rnd, mine_cy]
            send(piece, piece, rnd, XG, dev(z, x, h, y2, c2))
        landed(gys.at[rnd, pl.ds(0, 3)], rnd, GY)
        gsum[rnd] = (gys[rnd, 0] + gys[rnd, 1]) + (gys[rnd, 2] + gys[rnd, 3])
        for x2 in x_peers:
            send(gsum.at[rnd], gxs.at[rnd, x], rnd, GX, dev(z, x2, h, y, c))
        gxs[rnd, x] = gsum[rnd]

        landed(xt.at[rnd, pl.ds(0, 7)], rnd, XG)

        rows = [jnp.concatenate([xt[rnd, i * 4 + m] for m in range(4)], axis=1) for i in range(2)]
        lhs = stacked(jnp.concatenate(rows, axis=0))
        for n, (lo, size) in enumerate(PARTS):
            part = folded(jnp.dot(lhs, b[:, lo : lo + size], preferred_element_type=F32))
            ps[rnd, :, :, lo : lo + size] = part.reshape(4, 8, size)
            for z2 in z_peers:
                span = pl.ds(lo, size)
                send(ps.at[rnd, z2, :, span], prs.at[rnd, z, :, span], rnd, PR[n], dev(z2, x, h, y, c))
            if n == 0:
                landed(gxs.at[rnd, pl.ds(0, 3)], rnd, GX)
                gfull[rnd, c, z] = (gxs[rnd, 0] + gxs[rnd, 1]) + (gxs[rnd, 2] + gxs[rnd, 3])
                for z2 in z_peers:
                    piece = gfull.at[rnd, c, z]
                    send(piece, piece, rnd, GZ, dev(z2, x, h, y, c))
        prs[rnd, z] = ps[rnd, z]

        @pl.when(rnd == ROUNDS - 1)
        def _():
            for y2 in y_peers:
                send(
                    mt.at[rnd, :, pl.ds(pl.multiple_of(c * 256, 256), 256)],
                    mg.at[y, c],
                    0, PHASES,
                    dev(z, x, h, y2, c),
                )

        @pl.when(rnd == ROUNDS - 1)
        def _():
            share_gram(rnd)
            landed(gfull.at[rnd, o], rnd, GC)
            factor_start(rnd)

        for n, (lo, size) in enumerate(PARTS):
            span = pl.ds(lo, size)
            landed(prs.at[rnd, pl.ds(0, 3), :, span], rnd, PR[n])
            got = [prs[rnd, i, :, lo : lo + size] for i in range(4)]
            pt[rnd + 1, z, :, lo : lo + size] = (got[0] + got[1]) + (got[2] + got[3])
            for z2 in z_peers:
                piece = pt.at[rnd + 1, z, :, span]
                send(piece, piece, rnd, PG[n] + z, dev(z2, x, h, y, c))

            @pl.when(rnd == ROUNDS - 1)
            def _():
                to_row(z, n)
                factor_blocks(n * 6 // len(PARTS), (n + 1) * 6 // len(PARTS))


        @pl.when(rnd < ROUNDS - 1)
        def _():
            share_gram(rnd)

            def ready(n):
                for z2 in z_peers:
                    gathered_p(rnd, n, z2)

            tokens_part(rnd + 1, ready)

        return carry

    lax.fori_loop(0, ROUNDS, one_round, 0)

    last = ROUNDS - 1
    done = 6
    for n in range(len(PARTS)):
        for k in (1, 3, 2):
            z2 = (z + k) % 4
            gathered_p(last, n, z2)
            to_row(z2, n)
        if n < len(PARTS) - 1:
            factor_blocks(done, done + 1)
            done += 1
    landed(mg.at[pl.ds(0, 3), 0], 0, PHASES)
    for y2 in y_peers:
        piece = mg.at[y2, c]
        send(piece, piece, 1, PHASES, partner)
    for cc in range(2):
        mg[y, cc] = mt[last, :, cc * 256 : cc * 256 + 256]
    cf[x] = pt[ROUNDS]
    factor_blocks(done, 16)
    final = work[:, RANK:]
    scaled = final * math.sqrt(D)
    landed(mg.at[pl.ds(0, 3), 0], 1, PHASES)
    for i in range(4):
        for cc in range(2):
            r0 = i * FEAT + cc * 256
            basis_ref[r0 : r0 + 256, :] = lax.dot_general(
                mg[i, cc].T, scaled, NT, precision=HIGHEST, preferred_element_type=F32
            )
    for n, (lo, size) in enumerate(PARTS):
        landed(cf.at[pl.ds(0, 3), :, :, pl.ds(lo, size)], 2, PHASES + 1 + n)
        coef_ref[:, lo : lo + size] = jnp.dot(
            final, cf[:, :, :, lo : lo + size].reshape(RANK, size), precision=HIGHEST, preferred_element_type=F32
        )

    def drain(rnd, carry):
        left(yrs.at[rnd, pl.ds(0, 7)], rnd, YR)
        left(yt.at[rnd, pl.ds(0, 15)], rnd, YG)
        for n, (lo, size) in enumerate(HALVES):
            span = pl.ds(lo, size)
            left(mrs.at[rnd, pl.ds(0, 7), :, span], rnd, MR[n])
            left(mraw.at[rnd, 0, pl.ds(0, 7), :, span], rnd, MG[n])
        left(mraw.at[rnd, 0], rnd, MC)
        left(xrs.at[rnd, pl.ds(0, 15)], rnd, XR)
        left(xt.at[rnd, pl.ds(0, 7)], rnd, XG)
        for n, (lo, size) in enumerate(PARTS):
            span = pl.ds(lo, size)
            left(prs.at[rnd, pl.ds(0, 3), :, span], rnd, PR[n])
            left(pt.at[rnd, pl.ds(0, 3), :, span], rnd, PG[n] + z)
        left(gys.at[rnd, pl.ds(0, 3)], rnd, GY)
        left(gxs.at[rnd, pl.ds(0, 3)], rnd, GX)
        left(gfull.at[rnd, 0, pl.ds(0, 3)], rnd, GZ)
        left(gfull.at[rnd, 0], rnd, GC)
        return carry

    lax.fori_loop(0, ROUNDS, drain, 0)
    left(mg.at[pl.ds(0, 3), 0], 0, PHASES)
    left(mg.at[pl.ds(0, 3), 0], 1, PHASES)
    for n, (lo, size) in enumerate(PARTS):
        left(cf.at[pl.ds(0, 3), :, :, pl.ds(lo, size)], 2, PHASES + 1 + n)


def hand_over(basis_in, coef_in, basis_out, coef_out, sem):
    copies = [
        pltpu.make_async_copy(basis_in, basis_out, sem.at[0]),
        pltpu.make_async_copy(coef_in, coef_out, sem.at[1]),
    ]
    for copy in copies:
        copy.start()
    for copy in copies:
        copy.wait()


def body(activations, grad_out, sketch):
    anywhere = pl.BlockSpec(memory_space=pl.ANY)
    inside = pl.BlockSpec(memory_space=pltpu.VMEM)
    vm = pltpu.VMEM
    n = ROUNDS
    shapes = (
        jax.ShapeDtypeStruct((2048, RANK), F32),
        jax.ShapeDtypeStruct((RANK, HID), F32),
    )
    found = pl.pallas_call(
        kernel,
        name="range_finder",
        out_shape=shapes,
        in_specs=[anywhere] * 3,
        out_specs=(inside, inside),
        scratch_shapes=[
            vm((TOK, FEAT), BF16),
            vm((TOK, HID), BF16),
            vm((HID, RANK), F32),
            vm((RANK, HID), F32),
            vm((n + 1, 4, 8, HID), F32),
            vm((4, 32, 256), F32),
            vm((n, 8, 16, 256), F32),
            vm((n, 8, 16, 256), F32),
            vm((n, 16, 16, 256), F32),
            vm((n, 8, 8, FEAT), F32),
            vm((n, 8, 8, FEAT), F32),
            vm((n, 2, 8, 8, FEAT), F32),
            vm((RANK, FEAT), F32),
            vm((n, RANK, FEAT), F32),
            vm((64, FEAT), F32),
            vm((n, 16, 16, 256), F32),
            vm((n, 16, 16, 256), F32),
            vm((n, 8, 16, 256), F32),
            vm((n, 4, 8, HID), F32),
            vm((n, 4, 8, HID), F32),
            vm((n, 16, RANK), F32),
            vm((n, 4, 16, RANK), F32),
            vm((n, 16, RANK), F32),
            vm((n, 4, 16, RANK), F32),
            vm((n, 2, 4, 16, RANK), F32),
            vm((RANK, 2 * RANK), F32),
            vm((4, 4, 8, HID), F32),
            vm((4, 2, RANK, 256), F32),
            pltpu.SemaphoreType.DMA((2 + len(PARTS),)),
            pltpu.SemaphoreType.DMA((n, PHASES + 1 + len(PARTS))),
            pltpu.SemaphoreType.DMA((n, PHASES + 1 + len(PARTS))),
        ],
        compiler_params=pltpu.CompilerParams(
            collective_id=0, has_side_effects=True, vmem_limit_bytes=50 * 2**20
        ),
    )(activations, grad_out, pltpu.with_memory_space_constraint(sketch, pltpu.HBM))
    return pl.pallas_call(
        hand_over,
        name="hand_over",
        out_shape=shapes,
        in_specs=[anywhere] * 2,
        out_specs=(anywhere, anywhere),
        scratch_shapes=[pltpu.SemaphoreType.DMA((2,))],
        cost_estimate=pl.CostEstimate(flops=0, bytes_accessed=4 * 2**20, transcendentals=0),
    )(*found)


def solution(mesh):
    in_specs = (P("dp", "row"), P("dp", "col"), P("col", None))
    out_specs = (P("row", None), P(None, "col"))
    return jax.shard_map(body, mesh=mesh, in_specs=in_specs, out_specs=out_specs, check_vma=False)
```

```python
import functools
import math

import jax
import jax.numpy as jnp
from jax import lax
from jax.experimental import pallas as pl
from jax.experimental.pallas import tpu as pltpu
from jax.sharding import PartitionSpec as P

MESH = pl.DeviceIdType.MESH
F32 = jnp.float32
BF16 = jnp.bfloat16
HIGHEST = lax.Precision.HIGHEST
D = 8192
RANK = 128
ROUNDS = 3
TOK = 1024
HID = 1664
FEAT = 512
NT = (((1,), (1,)), ((), ()))
TN = (((0,), (0,)), ((), ()))
PARTS = ((0, 256), (256, 384), (640, 384), (1024, 384), (1408, 256))
HALVES = ((0, 256), (256, 256))
YR, YG, MC, XR, XG, GY, GX, GZ, GC = range(9)
MR = range(9, 9 + len(HALVES))
MG = range(MR.stop, MR.stop + len(HALVES))
PR = range(MG.stop, MG.stop + len(PARTS))
PG = range(PR.stop, PR.stop + 4 * len(PARTS), 4)
PHASES = PG.stop
XY = (
    (2, 2), (2, 1), (2, 3), (1, 2), (3, 2), (1, 1), (1, 3), (3, 1), (3, 3),
    (2, 0), (0, 2), (1, 0), (3, 0), (0, 1), (0, 3),
)
ZH = ((2, 1), (1, 1), (3, 1), (0, 1), (2, 0), (1, 0), (3, 0))


def stacked(mat):
    high = mat.astype(BF16)
    rest = mat - high.astype(F32)
    mid = rest.astype(BF16)
    low = (rest - mid.astype(F32)).astype(BF16)
    return jnp.concatenate([high, mid, low], axis=0)


def outer(left, right):
    def three(mat):
        high = mat.astype(BF16).astype(F32)
        mid = (mat - high).astype(BF16).astype(F32)
        return high, mid, (mat - high - mid).astype(BF16).astype(F32)

    lh, lm, ll = three(left)
    rh, rm, rl = three(right)
    return lax.dot_general(
        jnp.concatenate([lh, lh, lm, lh, ll, lm], axis=0).astype(BF16),
        jnp.concatenate([rh, rm, rh, rl, rh, rm], axis=0).astype(BF16),
        TN, preferred_element_type=F32,
    )


def folded(wide):
    rows = wide.shape[0] // 3
    return wide[:rows] + (wide[rows : 2 * rows] + wide[2 * rows :])


def kernel(
    a_hbm, b_hbm, s_hbm, basis_ref, coef_ref,
    a, b, s, st, pt, yacc, ysend, yrs, yt, ms, mrs, mraw, mfull, mt, xl, xs, xrs, xt,
    ps, prs, gown, gys, gsum, gxs, gfull, work, cf, mg,
    load_sem, send_sem, recv_sem,
):
    z, x, j = lax.axis_index("dp"), lax.axis_index("row"), lax.axis_index("col")
    c = j % 2
    y = (j // 2) % 4
    h = j // 8
    o = 1 - c
    mine_xy = x * 4 + y
    mine_hz = h * 4 + z
    mine_cy = c * 4 + y

    def dev(z_, x_, h_, y_, c_):
        return (z_, x_, (h_ * 4 + y_) * 2 + c_)

    partner = dev(z, x, h, y, o)
    xy_peers = [((x + dx) % 4, (y + dy) % 4) for dx, dy in XY]
    zh_peers = [((z + dz) % 4, (h + dh) % 2) for dz, dh in ZH]
    z_peers = [(z + k) % 4 for k in (2, 1, 3)]
    y_peers = [(y + k) % 4 for k in (2, 1, 3)]
    yc_peers = [((y + k) % 4, c2) for k in (2, 1, 3) for c2 in (c, o)] + [(y, o)]
    x_peers = [(x + k) % 4 for k in (2, 1, 3)]

    barrier = pltpu.get_barrier_semaphore()

    def greet(device):
        pl.semaphore_signal(barrier, inc=1, device_id=device, device_id_type=MESH)

    loads = [
        pltpu.make_async_copy(s_hbm, s, load_sem.at[0]),
    ]
    for n, (lo, size) in enumerate(PARTS):
        span = pl.ds(lo, size)
        loads.append(pltpu.make_async_copy(b_hbm.at[:, span], b.at[:, span], load_sem.at[1 + n]))
    loads.append(
        pltpu.make_async_copy(
            a_hbm.at[:, pl.ds(pl.multiple_of(y * FEAT, FEAT), FEAT)], a, load_sem.at[1 + len(PARTS)]
        )
    )
    for load in loads:
        load.start()

    for (x2, y2), (dx, _) in zip(xy_peers, XY):
        if dx:
            greet(dev(z, x2, h, y2, c))
    for z2, h2 in zh_peers:
        greet(dev(z2, x, h2, y, c))
    for y2, c2 in yc_peers:
        greet(dev(z, x, h, y2, c2))

    def send(src, dst, rnd, phase, device):
        pltpu.make_async_remote_copy(
            src_ref=src,
            dst_ref=dst,
            send_sem=send_sem.at[rnd, phase],
            recv_sem=recv_sem.at[rnd, phase],
            device_id=device,
            device_id_type=MESH,
        ).start()

    def landed(like, rnd, phase):
        pltpu.make_async_copy(like, like, recv_sem.at[rnd, phase]).wait()

    def left(like, rnd, phase):
        pltpu.make_async_copy(like, like, send_sem.at[rnd, phase]).wait()

    row_iota = lax.broadcasted_iota(jnp.int32, (RANK, RANK), 0)
    col_iota = lax.broadcasted_iota(jnp.int32, (RANK, RANK), 1)
    eye = jnp.where(row_iota == col_iota, 1.0, 0.0).astype(F32)

    def factor_start(rnd):
        work[:, :RANK] = gfull[rnd].reshape(RANK, RANK)
        work[:, RANK:] = eye

    sub = lax.broadcasted_iota(jnp.int32, (8, RANK), 0)
    lane = lax.broadcasted_iota(jnp.int32, (8, RANK), 1)

    def spread(row):
        return jnp.broadcast_to(row, (8, RANK))

    def factor_block(blk, carry):
        r0 = pl.multiple_of(blk * 8, 8)
        gp = work[pl.ds(r0, 8), :RANK]
        ep = work[pl.ds(r0, 8), RANK:]
        diag = pltpu.roll(gp, RANK - r0, 1)
        cols = [jnp.broadcast_to(diag[:, i : i + 1], (8, RANK)) for i in range(8)]
        inv = [jnp.where(sub == i, 1.0, 0.0).astype(F32) for i in range(8)]
        pivots = jnp.ones((8, RANK), F32)
        for i in range(8):
            pivot = spread(cols[i][i : i + 1])
            pivots = jnp.where(sub == i, pivot, pivots)
            if i == 7:
                break
            scale = jnp.where(sub > i, cols[i] * (1.0 / pivot), 0.0)
            for m in range(i + 1, 8):
                cols[m] = cols[m] - scale * spread(cols[m][i : i + 1])
            for m in range(i + 1):
                inv[m] = inv[m] - scale * spread(inv[m][i : i + 1])
        root = lax.rsqrt(pivots)
        root = root * (1.5 - 0.5 * pivots * root * root)
        ug = jnp.zeros((8, RANK), F32)
        ue = jnp.zeros((8, RANK), F32)
        for m in range(8):
            weight = inv[m] * root
            ug = ug + weight * spread(gp[m : m + 1])
            ue = ue + weight * spread(ep[m : m + 1])
        work[pl.ds(r0, 8), RANK:] = ue
        rest = jnp.where(lane >= r0 + 8, ug, 0.0)
        work[...] -= outer(rest, jnp.concatenate([ug, ue], axis=1))
        return carry

    def factor_blocks(lo, hi):
        lax.fori_loop(lo, hi, factor_block, 0)

    def tokens_part(rnd, ready):
        for n, (lo, size) in enumerate(PARTS):
            ready(n)
            lhs = stacked(pt[rnd, :, :, lo : lo + size].reshape(32, size))
            if n < len(PARTS) - 1:
                part = folded(lax.dot_general(lhs, b[:, lo : lo + size], NT, preferred_element_type=F32))
                for m in range(4):
                    quarter = part[:, m * 256 : m * 256 + 256]
                    yacc[m] = yacc[m] + quarter if n else quarter
        for k in (2, 1, 3, 0):
            y2 = (y + k) % 4
            rows = b[pl.ds(pl.multiple_of(y2 * 256, 256), 256), lo : lo + size]
            quarter = folded(lax.dot_general(lhs, rows, NT, preferred_element_type=F32))
            if len(PARTS) > 1:
                quarter = yacc[y2] + quarter
            ysend[rnd, y2] = quarter[:16]
            ysend[rnd, 4 + y2] = quarter[16:]
            for c2 in (c, o) if k else (o,):
                send(ysend.at[rnd, c2 * 4 + y2], yrs.at[rnd, mine_cy], rnd, YR, dev(z, x, h, y2, c2))

    loads[0].wait()
    st[...] = s[...].T
    pt[0] = st[pl.ds(pl.multiple_of(x * 32, 32), 32), :].reshape(4, 8, HID)

    def begin(n):
        loads[1 + n].wait()
        if n == len(PARTS) - 1:
            pl.semaphore_wait(barrier, 26)

    tokens_part(0, begin)
    loads[-1].wait()

    def to_row(z2, n):
        span = pl.ds(*PARTS[n])
        for x2 in x_peers:
            send(pt.at[ROUNDS, z2, :, span], cf.at[x, z2, :, span], 2, PHASES + 1 + n, dev(z, x2, h, y, c))

    def gathered_p(rnd, n, z2):
        lo, size = PARTS[n]
        landed(pt.at[rnd + 1, z2, :, pl.ds(lo, size)], rnd, PG[n] + z2)

    def share_gram(rnd):
        landed(gfull.at[rnd, c, pl.ds(0, 3)], rnd, GZ)
        send(gfull.at[rnd, c], gfull.at[rnd, c], rnd, GC, partner)

    def one_round(rnd, carry):
        yrs[rnd, mine_cy] = ysend[rnd, mine_cy]

        @pl.when(rnd > 0)
        def _():
            landed(gfull.at[rnd - 1, o], rnd - 1, GC)
            factor_start(rnd - 1)
            factor_blocks(0, 4)

        landed(yrs.at[rnd, pl.ds(0, 7)], rnd, YR)
        got = [yrs[rnd, i] for i in range(8)]
        yt[rnd, mine_xy] = ((got[0] + got[1]) + (got[2] + got[3])) + ((got[4] + got[5]) + (got[6] + got[7]))
        for x2, y2 in xy_peers:
            piece = yt.at[rnd, mine_xy]
            send(piece, piece, rnd, YG, dev(z, x2, h, y2, c))

        @pl.when(rnd > 0)
        def _():
            factor_blocks(4, 9)

        landed(yt.at[rnd, pl.ds(0, 15)], rnd, YG)

        rows = [jnp.concatenate([yt[rnd, i * 4 + m] for m in range(4)], axis=1) for i in range(4)]
        lhs = stacked(jnp.concatenate(rows, axis=0))
        for n, (lo, size) in enumerate(HALVES):
            span = pl.ds(lo, size)
            part = folded(jnp.dot(lhs, a[:, lo : lo + size], preferred_element_type=F32))
            for i in range(8):
                ms[rnd, i, :, lo : lo + size] = part[i * 8 : i * 8 + 8]
            for z2, h2 in zh_peers:
                send(
                    ms.at[rnd, h2 * 4 + z2, :, span], mrs.at[rnd, mine_hz, :, span], rnd, MR[n], dev(z2, x, h2, y, c)
                )
        mrs[rnd, mine_hz] = ms[rnd, mine_hz]

        @pl.when(rnd > 0)
        def _():
            factor_blocks(9, 14)

        for n, (lo, size) in enumerate(HALVES):
            span = pl.ds(lo, size)
            landed(mrs.at[rnd, pl.ds(0, 7), :, span], rnd, MR[n])
            got = [mrs[rnd, i, :, lo : lo + size] for i in range(8)]
            mraw[rnd, c, mine_hz, :, lo : lo + size] = ((got[0] + got[1]) + (got[2] + got[3])) + (
                (got[4] + got[5]) + (got[6] + got[7])
            )
            for z2, h2 in zh_peers:
                piece = mraw.at[rnd, c, mine_hz, :, span]
                send(piece, piece, rnd, MG[n], dev(z2, x, h2, y, c))

        @pl.when(rnd > 0)
        def _():
            factor_blocks(14, 16)

        for n, (lo, size) in enumerate(HALVES):
            landed(mraw.at[rnd, c, pl.ds(0, 7), :, pl.ds(lo, size)], rnd, MG[n])
        send(mraw.at[rnd, c], mraw.at[rnd, c], rnd, MC, partner)

        def all_columns():
            landed(mraw.at[rnd, o], rnd, MC)
            for cc in range(2):
                for i in range(8):
                    r0 = (i // 2) * 32 + cc * 16 + (i % 2) * 8
                    mfull[r0 : r0 + 8, :] = mraw[rnd, cc, i]

        @pl.when(rnd == 0)
        def _():
            for i in range(8):
                xl[i * 8 : i * 8 + 8, :] = mraw[rnd, c, i]

        @pl.when(rnd > 0)
        def _():
            all_columns()
            mt[rnd] = jnp.dot(work[:, RANK:], mfull[...], precision=HIGHEST, preferred_element_type=F32)
            for i in range(4):
                xl[i * 16 : i * 16 + 16, :] = mt[rnd, pl.ds(pl.multiple_of(i * 32 + c * 16, 16), 16), :]

        lhs = stacked(xl[...])
        for k in (2, 1, 3, 0):
            y2 = (y + k) % 4
            rows = a[pl.ds(pl.multiple_of(y2 * 256, 256), 256), :]
            part = folded(lax.dot_general(lhs, rows, NT, preferred_element_type=F32))
            for i in range(4):
                xs[rnd, i * 4 + y2] = part[i * 16 : i * 16 + 16]
            for x2 in x_peers + ([x] if k else []):
                send(xs.at[rnd, x2 * 4 + y2], xrs.at[rnd, mine_xy], rnd, XR, dev(z, x2, h, y2, c))
        xrs[rnd, mine_xy] = xs[rnd, mine_xy]

        @pl.when(rnd == 0)
        def _():
            all_columns()
            mt[rnd] = mfull[...]

        gown[rnd] = lax.dot_general(
            mt[rnd, pl.ds(pl.multiple_of((c * 4 + z) * 16, 16), 16), :],
            mt[rnd], NT, precision=HIGHEST, preferred_element_type=F32,
        )
        for y2 in y_peers:
            send(gown.at[rnd], gys.at[rnd, y], rnd, GY, dev(z, x, h, y2, c))
        gys[rnd, y] = gown[rnd]
        landed(xrs.at[rnd, pl.ds(0, 15)], rnd, XR)
        total = xrs[rnd, 0]
        for i in range(1, 16):
            total = total + xrs[rnd, i]
        xt[rnd, mine_cy] = total
        for y2, c2 in yc_peers:
            piece = xt.at[rnd, mine_cy]
            send(piece, piece, rnd, XG, dev(z, x, h, y2, c2))
        landed(gys.at[rnd, pl.ds(0, 3)], rnd, GY)
        gsum[rnd] = (gys[rnd, 0] + gys[rnd, 1]) + (gys[rnd, 2] + gys[rnd, 3])
        for x2 in x_peers:
            send(gsum.at[rnd], gxs.at[rnd, x], rnd, GX, dev(z, x2, h, y, c))
        gxs[rnd, x] = gsum[rnd]

        landed(xt.at[rnd, pl.ds(0, 7)], rnd, XG)

        rows = [jnp.concatenate([xt[rnd, i * 4 + m] for m in range(4)], axis=1) for i in range(2)]
        lhs = stacked(jnp.concatenate(rows, axis=0))
        for n, (lo, size) in enumerate(PARTS):
            part = folded(jnp.dot(lhs, b[:, lo : lo + size], preferred_element_type=F32))
            ps[rnd, :, :, lo : lo + size] = part.reshape(4, 8, size)
            for z2 in z_peers:
                span = pl.ds(lo, size)
                send(ps.at[rnd, z2, :, span], prs.at[rnd, z, :, span], rnd, PR[n], dev(z2, x, h, y, c))
            if n == 0:
                landed(gxs.at[rnd, pl.ds(0, 3)], rnd, GX)
                gfull[rnd, c, z] = (gxs[rnd, 0] + gxs[rnd, 1]) + (gxs[rnd, 2] + gxs[rnd, 3])
                for z2 in z_peers:
                    piece = gfull.at[rnd, c, z]
                    send(piece, piece, rnd, GZ, dev(z2, x, h, y, c))
        prs[rnd, z] = ps[rnd, z]

        @pl.when(rnd == ROUNDS - 1)
        def _():
            for y2 in y_peers:
                send(
                    mt.at[rnd, :, pl.ds(pl.multiple_of(c * 256, 256), 256)],
                    mg.at[y, c],
                    0, PHASES,
                    dev(z, x, h, y2, c),
                )

        @pl.when(rnd == ROUNDS - 1)
        def _():
            share_gram(rnd)
            landed(gfull.at[rnd, o], rnd, GC)
            factor_start(rnd)

        for n, (lo, size) in enumerate(PARTS):
            span = pl.ds(lo, size)
            landed(prs.at[rnd, pl.ds(0, 3), :, span], rnd, PR[n])
            got = [prs[rnd, i, :, lo : lo + size] for i in range(4)]
            pt[rnd + 1, z, :, lo : lo + size] = (got[0] + got[1]) + (got[2] + got[3])
            for z2 in z_peers:
                piece = pt.at[rnd + 1, z, :, span]
                send(piece, piece, rnd, PG[n] + z, dev(z2, x, h, y, c))

            @pl.when(rnd == ROUNDS - 1)
            def _():
                to_row(z, n)
                factor_blocks(n * 6 // len(PARTS), (n + 1) * 6 // len(PARTS))


        @pl.when(rnd < ROUNDS - 1)
        def _():
            share_gram(rnd)

            def ready(n):
                for z2 in z_peers:
                    gathered_p(rnd, n, z2)

            tokens_part(rnd + 1, ready)

        return carry

    lax.fori_loop(0, ROUNDS, one_round, 0)

    last = ROUNDS - 1
    done = 6
    for n in range(len(PARTS)):
        for k in (1, 3, 2):
            z2 = (z + k) % 4
            gathered_p(last, n, z2)
            to_row(z2, n)
        if n < len(PARTS) - 1:
            factor_blocks(done, done + 1)
            done += 1
    landed(mg.at[pl.ds(0, 3), 0], 0, PHASES)
    for y2 in y_peers:
        piece = mg.at[y2, c]
        send(piece, piece, 1, PHASES, partner)
    for cc in range(2):
        mg[y, cc] = mt[last, :, cc * 256 : cc * 256 + 256]
    cf[x] = pt[ROUNDS]
    factor_blocks(done, 16)
    final = work[:, RANK:]
    scaled = final * math.sqrt(D)
    landed(mg.at[pl.ds(0, 3), 0], 1, PHASES)
    for i in range(4):
        for cc in range(2):
            r0 = i * FEAT + cc * 256
            basis_ref[r0 : r0 + 256, :] = lax.dot_general(
                mg[i, cc].T, scaled, NT, precision=HIGHEST, preferred_element_type=F32
            )
    for n, (lo, size) in enumerate(PARTS):
        landed(cf.at[pl.ds(0, 3), :, :, pl.ds(lo, size)], 2, PHASES + 1 + n)
        coef_ref[:, lo : lo + size] = jnp.dot(
            final, cf[:, :, :, lo : lo + size].reshape(RANK, size), precision=HIGHEST, preferred_element_type=F32
        )

    def drain(rnd, carry):
        left(yrs.at[rnd, pl.ds(0, 7)], rnd, YR)
        left(yt.at[rnd, pl.ds(0, 15)], rnd, YG)
        for n, (lo, size) in enumerate(HALVES):
            span = pl.ds(lo, size)
            left(mrs.at[rnd, pl.ds(0, 7), :, span], rnd, MR[n])
            left(mraw.at[rnd, 0, pl.ds(0, 7), :, span], rnd, MG[n])
        left(mraw.at[rnd, 0], rnd, MC)
        left(xrs.at[rnd, pl.ds(0, 15)], rnd, XR)
        left(xt.at[rnd, pl.ds(0, 7)], rnd, XG)
        for n, (lo, size) in enumerate(PARTS):
            span = pl.ds(lo, size)
            left(prs.at[rnd, pl.ds(0, 3), :, span], rnd, PR[n])
            left(pt.at[rnd, pl.ds(0, 3), :, span], rnd, PG[n] + z)
        left(gys.at[rnd, pl.ds(0, 3)], rnd, GY)
        left(gxs.at[rnd, pl.ds(0, 3)], rnd, GX)
        left(gfull.at[rnd, 0, pl.ds(0, 3)], rnd, GZ)
        left(gfull.at[rnd, 0], rnd, GC)
        return carry

    lax.fori_loop(0, ROUNDS, drain, 0)
    left(mg.at[pl.ds(0, 3), 0], 0, PHASES)
    left(mg.at[pl.ds(0, 3), 0], 1, PHASES)
    for n, (lo, size) in enumerate(PARTS):
        left(cf.at[pl.ds(0, 3), :, :, pl.ds(lo, size)], 2, PHASES + 1 + n)


def hand_over(basis_in, coef_in, basis_out, coef_out):
    basis_out[...] = basis_in[...]
    coef_out[...] = coef_in[...]


def body(activations, grad_out, sketch):
    anywhere = pl.BlockSpec(memory_space=pl.ANY)
    inside = pl.BlockSpec(memory_space=pltpu.VMEM)
    vm = pltpu.VMEM
    n = ROUNDS
    shapes = (
        jax.ShapeDtypeStruct((2048, RANK), F32),
        jax.ShapeDtypeStruct((RANK, HID), F32),
    )
    found = pl.pallas_call(
        kernel,
        name="range_finder",
        out_shape=shapes,
        in_specs=[anywhere] * 3,
        out_specs=(inside, inside),
        scratch_shapes=[
            vm((TOK, FEAT), BF16),
            vm((TOK, HID), BF16),
            vm((HID, RANK), F32),
            vm((RANK, HID), F32),
            vm((n + 1, 4, 8, HID), F32),
            vm((4, 32, 256), F32),
            vm((n, 8, 16, 256), F32),
            vm((n, 8, 16, 256), F32),
            vm((n, 16, 16, 256), F32),
            vm((n, 8, 8, FEAT), F32),
            vm((n, 8, 8, FEAT), F32),
            vm((n, 2, 8, 8, FEAT), F32),
            vm((RANK, FEAT), F32),
            vm((n, RANK, FEAT), F32),
            vm((64, FEAT), F32),
            vm((n, 16, 16, 256), F32),
            vm((n, 16, 16, 256), F32),
            vm((n, 8, 16, 256), F32),
            vm((n, 4, 8, HID), F32),
            vm((n, 4, 8, HID), F32),
            vm((n, 16, RANK), F32),
            vm((n, 4, 16, RANK), F32),
            vm((n, 16, RANK), F32),
            vm((n, 4, 16, RANK), F32),
            vm((n, 2, 4, 16, RANK), F32),
            vm((RANK, 2 * RANK), F32),
            vm((4, 4, 8, HID), F32),
            vm((4, 2, RANK, 256), F32),
            pltpu.SemaphoreType.DMA((2 + len(PARTS),)),
            pltpu.SemaphoreType.DMA((n, PHASES + 1 + len(PARTS))),
            pltpu.SemaphoreType.DMA((n, PHASES + 1 + len(PARTS))),
        ],
        compiler_params=pltpu.CompilerParams(
            collective_id=0, has_side_effects=True, vmem_limit_bytes=50 * 2**20
        ),
    )(activations, grad_out, pltpu.with_memory_space_constraint(sketch, pltpu.HBM))
    return pl.pallas_call(
        hand_over,
        name="hand_over",
        out_shape=shapes,
        in_specs=[inside] * 2,
        out_specs=(inside, inside),
        compiler_params=pltpu.CompilerParams(vmem_limit_bytes=8 * 2**20),
        cost_estimate=pl.CostEstimate(flops=0, bytes_accessed=4 * 2**20, transcendentals=0),
    )(*found)


def solution(mesh):
    in_specs = (P("dp", "row"), P("dp", "col"), P("col", None))
    out_specs = (P("row", None), P(None, "col"))
    return jax.shard_map(body, mesh=mesh, in_specs=in_specs, out_specs=out_specs, check_vma=False)
```

```python
import functools
import math

import jax
import jax.numpy as jnp
from jax import lax
from jax.experimental import pallas as pl
from jax.experimental.pallas import tpu as pltpu
from jax.sharding import PartitionSpec as P

MESH = pl.DeviceIdType.MESH
F32 = jnp.float32
BF16 = jnp.bfloat16
HIGHEST = lax.Precision.HIGHEST
D = 8192
RANK = 128
ROUNDS = 3
TOK = 1024
HID = 1664
FEAT = 512
NT = (((1,), (1,)), ((), ()))
TN = (((0,), (0,)), ((), ()))
PARTS = ((0, 256), (256, 384), (640, 384), (1024, 384), (1408, 256))
HALVES = ((0, 256), (256, 256))
YR, YG, MC, XR, XG, GY, GX, GZ, GC = range(9)
MR = range(9, 9 + len(HALVES))
MG = range(MR.stop, MR.stop + len(HALVES))
PR = range(MG.stop, MG.stop + len(PARTS))
PG = range(PR.stop, PR.stop + 4 * len(PARTS), 4)
PHASES = PG.stop
XY = (
    (2, 2), (2, 1), (2, 3), (1, 2), (3, 2), (1, 1), (1, 3), (3, 1), (3, 3),
    (2, 0), (0, 2), (1, 0), (3, 0), (0, 1), (0, 3),
)
ZH = ((2, 1), (1, 1), (3, 1), (0, 1), (2, 0), (1, 0), (3, 0))


def stacked(mat):
    high = mat.astype(BF16)
    rest = mat - high.astype(F32)
    mid = rest.astype(BF16)
    low = (rest - mid.astype(F32)).astype(BF16)
    return jnp.concatenate([high, mid, low], axis=0)


def outer(left, right):
    def three(mat):
        high = mat.astype(BF16).astype(F32)
        mid = (mat - high).astype(BF16).astype(F32)
        return high, mid, (mat - high - mid).astype(BF16).astype(F32)

    lh, lm, ll = three(left)
    rh, rm, rl = three(right)
    return lax.dot_general(
        jnp.concatenate([lh, lh, lm, lh, ll, lm], axis=0).astype(BF16),
        jnp.concatenate([rh, rm, rh, rl, rh, rm], axis=0).astype(BF16),
        TN, preferred_element_type=F32,
    )


def folded(wide):
    rows = wide.shape[0] // 3
    return wide[:rows] + (wide[rows : 2 * rows] + wide[2 * rows :])


def kernel(
    a_hbm, b_hbm, s_hbm, basis_ref, coef_ref,
    a, b, s, st, pt, yacc, ysend, yrs, yt, ms, mrs, mraw, mfull, mt, xl, xs, xrs, xt,
    ps, prs, gown, gys, gsum, gxs, gfull, work, cf, mg,
    load_sem, send_sem, recv_sem,
):
    z, x, j = lax.axis_index("dp"), lax.axis_index("row"), lax.axis_index("col")
    c = j % 2
    y = (j // 2) % 4
    h = j // 8
    o = 1 - c
    mine_xy = x * 4 + y
    mine_hz = h * 4 + z
    mine_cy = c * 4 + y

    def dev(z_, x_, h_, y_, c_):
        return (z_, x_, (h_ * 4 + y_) * 2 + c_)

    partner = dev(z, x, h, y, o)
    xy_peers = [((x + dx) % 4, (y + dy) % 4) for dx, dy in XY]
    zh_peers = [((z + dz) % 4, (h + dh) % 2) for dz, dh in ZH]
    z_peers = [(z + k) % 4 for k in (2, 1, 3)]
    y_peers = [(y + k) % 4 for k in (2, 1, 3)]
    yc_peers = [((y + k) % 4, c2) for k in (2, 1, 3) for c2 in (c, o)] + [(y, o)]
    x_peers = [(x + k) % 4 for k in (2, 1, 3)]

    barrier = pltpu.get_barrier_semaphore()

    def greet(device):
        pl.semaphore_signal(barrier, inc=1, device_id=device, device_id_type=MESH)

    loads = [
        pltpu.make_async_copy(s_hbm, s, load_sem.at[0]),
    ]
    for n, (lo, size) in enumerate(PARTS):
        span = pl.ds(lo, size)
        loads.append(pltpu.make_async_copy(b_hbm.at[:, span], b.at[:, span], load_sem.at[1 + n]))
    loads.append(
        pltpu.make_async_copy(
            a_hbm.at[:, pl.ds(pl.multiple_of(y * FEAT, FEAT), FEAT)], a, load_sem.at[1 + len(PARTS)]
        )
    )
    for load in loads:
        load.start()

    for (x2, y2), (dx, _) in zip(xy_peers, XY):
        if dx:
            greet(dev(z, x2, h, y2, c))
    for z2, h2 in zh_peers:
        greet(dev(z2, x, h2, y, c))
    for y2, c2 in yc_peers:
        greet(dev(z, x, h, y2, c2))

    def send(src, dst, rnd, phase, device):
        pltpu.make_async_remote_copy(
            src_ref=src,
            dst_ref=dst,
            send_sem=send_sem.at[rnd, phase],
            recv_sem=recv_sem.at[rnd, phase],
            device_id=device,
            device_id_type=MESH,
        ).start()

    def landed(like, rnd, phase):
        pltpu.make_async_copy(like, like, recv_sem.at[rnd, phase]).wait()

    def left(like, rnd, phase):
        pltpu.make_async_copy(like, like, send_sem.at[rnd, phase]).wait()

    row_iota = lax.broadcasted_iota(jnp.int32, (RANK, RANK), 0)
    col_iota = lax.broadcasted_iota(jnp.int32, (RANK, RANK), 1)
    eye = jnp.where(row_iota == col_iota, 1.0, 0.0).astype(F32)

    def factor_start(rnd):
        work[:, :RANK] = gfull[rnd].reshape(RANK, RANK)
        work[:, RANK:] = eye

    sub = lax.broadcasted_iota(jnp.int32, (8, RANK), 0)
    lane = lax.broadcasted_iota(jnp.int32, (8, RANK), 1)

    def spread(row):
        return jnp.broadcast_to(row, (8, RANK))

    def factor_block(blk, carry):
        r0 = pl.multiple_of(blk * 8, 8)
        gp = work[pl.ds(r0, 8), :RANK]
        ep = work[pl.ds(r0, 8), RANK:]
        diag = pltpu.roll(gp, RANK - r0, 1)
        cols = [jnp.broadcast_to(diag[:, i : i + 1], (8, RANK)) for i in range(8)]
        inv = [jnp.where(sub == i, 1.0, 0.0).astype(F32) for i in range(8)]
        pivots = jnp.ones((8, RANK), F32)
        for i in range(8):
            pivot = spread(cols[i][i : i + 1])
            pivots = jnp.where(sub == i, pivot, pivots)
            if i == 7:
                break
            scale = jnp.where(sub > i, cols[i] * (1.0 / pivot), 0.0)
            for m in range(i + 1, 8):
                cols[m] = cols[m] - scale * spread(cols[m][i : i + 1])
            for m in range(i + 1):
                inv[m] = inv[m] - scale * spread(inv[m][i : i + 1])
        root = lax.rsqrt(pivots)
        root = root * (1.5 - 0.5 * pivots * root * root)
        ug = jnp.zeros((8, RANK), F32)
        ue = jnp.zeros((8, RANK), F32)
        for m in range(8):
            weight = inv[m] * root
            ug = ug + weight * spread(gp[m : m + 1])
            ue = ue + weight * spread(ep[m : m + 1])
        work[pl.ds(r0, 8), RANK:] = ue
        rest = jnp.where(lane >= r0 + 8, ug, 0.0)
        work[...] -= outer(rest, jnp.concatenate([ug, ue], axis=1))
        return carry

    def factor_blocks(lo, hi):
        lax.fori_loop(lo, hi, factor_block, 0)

    def tokens_part(rnd, ready):
        for n, (lo, size) in enumerate(PARTS):
            ready(n)
            lhs = stacked(pt[rnd, :, :, lo : lo + size].reshape(32, size))
            if n < len(PARTS) - 1:
                part = folded(lax.dot_general(lhs, b[:, lo : lo + size], NT, preferred_element_type=F32))
                for m in range(4):
                    quarter = part[:, m * 256 : m * 256 + 256]
                    yacc[m] = yacc[m] + quarter if n else quarter
        for k in (2, 1, 3, 0):
            y2 = (y + k) % 4
            rows = b[pl.ds(pl.multiple_of(y2 * 256, 256), 256), lo : lo + size]
            quarter = folded(lax.dot_general(lhs, rows, NT, preferred_element_type=F32))
            if len(PARTS) > 1:
                quarter = yacc[y2] + quarter
            ysend[rnd, y2] = quarter[:16]
            ysend[rnd, 4 + y2] = quarter[16:]
            for c2 in (c, o) if k else (o,):
                send(ysend.at[rnd, c2 * 4 + y2], yrs.at[rnd, mine_cy], rnd, YR, dev(z, x, h, y2, c2))

    loads[0].wait()
    st[...] = s[...].T
    pt[0] = st[pl.ds(pl.multiple_of(x * 32, 32), 32), :].reshape(4, 8, HID)

    def begin(n):
        loads[1 + n].wait()
        if n == len(PARTS) - 1:
            pl.semaphore_wait(barrier, 26)

    tokens_part(0, begin)
    loads[-1].wait()

    def to_row(z2, n):
        span = pl.ds(*PARTS[n])
        for x2 in x_peers:
            send(pt.at[ROUNDS, z2, :, span], cf.at[x, z2, :, span], 2, PHASES + 1 + n, dev(z, x2, h, y, c))

    def gathered_p(rnd, n, z2):
        lo, size = PARTS[n]
        landed(pt.at[rnd + 1, z2, :, pl.ds(lo, size)], rnd, PG[n] + z2)

    def share_gram(rnd):
        landed(gfull.at[rnd, c, pl.ds(0, 3)], rnd, GZ)
        send(gfull.at[rnd, c], gfull.at[rnd, c], rnd, GC, partner)

    def one_round(rnd, carry):
        yrs[rnd, mine_cy] = ysend[rnd, mine_cy]

        @pl.when(rnd > 0)
        def _():
            landed(gfull.at[rnd - 1, o], rnd - 1, GC)
            factor_start(rnd - 1)
            factor_blocks(0, 4)

        landed(yrs.at[rnd, pl.ds(0, 7)], rnd, YR)
        got = [yrs[rnd, i] for i in range(8)]
        yt[rnd, mine_xy] = ((got[0] + got[1]) + (got[2] + got[3])) + ((got[4] + got[5]) + (got[6] + got[7]))
        for x2, y2 in xy_peers:
            piece = yt.at[rnd, mine_xy]
            send(piece, piece, rnd, YG, dev(z, x2, h, y2, c))

        @pl.when(rnd > 0)
        def _():
            factor_blocks(4, 9)

        landed(yt.at[rnd, pl.ds(0, 15)], rnd, YG)

        rows = [jnp.concatenate([yt[rnd, i * 4 + m] for m in range(4)], axis=1) for i in range(4)]
        lhs = stacked(jnp.concatenate(rows, axis=0))
        for n, (lo, size) in enumerate(HALVES):
            span = pl.ds(lo, size)
            part = folded(jnp.dot(lhs, a[:, lo : lo + size], preferred_element_type=F32))
            for i in range(8):
                ms[rnd, i, :, lo : lo + size] = part[i * 8 : i * 8 + 8]
            for z2, h2 in zh_peers:
                send(
                    ms.at[rnd, h2 * 4 + z2, :, span], mrs.at[rnd, mine_hz, :, span], rnd, MR[n], dev(z2, x, h2, y, c)
                )
        mrs[rnd, mine_hz] = ms[rnd, mine_hz]

        @pl.when(rnd > 0)
        def _():
            factor_blocks(9, 14)

        for n, (lo, size) in enumerate(HALVES):
            span = pl.ds(lo, size)
            landed(mrs.at[rnd, pl.ds(0, 7), :, span], rnd, MR[n])
            got = [mrs[rnd, i, :, lo : lo + size] for i in range(8)]
            mraw[rnd, c, mine_hz, :, lo : lo + size] = ((got[0] + got[1]) + (got[2] + got[3])) + (
                (got[4] + got[5]) + (got[6] + got[7])
            )
            for z2, h2 in zh_peers:
                piece = mraw.at[rnd, c, mine_hz, :, span]
                send(piece, piece, rnd, MG[n], dev(z2, x, h2, y, c))

        @pl.when(rnd > 0)
        def _():
            factor_blocks(14, 16)

        for n, (lo, size) in enumerate(HALVES):
            landed(mraw.at[rnd, c, pl.ds(0, 7), :, pl.ds(lo, size)], rnd, MG[n])
        send(mraw.at[rnd, c], mraw.at[rnd, c], rnd, MC, partner)

        def all_columns():
            landed(mraw.at[rnd, o], rnd, MC)
            for cc in range(2):
                for i in range(8):
                    r0 = (i // 2) * 32 + cc * 16 + (i % 2) * 8
                    mfull[r0 : r0 + 8, :] = mraw[rnd, cc, i]

        @pl.when(rnd == 0)
        def _():
            for i in range(8):
                xl[i * 8 : i * 8 + 8, :] = mraw[rnd, c, i]

        @pl.when(rnd > 0)
        def _():
            all_columns()
            rows = [work[pl.ds(pl.multiple_of(i * 32 + c * 16, 16), 16), RANK:] for i in range(4)]
            xl[...] = jnp.dot(
                jnp.concatenate(rows, axis=0), mfull[...], precision=HIGHEST, preferred_element_type=F32
            )

        lhs = stacked(xl[...])
        for k in (2, 1, 3, 0):
            y2 = (y + k) % 4
            rows = a[pl.ds(pl.multiple_of(y2 * 256, 256), 256), :]
            part = folded(lax.dot_general(lhs, rows, NT, preferred_element_type=F32))
            for i in range(4):
                xs[rnd, i * 4 + y2] = part[i * 16 : i * 16 + 16]
            for x2 in x_peers + ([x] if k else []):
                send(xs.at[rnd, x2 * 4 + y2], xrs.at[rnd, mine_xy], rnd, XR, dev(z, x2, h, y2, c))
        xrs[rnd, mine_xy] = xs[rnd, mine_xy]

        @pl.when(rnd == 0)
        def _():
            all_columns()
            mt[rnd] = mfull[...]

        @pl.when(rnd > 0)
        def _():
            mt[rnd] = jnp.dot(work[:, RANK:], mfull[...], precision=HIGHEST, preferred_element_type=F32)

        gown[rnd] = lax.dot_general(
            mt[rnd, pl.ds(pl.multiple_of((c * 4 + z) * 16, 16), 16), :],
            mt[rnd], NT, precision=HIGHEST, preferred_element_type=F32,
        )
        for y2 in y_peers:
            send(gown.at[rnd], gys.at[rnd, y], rnd, GY, dev(z, x, h, y2, c))
        gys[rnd, y] = gown[rnd]
        landed(xrs.at[rnd, pl.ds(0, 15)], rnd, XR)
        total = xrs[rnd, 0]
        for i in range(1, 16):
            total = total + xrs[rnd, i]
        xt[rnd, mine_cy] = total
        for y2, c2 in yc_peers:
            piece = xt.at[rnd, mine_cy]
            send(piece, piece, rnd, XG, dev(z, x, h, y2, c2))
        landed(gys.at[rnd, pl.ds(0, 3)], rnd, GY)
        gsum[rnd] = (gys[rnd, 0] + gys[rnd, 1]) + (gys[rnd, 2] + gys[rnd, 3])
        for x2 in x_peers:
            send(gsum.at[rnd], gxs.at[rnd, x], rnd, GX, dev(z, x2, h, y, c))
        gxs[rnd, x] = gsum[rnd]

        landed(xt.at[rnd, pl.ds(0, 7)], rnd, XG)

        rows = [jnp.concatenate([xt[rnd, i * 4 + m] for m in range(4)], axis=1) for i in range(2)]
        lhs = stacked(jnp.concatenate(rows, axis=0))
        for n, (lo, size) in enumerate(PARTS):
            part = folded(jnp.dot(lhs, b[:, lo : lo + size], preferred_element_type=F32))
            ps[rnd, :, :, lo : lo + size] = part.reshape(4, 8, size)
            for z2 in z_peers:
                span = pl.ds(lo, size)
                send(ps.at[rnd, z2, :, span], prs.at[rnd, z, :, span], rnd, PR[n], dev(z2, x, h, y, c))
            if n == 0:
                landed(gxs.at[rnd, pl.ds(0, 3)], rnd, GX)
                gfull[rnd, c, z] = (gxs[rnd, 0] + gxs[rnd, 1]) + (gxs[rnd, 2] + gxs[rnd, 3])
                for z2 in z_peers:
                    piece = gfull.at[rnd, c, z]
                    send(piece, piece, rnd, GZ, dev(z2, x, h, y, c))
        prs[rnd, z] = ps[rnd, z]

        @pl.when(rnd == ROUNDS - 1)
        def _():
            for y2 in y_peers:
                send(
                    mt.at[rnd, :, pl.ds(pl.multiple_of(c * 256, 256), 256)],
                    mg.at[y, c],
                    0, PHASES,
                    dev(z, x, h, y2, c),
                )

        @pl.when(rnd == ROUNDS - 1)
        def _():
            share_gram(rnd)
            landed(gfull.at[rnd, o], rnd, GC)
            factor_start(rnd)

        for n, (lo, size) in enumerate(PARTS):
            span = pl.ds(lo, size)
            landed(prs.at[rnd, pl.ds(0, 3), :, span], rnd, PR[n])
            got = [prs[rnd, i, :, lo : lo + size] for i in range(4)]
            pt[rnd + 1, z, :, lo : lo + size] = (got[0] + got[1]) + (got[2] + got[3])
            for z2 in z_peers:
                piece = pt.at[rnd + 1, z, :, span]
                send(piece, piece, rnd, PG[n] + z, dev(z2, x, h, y, c))

            @pl.when(rnd == ROUNDS - 1)
            def _():
                to_row(z, n)
                factor_blocks(n * 6 // len(PARTS), (n + 1) * 6 // len(PARTS))


        @pl.when(rnd < ROUNDS - 1)
        def _():
            share_gram(rnd)

            def ready(n):
                for z2 in z_peers:
                    gathered_p(rnd, n, z2)

            tokens_part(rnd + 1, ready)

        return carry

    lax.fori_loop(0, ROUNDS, one_round, 0)

    last = ROUNDS - 1
    done = 6
    for n in range(len(PARTS)):
        for k in (1, 3, 2):
            z2 = (z + k) % 4
            gathered_p(last, n, z2)
            to_row(z2, n)
        if n < len(PARTS) - 1:
            factor_blocks(done, done + 1)
            done += 1
    landed(mg.at[pl.ds(0, 3), 0], 0, PHASES)
    for y2 in y_peers:
        piece = mg.at[y2, c]
        send(piece, piece, 1, PHASES, partner)
    for cc in range(2):
        mg[y, cc] = mt[last, :, cc * 256 : cc * 256 + 256]
    cf[x] = pt[ROUNDS]
    factor_blocks(done, 16)
    final = work[:, RANK:]
    scaled = final * math.sqrt(D)
    landed(mg.at[pl.ds(0, 3), 0], 1, PHASES)
    for i in range(4):
        for cc in range(2):
            r0 = i * FEAT + cc * 256
            basis_ref[r0 : r0 + 256, :] = lax.dot_general(
                mg[i, cc].T, scaled, NT, precision=HIGHEST, preferred_element_type=F32
            )
    for n, (lo, size) in enumerate(PARTS):
        landed(cf.at[pl.ds(0, 3), :, :, pl.ds(lo, size)], 2, PHASES + 1 + n)
        coef_ref[:, lo : lo + size] = jnp.dot(
            final, cf[:, :, :, lo : lo + size].reshape(RANK, size), precision=HIGHEST, preferred_element_type=F32
        )

    def drain(rnd, carry):
        left(yrs.at[rnd, pl.ds(0, 7)], rnd, YR)
        left(yt.at[rnd, pl.ds(0, 15)], rnd, YG)
        for n, (lo, size) in enumerate(HALVES):
            span = pl.ds(lo, size)
            left(mrs.at[rnd, pl.ds(0, 7), :, span], rnd, MR[n])
            left(mraw.at[rnd, 0, pl.ds(0, 7), :, span], rnd, MG[n])
        left(mraw.at[rnd, 0], rnd, MC)
        left(xrs.at[rnd, pl.ds(0, 15)], rnd, XR)
        left(xt.at[rnd, pl.ds(0, 7)], rnd, XG)
        for n, (lo, size) in enumerate(PARTS):
            span = pl.ds(lo, size)
            left(prs.at[rnd, pl.ds(0, 3), :, span], rnd, PR[n])
            left(pt.at[rnd, pl.ds(0, 3), :, span], rnd, PG[n] + z)
        left(gys.at[rnd, pl.ds(0, 3)], rnd, GY)
        left(gxs.at[rnd, pl.ds(0, 3)], rnd, GX)
        left(gfull.at[rnd, 0, pl.ds(0, 3)], rnd, GZ)
        left(gfull.at[rnd, 0], rnd, GC)
        return carry

    lax.fori_loop(0, ROUNDS, drain, 0)
    left(mg.at[pl.ds(0, 3), 0], 0, PHASES)
    left(mg.at[pl.ds(0, 3), 0], 1, PHASES)
    for n, (lo, size) in enumerate(PARTS):
        left(cf.at[pl.ds(0, 3), :, :, pl.ds(lo, size)], 2, PHASES + 1 + n)


def hand_over(basis_in, coef_in, basis_out, coef_out):
    basis_out[...] = basis_in[...]
    coef_out[...] = coef_in[...]


def body(activations, grad_out, sketch):
    anywhere = pl.BlockSpec(memory_space=pl.ANY)
    inside = pl.BlockSpec(memory_space=pltpu.VMEM)
    vm = pltpu.VMEM
    n = ROUNDS
    shapes = (
        jax.ShapeDtypeStruct((2048, RANK), F32),
        jax.ShapeDtypeStruct((RANK, HID), F32),
    )
    found = pl.pallas_call(
        kernel,
        name="range_finder",
        out_shape=shapes,
        in_specs=[anywhere] * 3,
        out_specs=(inside, inside),
        scratch_shapes=[
            vm((TOK, FEAT), BF16),
            vm((TOK, HID), BF16),
            vm((HID, RANK), F32),
            vm((RANK, HID), F32),
            vm((n + 1, 4, 8, HID), F32),
            vm((4, 32, 256), F32),
            vm((n, 8, 16, 256), F32),
            vm((n, 8, 16, 256), F32),
            vm((n, 16, 16, 256), F32),
            vm((n, 8, 8, FEAT), F32),
            vm((n, 8, 8, FEAT), F32),
            vm((n, 2, 8, 8, FEAT), F32),
            vm((RANK, FEAT), F32),
            vm((n, RANK, FEAT), F32),
            vm((64, FEAT), F32),
            vm((n, 16, 16, 256), F32),
            vm((n, 16, 16, 256), F32),
            vm((n, 8, 16, 256), F32),
            vm((n, 4, 8, HID), F32),
            vm((n, 4, 8, HID), F32),
            vm((n, 16, RANK), F32),
            vm((n, 4, 16, RANK), F32),
            vm((n, 16, RANK), F32),
            vm((n, 4, 16, RANK), F32),
            vm((n, 2, 4, 16, RANK), F32),
            vm((RANK, 2 * RANK), F32),
            vm((4, 4, 8, HID), F32),
            vm((4, 2, RANK, 256), F32),
            pltpu.SemaphoreType.DMA((2 + len(PARTS),)),
            pltpu.SemaphoreType.DMA((n, PHASES + 1 + len(PARTS))),
            pltpu.SemaphoreType.DMA((n, PHASES + 1 + len(PARTS))),
        ],
        compiler_params=pltpu.CompilerParams(
            collective_id=0, has_side_effects=True, vmem_limit_bytes=50 * 2**20
        ),
    )(activations, grad_out, pltpu.with_memory_space_constraint(sketch, pltpu.HBM))
    return pl.pallas_call(
        hand_over,
        name="hand_over",
        out_shape=shapes,
        in_specs=[inside] * 2,
        out_specs=(inside, inside),
        compiler_params=pltpu.CompilerParams(vmem_limit_bytes=8 * 2**20),
        cost_estimate=pl.CostEstimate(flops=0, bytes_accessed=4 * 2**20, transcendentals=0),
    )(*found)


def solution(mesh):
    in_specs = (P("dp", "row"), P("dp", "col"), P("col", None))
    out_specs = (P("row", None), P(None, "col"))
    return jax.shard_map(body, mesh=mesh, in_specs=in_specs, out_specs=out_specs, check_vma=False)
```
